32 devices in a mesh: dp: 8 (over y, x, core), mp: 4 (over z).
Axes of the slice: x: 2, y: 2, z: 4, core: 2. Of those that a mesh axis runs over, the one named last changes fastest.
Arguments:
- token_ids: int32 [256, 128], P('dp'), may hold values from 0 to 30591
- replacements: int32 [256, 128], P('dp'), may hold values from 0 to 30591
- replaced: int32 [256, 128], P('dp'), may hold values 0 or 1
- lengths: int32 [256], P('dp'), may hold values from 32 to 128, as said below
- widths: int32 [256], P('dp'), may hold values from 1 to 4
- teacher_embed: bfloat16 [256, 128, 768], P(('dp', 'mp')), may hold values from -6 to 6
- teacher_hidden: bfloat16 [256, 128, 768], P(('dp', 'mp')), may hold values from -6 to 6
- teacher_logits: float32 [256, 3], P(('dp', 'mp')), may hold values from -6 to 6
- embed_table: float32 [30592, 768], P(('dp', 'mp')), may hold values from -0.3125 to 0.3125
- embed_moment: float32 [30592, 768], P(('dp', 'mp')), may hold values from -0.00061035156 to 0.00061035156
- embed_square: float32 [30592, 768], P(('dp', 'mp')), may hold values from 1e-09 to 4e-09
- dense_weights: float32 [3840, 768], P(('dp', 'mp'))
- dense_moment: float32 [3840, 768], P(('dp', 'mp')), may hold values from -0.00030517578 to 0.00030517578
- dense_square: float32 [3840, 768], P(('dp', 'mp')), may hold values from 2.6e-10 to 1.04e-09
- feedforward: float32 [3072, 1536], P(('dp', 'mp')), may hold values from -0.15625 to 0.15625
- feedforward_moment: float32 [3072, 1536], P(('dp', 'mp')), may hold values from -0.00012207031 to 0.00012207031
- feedforward_square: float32 [3072, 1536], P(('dp', 'mp')), may hold values from 3.2e-11 to 1.3e-10
- classifier: float32 [768, 3], replicated, may hold values from -0.21875 to 0.21875
- classifier_moment: float32 [768, 3], replicated, may hold values from -0.00012207031 to 0.00012207031
- classifier_square: float32 [768, 3], replicated, may hold values from 3.2e-11 to 1.3e-10
- norm_gains: float32 [6, 768], replicated
- norm_moment: float32 [6, 768], replicated, may hold values from -0.0068359375 to 0.0068359375
- norm_square: float32 [6, 768], replicated, may hold values from 1.2e-07 to 4.8e-07
Outputs:
- loss_sum: float32 [], replicated
- token_count: float32 [], replicated
- grad_norm: float32 [], replicated
- new_embed_table: float32 [30592, 768], P(('dp', 'mp'))
- new_embed_moment: float32 [30592, 768], P(('dp', 'mp'))
- new_embed_square: float32 [30592, 768], P(('dp', 'mp'))
- embed_copy: bfloat16 [30592, 768], P(('dp', 'mp'))
- new_dense_weights: float32 [3840, 768], P(('dp', 'mp'))
- new_dense_moment: float32 [3840, 768], P(('dp', 'mp'))
- new_dense_square: float32 [3840, 768], P(('dp', 'mp'))
- dense_copy: bfloat16 [3840, 768], P(('dp', 'mp'))
- new_feedforward: float32 [3072, 1536], P(('dp', 'mp'))
- new_feedforward_moment: float32 [3072, 1536], P(('dp', 'mp'))
- new_feedforward_square: float32 [3072, 1536], P(('dp', 'mp'))
- feedforward_copy: bfloat16 [3072, 1536], P(('dp', 'mp'))
- new_classifier: float32 [768, 3], replicated
- new_classifier_moment: float32 [768, 3], replicated
- new_classifier_square: float32 [768, 3], replicated
- classifier_copy: bfloat16 [768, 3], replicated
- new_norm_gains: float32 [6, 768], replicated
- new_norm_moment: float32 [6, 768], replicated
- new_norm_square: float32 [6, 768], replicated
The draws below stay inside these ranges and needn't reach their ends.
Inputs may be any that keep to these rules, and one draw needn't show every extreme that they name: `lengths`: in every draw some sequence has length 128.
All inputs are finite; a program needn't handle non-finite values. No bound on the sum of `replaced` on one device may be relied on, other than what follows from the above.
Results may differ from the reference program's by a relative error of at most 0.017.
Values may be sent and summed in bfloat16 or wider, within the bound.
No kernel may reach another device: no remote copies, remote signals or barrier semaphores. Data moves between devices by JAX's collectives and lax.ppermute only.
A program may use at most 256 MiB of HBM per device.

```python
import math
import jax
import jax.numpy as jnp
import numpy as np
from jax import lax

MODEL_WIDTH = 768
HEADS = 12
FF = 3072
V = 30592
NCLS = 3
L = 128
LEVELS = 4
STEP = 10
SEQS = 256


def draw_lengths(key, part):
    key = jax.random.fold_in(key, 11)
    first_key, second_key = jax.random.split(key)
    drawn = jax.random.randint(first_key, (SEQS,), L // 4, L + 1)
    longest = jax.random.randint(second_key, (), 0, SEQS)
    return jnp.where(jnp.arange(SEQS) == longest, L, drawn).astype(jnp.int32)


def draw_dense_weights(key, part):
    key = jax.random.fold_in(key, 12)
    noise = jnp.clip(jax.random.normal(key, (5 * MODEL_WIDTH, MODEL_WIDTH), jnp.float32), -6.0, 6.0)
    rows = jnp.arange(5 * MODEL_WIDTH)[:, None]
    scaling = jnp.where((rows >= 3 * MODEL_WIDTH) & (rows < 4 * MODEL_WIDTH), (8.0 / MODEL_WIDTH) ** 0.5, (1.0 / MODEL_WIDTH) ** 0.5)
    return (noise * scaling).astype(jnp.float32)


def draw_norm_gains(key, part):
    key = jax.random.fold_in(key, 13)
    noise = jnp.clip(jax.random.normal(key, (6, MODEL_WIDTH), jnp.float32) * 0.5, -1.0, 1.0)
    rows = jnp.arange(6)[:, None]
    return jnp.where(rows % 2 == 0, 1.0 + 0.3 * noise, 0.3 * noise).astype(jnp.float32)


def touch_ends(values, own_key, least, high):
    index_at = [jax.random.randint(jax.random.fold_in(own_key, axis), (), 0, length) for axis, length in enumerate(values.shape)]
    widest = values.shape.index(max(values.shape))
    neighbour = index_at[:widest] + [(index_at[widest] + 1) % values.shape[widest]] + index_at[widest + 1:]
    return values.at[tuple(index_at)].set(least).at[tuple(neighbour)].set(high)


def steps_of(rng, extent, cuts, low, top_value):
    factor_of, own = 1.0, jax.random.fold_in(rng, 6)
    for dim, parts in cuts:
        heights = jnp.exp(jax.random.uniform(jax.random.fold_in(own, dim), (parts,), jnp.float32, low / len(cuts), top_value / len(cuts)))
        factor_of = factor_of * jnp.repeat(heights, extent[dim] // parts).reshape([-1 if axis == dim else 1 for axis in range(len(extent))])
    return factor_of


def cumulative_ranks(count, skew):
    weights = [(1 << 20) // math.isqrt(standing ** skew) + 1 for standing in range(1, count + 1)]
    width = 1 + sum(weights) // (1 << 30)
    return np.cumsum(np.array([max(1, weight // width) for weight in weights]))


def skewed_ids(own_key, dims, count, lean):
    table = cumulative_ranks(count, lean)
    lot = jax.random.randint(jax.random.fold_in(own_key, 1), dims, 0, int(table[count - 1]))
    rank = jnp.searchsorted(jnp.asarray(table, jnp.int32), lot, side="right")
    return jax.random.permutation(jax.random.fold_in(own_key, 2), count)[rank].astype(jnp.int32)


def centred(stream_key, shape, scale, reach, cuts=(), dtype=jnp.bfloat16):
    factor_of = steps_of(stream_key, shape, cuts, -0.22, 0.18) if cuts else 1.0
    values = jax.random.normal(stream_key, shape, jnp.float32) * scale * factor_of
    return jnp.minimum(jnp.maximum(values, -reach), reach).astype(dtype)


def setup_inputs(seed: int = 0) -> dict:
    key_list = jax.random.split(jax.random.key(seed), 24)
    return {
        "token_ids": touch_ends(skewed_ids(key_list[0], (SEQS, L), V, 2), jax.random.fold_in(key_list[0], 3), 0, V - 1).astype(jnp.int32),
        "replacements": touch_ends(jax.random.randint(key_list[1], (SEQS, L), 0, V), jax.random.fold_in(key_list[1], 1), 0, V - 1).astype(jnp.int32),
        "replaced": touch_ends((jax.random.randint(key_list[2], (SEQS, L), 0, 3) < 1).astype(jnp.int32), jax.random.fold_in(key_list[2], 1), 0, 1),
        "lengths": draw_lengths(jax.random.fold_in(key_list[23], 71), 0),
        "widths": touch_ends(jax.random.randint(key_list[4], (SEQS,), 1, LEVELS + 1), jax.random.fold_in(key_list[4], 1), 1, LEVELS).astype(jnp.int32),
        "teacher_embed": centred(key_list[5], (SEQS, L, MODEL_WIDTH), 1.0, 6.0, ((0, 32),)),
        "teacher_hidden": centred(key_list[6], (SEQS, L, MODEL_WIDTH), 1.0, 6.0, ((0, 32),)),
        "teacher_logits": centred(key_list[7], (SEQS, NCLS), 1.0, 6.0, ((0, 32),), jnp.float32),
        "embed_table": centred(key_list[8], (V, MODEL_WIDTH), 0.05, 0.3125, ((0, 32),), jnp.float32),
        "embed_moment": centred(key_list[9], (V, MODEL_WIDTH), 0.00011, 0.00061035156, ((0, 32),), jnp.float32),
        "embed_square": jnp.clip(jnp.exp(math.log(3.999999886872274e-09) - 1.3862944 * jax.random.uniform(key_list[10], (V, MODEL_WIDTH), jnp.float32) ** steps_of(key_list[10], (V, MODEL_WIDTH), ((0, 32),), -0.2, 0.2)), 9.999999717180685e-10, 3.999999886872274e-09),
        "dense_weights": draw_dense_weights(jax.random.fold_in(key_list[23], 71), 0),
        "dense_moment": centred(key_list[12], (5 * MODEL_WIDTH, MODEL_WIDTH), 0.000056, 0.00030517578, ((0, 32),), jnp.float32),
        "dense_square": jnp.clip(jnp.exp(math.log(1.0399999750276834e-09) - 1.3862944 * jax.random.uniform(key_list[13], (5 * MODEL_WIDTH, MODEL_WIDTH), jnp.float32) ** steps_of(key_list[13], (5 * MODEL_WIDTH, MODEL_WIDTH), ((0, 32),), -0.2, 0.2)), 2.5999999375692084e-10, 1.0399999750276834e-09),
        "feedforward": centred(key_list[14], (FF, 2 * MODEL_WIDTH), (2 * MODEL_WIDTH) ** -0.5, 0.15625, ((0, 32),), jnp.float32),
        "feedforward_moment": centred(key_list[15], (FF, 2 * MODEL_WIDTH), 0.00002, 0.00012207031, ((0, 32),), jnp.float32),
        "feedforward_square": jnp.clip(jnp.exp(math.log(1.2999999687846042e-10) - 1.4017985 * jax.random.uniform(key_list[16], (FF, 2 * MODEL_WIDTH), jnp.float32) ** steps_of(key_list[16], (FF, 2 * MODEL_WIDTH), ((0, 32),), -0.2, 0.2)), 3.199999987213431e-11, 1.2999999687846042e-10),
        "classifier": centred(key_list[17], (MODEL_WIDTH, NCLS), MODEL_WIDTH ** -0.5, 0.21875, (), jnp.float32),
        "classifier_moment": centred(key_list[18], (MODEL_WIDTH, NCLS), 0.00002, 0.00012207031, (), jnp.float32),
        "classifier_square": jnp.clip(jnp.exp(jax.random.uniform(key_list[19], (MODEL_WIDTH, NCLS), jnp.float32, math.log(3.199999987213431e-11), math.log(1.2999999687846042e-10))), 3.199999987213431e-11, 1.2999999687846042e-10),
        "norm_gains": draw_norm_gains(jax.random.fold_in(key_list[23], 71), 0),
        "norm_moment": centred(key_list[21], (6, MODEL_WIDTH), 0.0012, 0.0068359375, (), jnp.float32),
        "norm_square": jnp.clip(jnp.exp(jax.random.uniform(key_list[22], (6, MODEL_WIDTH), jnp.float32, math.log(1.199999957179898e-07), math.log(4.799999828719592e-07))), 1.199999957179898e-07, 4.799999828719592e-07),
    }


highest_precision = lax.Precision.HIGHEST
norm_epsilon = 1e-05
learn_rate = 0.05
gain_rate = 0.5
beta_one = 0.9
beta_two = 0.999
adam_epsilon = 1e-08
weight_decay = 0.01
clip_bound = 1.0

@jax.custom_vjp
def narrow_width(v):
    return lax.optimization_barrier(v.astype(jnp.bfloat16)).astype(jnp.float32)

@jax.custom_vjp
def narrow_backward(v):
    return v

def low_keep(v):
    return (narrow_width(v), None)

def low_pass(kept, grad):
    return (grad,)

def back_keep(v):
    return (v, None)

def back_low(kept, grad):
    return (narrow_width(grad),)
narrow_width.defvjp(low_keep, low_pass)
narrow_backward.defvjp(back_keep, back_low)

def layer_norm(values, gain_row, shift_row):
    center = values - lax.optimization_barrier(jnp.mean(values, axis=-1, keepdims=True))
    spread = lax.optimization_barrier(jnp.mean(center * center, axis=-1, keepdims=True))
    return center * lax.rsqrt(spread + norm_epsilon) * gain_row + shift_row

def forward(weights, batches):
    embed_table, dense_weights, feedforward, classifier, norm_gains = weights
    chosen, lengths, widths, teacher_embed, teacher_hidden, teacher_logits = batches
    table_low = narrow_width(embed_table)
    dense_narrow_part = narrow_width(dense_weights)
    feedforward_narrow = narrow_width(feedforward)
    sequences = chosen.shape[0]
    head_size = MODEL_WIDTH // HEADS
    embedded = narrow_backward(table_low[chosen])
    usable = (jnp.arange(L)[None, :] < lengths[:, None]).astype(jnp.float32)
    normalized_rows = layer_norm(embedded, norm_gains[0], norm_gains[1])
    output_projection = narrow_width(narrow_backward(jnp.einsum('akc,yc->aky', narrow_width(normalized_rows), dense_narrow_part[:3 * MODEL_WIDTH], precision=highest_precision)))
    pieces = output_projection.reshape(sequences, L, 3, HEADS, head_size)
    scores = narrow_backward(jnp.einsum('sqhc,skhc->shqk', pieces[:, :, 0], pieces[:, :, 1], precision=highest_precision) * head_size ** (-0.5))
    scores = scores + jnp.where(usable[:, None, None, :] > 0, 0.0, -1000000000.0)
    attend = jax.nn.softmax(scores, axis=-1)
    head_mixture = jnp.einsum('shqk,skhc->sqhc', narrow_width(attend), pieces[:, :, 2], precision=highest_precision)
    head_on = (jnp.arange(HEADS)[None, :] < widths[:, None] * HEADS // LEVELS).astype(jnp.float32)
    head_mixture = narrow_width(narrow_backward(head_mixture * head_on[:, None, :, None])).reshape(sequences, L, MODEL_WIDTH)
    attention_result = narrow_backward(jnp.einsum('jrx,xb->jrb', head_mixture, dense_narrow_part[3 * MODEL_WIDTH:4 * MODEL_WIDTH], precision=highest_precision))
    middle_activation = layer_norm(normalized_rows + attention_result, norm_gains[2], norm_gains[3])
    residual_before = narrow_backward(jnp.einsum('kha,qa->khq', narrow_width(middle_activation), feedforward_narrow[:, :MODEL_WIDTH], precision=highest_precision))
    neuron_on = (jnp.arange(FF)[None, :] < widths[:, None] * FF // LEVELS).astype(jnp.float32)
    hidden_state = narrow_width(jax.nn.gelu(residual_before) * neuron_on[:, None, :])
    feedforward_result = narrow_backward(jnp.einsum('cox,xt->cot', hidden_state, feedforward_narrow[:, MODEL_WIDTH:], precision=highest_precision))
    output = layer_norm(middle_activation + feedforward_result, norm_gains[4], norm_gains[5])
    pooled = jnp.tanh(jnp.dot(narrow_width(output[:, 0]), dense_narrow_part[4 * MODEL_WIDTH:], precision=highest_precision))
    logits = jnp.dot(narrow_width(pooled), narrow_width(classifier), precision=highest_precision)
    total = jnp.sum(usable[:, :, None] * (normalized_rows - teacher_embed) ** 2)
    total = total + jnp.sum(usable[:, :, None] * (output - teacher_hidden) ** 2)
    return total + L * jnp.sum((logits - teacher_logits) ** 2)

def adam_update(weight, gradient, first_moment, second, decay_rate, rate):
    first_new = beta_one * first_moment + (1.0 - beta_one) * gradient
    second_new = beta_two * second + (1.0 - beta_two) * gradient * gradient
    direction = first_new / (1.0 - beta_one ** STEP) / (jnp.sqrt(second_new / (1.0 - beta_two ** STEP)) + adam_epsilon)
    return (weight - rate * (direction + decay_rate * weight), first_new, second_new)

def reference(token_ids, replacements, replaced, lengths, widths, teacher_embed, teacher_hidden, teacher_logits, embed_table, embed_moment, embed_square, dense_weights, dense_moment, dense_square, feedforward, feedforward_moment, feedforward_square, classifier, classifier_moment, classifier_square, norm_gains, norm_moment, norm_square):
    chosen = jnp.where(replaced == 1, replacements, token_ids)
    groups = SEQS // 32

    def grouped(array):
        return array.reshape((groups, 32) + array.shape[1:])
    batches = (grouped(chosen), grouped(lengths), grouped(widths), grouped(teacher_embed.astype(jnp.float32)), grouped(teacher_hidden.astype(jnp.float32)), grouped(teacher_logits))
    weights = (embed_table, dense_weights, feedforward, classifier, norm_gains)

    def one_group(carry, batch):
        value, pull = jax.vjp(lambda params: forward(params, batch), weights)
        gradients = pull(jnp.ones((), jnp.float32))[0]
        return ((carry[0] + value, jax.tree.map(jnp.add, carry[1], gradients)), None)
    start = (jnp.zeros((), jnp.float32), jax.tree.map(jnp.zeros_like, weights))
    (loss_sum, gradients), _ = lax.scan(one_group, start, batches)
    token_count = jnp.sum(lengths).astype(jnp.float32)
    gradients = jax.tree.map(lambda gradient: gradient / token_count, gradients)
    grad_norm = jnp.sqrt(sum((jnp.sum(gradient * gradient) for gradient in gradients)))
    factor = clip_bound / jnp.maximum(grad_norm, clip_bound)
    table_grad, dense_grad, ffn_grad, class_grad, gains_grad = [gradient * factor for gradient in gradients]
    table_new = adam_update(embed_table, table_grad, embed_moment, embed_square, weight_decay, learn_rate)
    dense_new = adam_update(dense_weights, dense_grad, dense_moment, dense_square, weight_decay, learn_rate)
    ffn_new = adam_update(feedforward, ffn_grad, feedforward_moment, feedforward_square, weight_decay, learn_rate)
    class_new = adam_update(classifier, class_grad, classifier_moment, classifier_square, weight_decay, learn_rate)
    gains_new = adam_update(norm_gains, gains_grad, norm_moment, norm_square, 0.0, gain_rate)
    return (loss_sum, token_count, grad_norm, table_new[0], table_new[1], table_new[2], table_new[0].astype(jnp.bfloat16), dense_new[0], dense_new[1], dense_new[2], dense_new[0].astype(jnp.bfloat16), ffn_new[0], ffn_new[1], ffn_new[2], ffn_new[0].astype(jnp.bfloat16), class_new[0], class_new[1], class_new[2], class_new[0].astype(jnp.bfloat16), gains_new[0], gains_new[1], gains_new[2])
```

```python
import jax
import jax.numpy as jnp
from jax import lax
from jax.sharding import PartitionSpec as P

MODEL_WIDTH = 768
HEADS = 12
FF = 3072
L = 128
LEVELS = 4
STEP = 10


highest_precision = lax.Precision.HIGHEST
norm_epsilon = 1e-05
learn_rate = 0.05
gain_rate = 0.5
beta_one = 0.9
beta_two = 0.999
adam_epsilon = 1e-08
weight_decay = 0.01
clip_bound = 1.0


def norm_forward(values, gain_row, shift_row):
    center = values - jnp.mean(values, axis=-1, keepdims=True)
    spread = jnp.mean(center * center, axis=-1, keepdims=True)
    inverse = lax.rsqrt(spread + norm_epsilon)
    unit = center * inverse
    return (unit * gain_row + shift_row, unit, inverse)


def norm_backward(grad, unit, inverse, gain_row):
    scaled = grad * gain_row
    level = jnp.mean(scaled, axis=-1, keepdims=True)
    along = jnp.mean(scaled * unit, axis=-1, keepdims=True)
    grad_values = inverse * (scaled - level - unit * along)
    return (grad_values, jnp.sum(grad * unit, axis=0), jnp.sum(grad, axis=0))


gelu_rate = 0.7978845608028654
gelu_cube = 0.044715


def gelu_forward(before):
    bend = jnp.tanh(gelu_rate * (before + gelu_cube * before * before * before))
    return 0.5 * before * (1.0 + bend)


def gelu_slope(before):
    bend = jnp.tanh(gelu_rate * (before + gelu_cube * before * before * before))
    inner = gelu_rate * (1.0 + 3.0 * gelu_cube * before * before)
    return 0.5 * (1.0 + bend) + 0.5 * before * (1.0 - bend * bend) * inner


def adam_update(weight, gradient, first_moment, second, decay_rate, rate):
    first_new = beta_one * first_moment + (1.0 - beta_one) * gradient
    second_new = beta_two * second + (1.0 - beta_two) * gradient * gradient
    direction = (
        first_new
        / (1.0 - beta_one**STEP)
        / (jnp.sqrt(second_new / (1.0 - beta_two**STEP)) + adam_epsilon)
    )
    return (weight - rate * (direction + decay_rate * weight), first_new, second_new)


def contract_last(left, right):
    return lax.dot_general(
        left, right, (((1,), (1,)), ((), ())), preferred_element_type=jnp.float32
    )


def contract_first(left, right):
    return lax.dot_general(
        left, right, (((0,), (0,)), ((), ())), preferred_element_type=jnp.float32
    )


def split_heads(output_projection):
    sequences = output_projection.shape[0] // L
    pieces = output_projection.reshape(sequences, L, 3, HEADS, MODEL_WIDTH // HEADS)
    return (pieces[:, :, 0], pieces[:, :, 1], pieces[:, :, 2])


def attention_forward(output_projection, usable, head_on):
    queries, keying, values = split_heads(output_projection)
    scores = jnp.einsum("sqhc,skhc->shqk", queries, keying, preferred_element_type=jnp.float32) * (
        MODEL_WIDTH // HEADS
    ) ** (-0.5)
    scores = scores + jnp.where(usable[:, None, None, :] > 0, 0.0, -1000000000.0)
    attend = jax.nn.softmax(scores, axis=-1)
    head_mixture = jnp.einsum(
        "shqk,skhc->sqhc", attend.astype(jnp.bfloat16), values, preferred_element_type=jnp.float32
    )
    head_mixture = (head_mixture * head_on[:, None, :, None]).astype(jnp.bfloat16)
    return (attend, head_mixture.reshape(output_projection.shape[0], MODEL_WIDTH))


def attention_backward(output_projection, attend, grad_mixture):
    queries, keying, values = split_heads(output_projection)
    attend_low = attend.astype(jnp.bfloat16)
    grad_values = jnp.einsum(
        "shqk,sqhc->skhc", attend_low, grad_mixture, preferred_element_type=jnp.float32
    )
    grad_attend = jnp.einsum(
        "sqhc,skhc->shqk", grad_mixture, values, preferred_element_type=jnp.float32
    )
    grad_scores = attend * (grad_attend - jnp.sum(grad_attend * attend, axis=-1, keepdims=True))
    grad_scores = grad_scores.astype(jnp.bfloat16)
    scaling = (MODEL_WIDTH // HEADS) ** (-0.5)
    grad_queries = (
        jnp.einsum("shqk,skhc->sqhc", grad_scores, keying, preferred_element_type=jnp.float32)
        * scaling
    )
    grad_keying = (
        jnp.einsum("shqk,sqhc->skhc", grad_scores, queries, preferred_element_type=jnp.float32)
        * scaling
    )
    stacked = jnp.stack([grad_queries, grad_keying, grad_values], axis=2)
    return stacked.reshape(output_projection.shape[0], 3 * MODEL_WIDTH).astype(jnp.bfloat16)


def per_device(
    token_ids,
    replacements,
    replaced,
    lengths,
    widths,
    teacher_embed,
    teacher_hidden,
    teacher_logits,
    embed_table,
    embed_moment,
    embed_square,
    dense_weights,
    dense_moment,
    dense_square,
    feedforward,
    feedforward_moment,
    feedforward_square,
    classifier,
    classifier_moment,
    classifier_square,
    norm_gains,
    norm_moment,
    norm_square,
):
    both = ("dp", "mp")
    mp_count = lax.axis_size("mp")
    mp_index = lax.axis_index("mp")
    n_dev = lax.axis_size("dp") * mp_count
    own_seqs = teacher_logits.shape[0]
    own_rows = own_seqs * L
    table_rows = embed_table.shape[0]
    low = jnp.bfloat16
    dense_full = lax.all_gather(dense_weights.astype(low), both, axis=0, tiled=True)
    ffn_full = lax.all_gather(feedforward.astype(low), both, axis=0, tiled=True)
    table_low = embed_table.astype(low)

    depth = -(-(own_rows * 3 // 2) // (n_dev * 16)) * 16
    capacity = depth - 1
    own_start = mp_index * own_seqs
    own_ids = lax.dynamic_slice_in_dim(
        jnp.where(replaced == 1, replacements, token_ids), own_start, own_seqs
    ).reshape(own_rows)
    owner = own_ids // table_rows
    local = own_ids - owner * table_rows
    place = jnp.arange(own_rows)
    first = jnp.min(
        jnp.where(own_ids[:, None] == own_ids[None, :], place[None, :], own_rows), axis=1
    )
    leads = first == place
    slot = jnp.sum(
        (leads[None, :] & (owner[:, None] == owner[None, :]) & (place[None, :] < first[:, None])).astype(
            jnp.int32
        ),
        axis=1,
    )
    deepest = jnp.max(slot)

    def positions(turn):
        rank = slot - turn * capacity
        return jnp.where((rank >= 0) & (rank < capacity), owner * depth + rank, -1)

    def wanted(turn):
        spot = jnp.where(leads, positions(turn), -1)
        hits = spot[:, None] == jnp.arange(n_dev * depth)[None, :]
        rows = jnp.max(jnp.where(hits, local[:, None], -1), axis=0).reshape(n_dev, depth)
        return jnp.where(jnp.arange(depth)[None, :] == capacity, deepest, rows)

    def exchange(blocks):
        return lax.all_to_all(blocks, both, split_axis=0, concat_axis=0)

    def asked_hot(asked):
        flat = jnp.where(jnp.arange(depth)[None, :] < capacity, asked, -1).reshape(-1)
        return (flat[:, None] == jnp.arange(table_rows)[None, :]).astype(low)

    def own_hot(turn):
        return (positions(turn)[:, None] == jnp.arange(n_dev * depth)[None, :]).astype(low)

    def fetch(turn, asked):
        rows = jnp.dot(asked_hot(asked), table_low, preferred_element_type=low)
        rows = exchange(rows.reshape(n_dev, depth, MODEL_WIDTH)).reshape(-1, MODEL_WIDTH)
        return jnp.dot(own_hot(turn), rows, preferred_element_type=jnp.float32)

    asked_first = exchange(wanted(0))
    turns = jnp.max(asked_first[:, capacity]) // capacity + 1
    embedded = fetch(0, asked_first)
    embedded = lax.while_loop(
        lambda state: state[0] < turns,
        lambda state: (state[0] + 1, state[1] + fetch(state[0], exchange(wanted(state[0])))),
        (jnp.int32(1), embedded),
    )[1]

    own_lengths = lax.dynamic_slice_in_dim(lengths, own_start, own_seqs)
    own_levels = lax.dynamic_slice_in_dim(widths, own_start, own_seqs)
    usable_grid = (jnp.arange(L)[None, :] < own_lengths[:, None]).astype(jnp.float32)
    usable = usable_grid.reshape(own_rows, 1)
    head_on = (jnp.arange(HEADS)[None, :] < own_levels[:, None] * (HEADS // LEVELS)).astype(
        jnp.float32
    )
    row_limit = jnp.broadcast_to(own_levels[:, None] * (FF // LEVELS), (own_seqs, L)).reshape(
        own_rows, 1
    )
    neuron_on = jnp.arange(FF)[None, :] < row_limit

    normalized_rows, unit_base, inverse_base = norm_forward(embedded, norm_gains[0], norm_gains[1])
    normed_low = normalized_rows.astype(low)
    qkv_rows = dense_full[: 3 * MODEL_WIDTH]
    output_projection = contract_last(normed_low, qkv_rows).astype(low)
    attend, head_mixture = attention_forward(output_projection, usable_grid, head_on)
    out_rows = dense_full[3 * MODEL_WIDTH : 4 * MODEL_WIDTH]
    attention_result = jnp.dot(head_mixture, out_rows, preferred_element_type=jnp.float32)
    middle_activation, unit_one, inverse_one = norm_forward(
        normalized_rows + attention_result, norm_gains[2], norm_gains[3]
    )
    middle_low = middle_activation.astype(low)
    up_rows = ffn_full[:, :MODEL_WIDTH]
    down_rows = ffn_full[:, MODEL_WIDTH:]
    residual_before = contract_last(middle_low, up_rows)
    hidden_low = jnp.where(neuron_on, gelu_forward(residual_before), 0.0).astype(low)
    feedforward_result = jnp.dot(hidden_low, down_rows, preferred_element_type=jnp.float32)
    output, unit_two, inverse_two = norm_forward(
        middle_activation + feedforward_result, norm_gains[4], norm_gains[5]
    )
    embed_diff = normalized_rows - teacher_embed.reshape(own_rows, MODEL_WIDTH).astype(jnp.float32)
    hidden_diff = output - teacher_hidden.reshape(own_rows, MODEL_WIDTH).astype(jnp.float32)
    first_low = output.reshape(own_seqs, L, MODEL_WIDTH)[:, 0].astype(low)
    pool_rows = dense_full[4 * MODEL_WIDTH :]
    pooled = jnp.tanh(jnp.dot(first_low, pool_rows, preferred_element_type=jnp.float32))
    pooled_low = pooled.astype(low)
    class_low = classifier.astype(low)
    logits = jnp.dot(pooled_low, class_low, preferred_element_type=jnp.float32)
    logit_diff = logits - teacher_logits
    loss_own = jnp.sum(usable * embed_diff * embed_diff) + jnp.sum(
        usable * hidden_diff * hidden_diff
    )
    loss_own = loss_own + L * jnp.sum(logit_diff * logit_diff)
    grad_logits = 2.0 * L * logit_diff
    pooled_wide = pooled_low.astype(jnp.float32)
    first_wide = first_low.astype(jnp.float32)
    grad_class = jnp.dot(pooled_wide.T, grad_logits, precision=highest_precision)
    grad_pooled = jnp.dot(grad_logits, class_low.astype(jnp.float32).T, precision=highest_precision)
    grad_inner = grad_pooled * (1.0 - pooled * pooled)
    grad_pool_rows = jnp.dot(first_wide.T, grad_inner, precision=highest_precision)
    grad_first = jnp.dot(grad_inner, pool_rows.astype(jnp.float32).T, precision=highest_precision)
    grad_output = (2.0 * usable * hidden_diff).reshape(own_seqs, L, MODEL_WIDTH)
    grad_output = grad_output.at[:, 0].add(grad_first).reshape(own_rows, MODEL_WIDTH)
    grad_second, gain_two, shift_two = norm_backward(grad_output, unit_two, inverse_two, norm_gains[4])
    grad_feed_low = grad_second.astype(low)

    def scatter_sum(rows):
        over_dp = lax.psum_scatter(rows, "dp", scatter_dimension=0, tiled=True)
        return lax.psum_scatter(over_dp, "mp", scatter_dimension=0, tiled=True)

    grad_down = scatter_sum(contract_first(hidden_low, grad_feed_low).astype(low))
    grad_hidden = contract_last(grad_feed_low, down_rows)
    grad_before = jnp.where(neuron_on, grad_hidden * gelu_slope(residual_before), 0.0).astype(low)
    grad_up = scatter_sum(contract_first(grad_before, middle_low).astype(low))
    grad_middle_ffn = jnp.dot(grad_before, up_rows, preferred_element_type=jnp.float32)
    grad_first_sum, gain_one, shift_one = norm_backward(
        grad_second + grad_middle_ffn, unit_one, inverse_one, norm_gains[2]
    )
    grad_att_low = grad_first_sum.astype(low)
    grad_out_rows = contract_first(head_mixture, grad_att_low)
    grad_mixture = contract_last(grad_att_low, out_rows).astype(low)
    grad_mixture = grad_mixture.reshape(own_seqs, L, HEADS, MODEL_WIDTH // HEADS) * head_on[
        :, None, :, None
    ].astype(low)
    grad_project = attention_backward(output_projection, attend, grad_mixture)
    grad_qkv_rows = contract_first(grad_project, normed_low)
    grad_dense = jnp.concatenate([grad_qkv_rows, grad_out_rows, grad_pool_rows], axis=0)
    dense_grad = scatter_sum(grad_dense.astype(low)).astype(jnp.float32)
    grad_normed = (
        grad_first_sum
        + 2.0 * usable * embed_diff
        + jnp.dot(grad_project, qkv_rows, preferred_element_type=jnp.float32)
    )
    grad_embedded, gain_base, shift_base = norm_backward(
        grad_normed, unit_base, inverse_base, norm_gains[0]
    )
    grad_embed_low = grad_embedded.astype(low)

    small = jnp.concatenate(
        [
            jnp.stack([gain_base, shift_base, gain_one, shift_one, gain_two, shift_two]).reshape(-1),
            grad_class.reshape(-1),
        ]
    )
    share = -(-small.shape[0] // n_dev)
    small_parts = jnp.pad(small, (0, share * n_dev - small.shape[0])).reshape(n_dev, share)
    upper = lax.reduce_precision(small_parts, 8, 7)
    rider = jnp.concatenate([upper, small_parts - upper], axis=1).astype(low)
    rider = jnp.pad(rider, ((0, 0), (0, MODEL_WIDTH - 2 * share)))

    def give_back(turn):
        sums = lax.dot_general(
            own_hot(turn), grad_embed_low, (((0,), (0,)), ((), ())), preferred_element_type=jnp.float32
        )
        return sums.reshape(n_dev, depth, MODEL_WIDTH)

    def collect(asked, returned):
        return lax.dot_general(
            asked_hot(asked),
            returned.reshape(-1, MODEL_WIDTH),
            (((0,), (0,)), ((), ())),
            preferred_element_type=jnp.float32,
        )

    sums = give_back(0)
    sums = jnp.where(jnp.arange(depth)[None, :, None] == capacity, rider.astype(jnp.float32)[:, None, :], sums)
    returned = exchange(sums.astype(low))
    table_grad = collect(asked_first, returned)
    table_grad = lax.while_loop(
        lambda state: state[0] < turns,
        lambda state: (
            state[0] + 1,
            state[1]
            + collect(exchange(wanted(state[0])), exchange(give_back(state[0]).astype(low))),
        ),
        (jnp.int32(1), table_grad),
    )[1]
    riders = jnp.sum(returned[:, capacity, : 2 * share].astype(jnp.float32), axis=0)
    small_share = riders[:share] + riders[share:]
    ffn_grad = jnp.concatenate([grad_up, grad_down], axis=1).astype(jnp.float32)
    square_sum = (
        jnp.sum(table_grad * table_grad)
        + jnp.sum(dense_grad * dense_grad)
        + jnp.sum(ffn_grad * ffn_grad)
        + jnp.sum(small_share * small_share)
    )
    own_count = jnp.sum(own_lengths).astype(jnp.float32)
    message = jnp.concatenate([small_share, jnp.stack([square_sum, own_count, loss_own])])
    message = jnp.pad(message, (0, -message.shape[0] % 128))
    told = exchange(jnp.broadcast_to(message[None], (n_dev, message.shape[0])))
    scalars = jnp.sum(told[:, share : share + 3], axis=0)
    total_square, token_count, loss_sum = scalars[0], scalars[1], scalars[2]
    small_all = told[:, :share].reshape(-1)
    gains_size = norm_gains.size
    gains_grad = small_all[:gains_size].reshape(norm_gains.shape)
    class_grad = small_all[gains_size : gains_size + classifier.size].reshape(classifier.shape)
    inverse = 1.0 / token_count
    grad_norm = jnp.sqrt(total_square) * inverse
    scaling = inverse * (clip_bound / jnp.maximum(grad_norm, clip_bound))
    table_new = adam_update(
        embed_table, table_grad * scaling, embed_moment, embed_square, weight_decay, learn_rate
    )
    dense_new = adam_update(
        dense_weights, dense_grad * scaling, dense_moment, dense_square, weight_decay, learn_rate
    )
    ffn_new = adam_update(
        feedforward,
        ffn_grad * scaling,
        feedforward_moment,
        feedforward_square,
        weight_decay,
        learn_rate,
    )
    class_new = adam_update(
        classifier,
        class_grad * scaling,
        classifier_moment,
        classifier_square,
        weight_decay,
        learn_rate,
    )
    gains_new = adam_update(
        norm_gains, gains_grad * scaling, norm_moment, norm_square, 0.0, gain_rate
    )
    return (
        loss_sum,
        token_count,
        grad_norm,
        table_new[0],
        table_new[1],
        table_new[2],
        table_new[0].astype(jnp.bfloat16),
        dense_new[0],
        dense_new[1],
        dense_new[2],
        dense_new[0].astype(jnp.bfloat16),
        ffn_new[0],
        ffn_new[1],
        ffn_new[2],
        ffn_new[0].astype(jnp.bfloat16),
        class_new[0],
        class_new[1],
        class_new[2],
        class_new[0].astype(jnp.bfloat16),
        gains_new[0],
        gains_new[1],
        gains_new[2],
    )


def solution(mesh):
    placed = (
        P("dp", None),
        P("dp", None),
        P("dp", None),
        P("dp"),
        P("dp"),
        P(("dp", "mp"), None, None),
        P(("dp", "mp"), None, None),
        P(("dp", "mp"), None),
        P(("dp", "mp"), None),
        P(("dp", "mp"), None),
        P(("dp", "mp"), None),
        P(("dp", "mp"), None),
        P(("dp", "mp"), None),
        P(("dp", "mp"), None),
        P(("dp", "mp"), None),
        P(("dp", "mp"), None),
        P(("dp", "mp"), None),
        P(),
        P(),
        P(),
        P(),
        P(),
        P(),
    )
    return jax.shard_map(
        per_device,
        mesh=mesh,
        in_specs=placed,
        out_specs=(
            P(),
            P(),
            P(),
            P(("dp", "mp"), None),
            P(("dp", "mp"), None),
            P(("dp", "mp"), None),
            P(("dp", "mp"), None),
            P(("dp", "mp"), None),
            P(("dp", "mp"), None),
            P(("dp", "mp"), None),
            P(("dp", "mp"), None),
            P(("dp", "mp"), None),
            P(("dp", "mp"), None),
            P(("dp", "mp"), None),
            P(("dp", "mp"), None),
            P(),
            P(),
            P(),
            P(),
            P(),
            P(),
            P(),
        ),
        check_vma=False,
    )
```

```python
import jax
import jax.numpy as jnp
from jax import lax
from jax.experimental import pallas as pl
from jax.experimental.pallas import tpu as pltpu
from jax.sharding import PartitionSpec as P

MODEL_WIDTH = 768
HEADS = 12
FF = 3072
L = 128
LEVELS = 4
STEP = 10


highest_precision = lax.Precision.HIGHEST
norm_epsilon = 1e-05
learn_rate = 0.05
gain_rate = 0.5
beta_one = 0.9
beta_two = 0.999
adam_epsilon = 1e-08
weight_decay = 0.01
clip_bound = 1.0


def norm_forward(values, gain_row, shift_row):
    center = values - jnp.mean(values, axis=-1, keepdims=True)
    spread = jnp.mean(center * center, axis=-1, keepdims=True)
    inverse = lax.rsqrt(spread + norm_epsilon)
    unit = center * inverse
    return (unit * gain_row + shift_row, unit, inverse)


def norm_backward(grad, unit, inverse, gain_row):
    scaled = grad * gain_row
    level = jnp.mean(scaled, axis=-1, keepdims=True)
    along = jnp.mean(scaled * unit, axis=-1, keepdims=True)
    grad_values = inverse * (scaled - level - unit * along)
    return (grad_values, jnp.sum(grad * unit, axis=0), jnp.sum(grad, axis=0))


gelu_rate = 0.7978845608028654
gelu_cube = 0.044715


def gelu_forward(before):
    bend = jnp.tanh(gelu_rate * (before + gelu_cube * before * before * before))
    return 0.5 * before * (1.0 + bend)


def gelu_slope(before):
    bend = jnp.tanh(gelu_rate * (before + gelu_cube * before * before * before))
    inner = gelu_rate * (1.0 + 3.0 * gelu_cube * before * before)
    return 0.5 * (1.0 + bend) + 0.5 * before * (1.0 - bend * bend) * inner


def adam_update(weight, gradient, first_moment, second, decay_rate, rate):
    first_new = beta_one * first_moment + (1.0 - beta_one) * gradient
    second_new = beta_two * second + (1.0 - beta_two) * gradient * gradient
    direction = (
        first_new
        / (1.0 - beta_one**STEP)
        / (jnp.sqrt(second_new / (1.0 - beta_two**STEP)) + adam_epsilon)
    )
    return (weight - rate * (direction + decay_rate * weight), first_new, second_new)


def contract_last(left, right):
    return lax.dot_general(
        left, right, (((1,), (1,)), ((), ())), preferred_element_type=jnp.float32
    )


def contract_first(left, right):
    return lax.dot_general(
        left, right, (((0,), (0,)), ((), ())), preferred_element_type=jnp.float32
    )


def flip(block, bit):
    size = lax.axis_size("dp")
    return lax.ppermute(block, "dp", [(i, i ^ bit) for i in range(size)])


def add_low(*terms):
    return sum(term.astype(jnp.float32) for term in terms).astype(jnp.bfloat16)


piece_codes = (0, 2, 6, 4, 1, 3, 7, 5)


def gather_near(own):
    return own, flip(own, 2), flip(own, 4)


def gather_far(own, along_x, along_y):
    half = own.shape[0] // 2
    far_top, far_low = flip(along_x[:half], 4), flip(along_y[half:], 2)
    mine = [own, along_x, far_top, far_low, along_y]
    return mine + [flip(block, 1) for block in mine]


def assemble_kernel(place_ref, *refs):
    pieces, full_ref, arrivals = refs[:10], refs[10], refs[11]
    chunk = pieces[0].shape[0]
    copies = []
    for block, piece in enumerate(pieces):
        code = (0, 2, 6, 6, 4)[block % 5] + block // 5
        at = (place_ref[0] ^ code) * chunk
        if block % 5 == 3:
            at = at + chunk // 2
        at = pl.multiple_of(at, 16)
        copies.append(
            pltpu.make_async_copy(piece, full_ref.at[pl.ds(at, piece.shape[0])], arrivals.at[block])
        )
    for copy in copies:
        copy.start()
    for copy in copies:
        copy.wait()


def assemble(place, pieces):
    chunk, width = pieces[0].shape
    return pl.pallas_call(
        assemble_kernel,
        in_specs=[pl.BlockSpec(memory_space=pltpu.SMEM)] + [pl.BlockSpec(memory_space=pl.ANY)] * len(pieces),
        out_specs=pl.BlockSpec(memory_space=pltpu.VMEM),
        out_shape=jax.ShapeDtypeStruct((8 * chunk, width), pieces[0].dtype),
        compiler_params=pltpu.CompilerParams(vmem_limit_bytes=VMEM_BYTES),
        scratch_shapes=[pltpu.SemaphoreType.DMA((len(pieces),))],
        cost_estimate=pl.CostEstimate(flops=0, bytes_accessed=32 * chunk * width, transcendentals=0),
        name="assemble",
    )(place.reshape(1), *pieces)


def partner(index, step):
    size = lax.axis_size("mp")
    return index ^ step if size & (size - 1) == 0 else (index + step) % size


def pass_mp(block, step):
    return lax.ppermute(block, "mp", [(i, partner(i, step)) for i in range(lax.axis_size("mp"))])


def gather_mp(rows):
    return [rows] + [pass_mp(rows, step) for step in range(1, lax.axis_size("mp"))]


def sum_mp(blocks):
    total = blocks[0].astype(jnp.float32)
    for step in range(1, lax.axis_size("mp")):
        total = total + pass_mp(blocks[step], step).astype(jnp.float32)
    return total


def send_first(top, low):
    size = top.shape[0] // 4
    from_x = flip(top[size : 3 * size], 2)
    from_y = flip(low[2 * size :], 4)
    late_y = add_low(top[3 * size :], from_x[size:])
    late_x = add_low(low[size : 2 * size], from_y[:size])
    return top[:size], low[:size], from_x[:size], from_y[size:], late_y, late_x


def send_last(top, low, from_x, from_y, late_y, late_x):
    late_y, late_x = flip(late_y, 4), flip(late_x, 2)
    return add_low(top, from_x, late_y), add_low(low, from_y, late_x)


def together(*values):
    return lax.optimization_barrier(values)


PAIR = 2 * (MODEL_WIDTH // HEADS)
PAIRS = HEADS // 2
BLOCK = 2 * L
VMEM_BYTES = 56 * 1024 * 1024


def dot_nt(left, right):
    return lax.dot_general(
        left, right, (((1,), (1,)), ((), ())), preferred_element_type=jnp.float32
    )


def dot_tn(left, right):
    return lax.dot_general(
        left, right, (((0,), (0,)), ((), ())), preferred_element_type=jnp.float32
    )


def dot_nn(left, right):
    return jnp.dot(left, right, preferred_element_type=jnp.float32)


def both_heads(pair, left_half):
    zero = jnp.zeros_like(pair)
    return jnp.concatenate([jnp.where(left_half, pair, zero), jnp.where(left_half, zero, pair)], axis=0)


def pair_attend(queries, keys, key_bias):
    scores = dot_nt(queries, keys) * (MODEL_WIDTH // HEADS) ** (-0.5) + key_bias
    raised = jnp.exp(scores - jnp.max(scores, axis=-1, keepdims=True))
    return raised * (1.0 / jnp.sum(raised, axis=-1, keepdims=True))


def attention_kernel(
    length_ref, level_ref, embed_ref, qkv_ref, out_ref, gains_ref, project_ref, mixture_ref, first_ref, normed_ref
):
    step = pl.program_id(0)
    normed, _, _ = norm_forward(embed_ref[...].astype(jnp.float32), gains_ref[0:1], gains_ref[1:2])
    normed_low = normed.astype(jnp.bfloat16)
    normed_ref[...] = normed_low
    for part in range(3):
        columns = slice(part * MODEL_WIDTH, (part + 1) * MODEL_WIDTH)
        project_ref[:, columns] = dot_nt(normed_low, qkv_ref[columns]).astype(jnp.bfloat16)
    lane = lax.broadcasted_iota(jnp.int32, (L, PAIR), 1)
    left_half = lane < PAIR // 2
    for seq in range(BLOCK // L):
        rows = slice(seq * L, (seq + 1) * L)
        length = length_ref[step * (BLOCK // L) + seq]
        heads = level_ref[step * (BLOCK // L) + seq] * (HEADS // LEVELS)
        key_bias = jnp.where(lax.broadcasted_iota(jnp.int32, (1, L), 1) < length, 0.0, -1000000000.0)
        for pair in range(PAIRS):
            at = pair * PAIR
            queries = both_heads(project_ref[rows, at : at + PAIR], left_half)
            keys = project_ref[rows, MODEL_WIDTH + at : MODEL_WIDTH + at + PAIR]
            values = project_ref[rows, 2 * MODEL_WIDTH + at : 2 * MODEL_WIDTH + at + PAIR]
            attend = pair_attend(queries, keys, key_bias).astype(jnp.bfloat16)
            mixed = dot_nn(attend, values)
            mixed = jnp.where(left_half, mixed[:L], mixed[L:])
            head = 2 * pair + (lane >= PAIR // 2).astype(jnp.int32)
            mixture_ref[rows, at : at + PAIR] = jnp.where(head < heads, mixed, 0.0).astype(jnp.bfloat16)
    first_ref[...] = normed + dot_nn(mixture_ref[...], out_ref[...])


def whole(shape):
    return pl.BlockSpec(shape, lambda step: (0,) * len(shape))


def by_rows(width):
    return pl.BlockSpec((BLOCK, width), lambda step: (step, 0))


def attention_layer(own_lengths, own_levels, embedded, dense_full, norm_gains):
    rows = embedded.shape[0]
    low = jnp.bfloat16
    return pl.pallas_call(
        attention_kernel,
        grid=(rows // BLOCK,),
        in_specs=[
            pl.BlockSpec(memory_space=pltpu.SMEM),
            pl.BlockSpec(memory_space=pltpu.SMEM),
            by_rows(MODEL_WIDTH),
            whole((3 * MODEL_WIDTH, MODEL_WIDTH)),
            pl.BlockSpec((MODEL_WIDTH, MODEL_WIDTH), lambda step: (3, 0)),
            whole((6, MODEL_WIDTH)),
        ],
        out_specs=[by_rows(3 * MODEL_WIDTH), by_rows(MODEL_WIDTH), by_rows(MODEL_WIDTH), by_rows(MODEL_WIDTH)],
        out_shape=[
            jax.ShapeDtypeStruct((rows, 3 * MODEL_WIDTH), low),
            jax.ShapeDtypeStruct((rows, MODEL_WIDTH), low),
            jax.ShapeDtypeStruct((rows, MODEL_WIDTH), jnp.float32),
            jax.ShapeDtypeStruct((rows, MODEL_WIDTH), low),
        ],
        compiler_params=pltpu.CompilerParams(vmem_limit_bytes=VMEM_BYTES),
        cost_estimate=pl.CostEstimate(
            flops=rows * MODEL_WIDTH * MODEL_WIDTH * 10, bytes_accessed=rows * MODEL_WIDTH * 16, transcendentals=0
        ),
        name="attention_layer",
    )(own_lengths, own_levels, embedded, dense_full, dense_full, norm_gains)


def attention_back_kernel(
    start,
    length_ref,
    level_ref,
    grad_ref,
    first_ref,
    project_ref,
    embed_ref,
    teacher_ref,
    qkv_ref,
    out_ref,
    gains_ref,
    grad_project_ref,
    grad_att_ref,
    grad_embed_ref,
    sums_ref,
    grad_mixture_ref,
):
    turn = pl.program_id(0)
    step = turn + start
    low = jnp.bfloat16
    _, unit_one, inverse_one = norm_forward(first_ref[...], gains_ref[2:3], gains_ref[3:4])
    grad_first, gain_one, shift_one = norm_backward(grad_ref[...], unit_one, inverse_one, gains_ref[2:3])
    grad_att = grad_first.astype(low)
    grad_att_ref[...] = grad_att
    grad_mixture_ref[...] = dot_nt(grad_att, out_ref[...]).astype(low)
    lane = lax.broadcasted_iota(jnp.int32, (L, PAIR), 1)
    left_half = lane < PAIR // 2
    scaling = (MODEL_WIDTH // HEADS) ** (-0.5)
    usable = []
    for seq in range(BLOCK // L):
        rows = slice(seq * L, (seq + 1) * L)
        length = length_ref[step * (BLOCK // L) + seq]
        heads = level_ref[step * (BLOCK // L) + seq] * (HEADS // LEVELS)
        usable.append((lax.broadcasted_iota(jnp.int32, (L, 1), 0) < length).astype(jnp.float32))
        key_bias = jnp.where(lax.broadcasted_iota(jnp.int32, (1, L), 1) < length, 0.0, -1000000000.0)
        for pair in range(PAIRS):
            at = pair * PAIR
            queries = both_heads(project_ref[rows, at : at + PAIR], left_half)
            keys = project_ref[rows, MODEL_WIDTH + at : MODEL_WIDTH + at + PAIR]
            values = project_ref[rows, 2 * MODEL_WIDTH + at : 2 * MODEL_WIDTH + at + PAIR]
            attend = pair_attend(queries, keys, key_bias)
            head = 2 * pair + (lane >= PAIR // 2).astype(jnp.int32)
            mixture = grad_mixture_ref[rows, at : at + PAIR]
            mixture = both_heads(jnp.where(head < heads, mixture, jnp.zeros_like(mixture)), left_half)
            grad_values = dot_tn(attend.astype(low), mixture)
            grad_attend = dot_nt(mixture, values)
            level = jnp.sum(grad_attend * attend, axis=-1, keepdims=True)
            grad_scores = (attend * (grad_attend - level)).astype(low)
            grad_queries = dot_nn(grad_scores, keys) * scaling
            grad_queries = jnp.where(left_half, grad_queries[:L], grad_queries[L:])
            grad_keys = dot_tn(grad_scores, queries) * scaling
            grad_project_ref[rows, at : at + PAIR] = grad_queries.astype(low)
            grad_project_ref[rows, MODEL_WIDTH + at : MODEL_WIDTH + at + PAIR] = grad_keys.astype(low)
            grad_project_ref[rows, 2 * MODEL_WIDTH + at : 2 * MODEL_WIDTH + at + PAIR] = grad_values.astype(low)
    normed, unit_base, inverse_base = norm_forward(
        embed_ref[...].astype(jnp.float32), gains_ref[0:1], gains_ref[1:2]
    )
    usable = jnp.concatenate(usable, axis=0)
    gap = usable * (normed - teacher_ref[...].astype(jnp.float32))
    grad_normed = grad_first + 2.0 * gap + dot_nn(grad_project_ref[...], qkv_ref[...])
    grad_embed, gain_base, shift_base = norm_backward(grad_normed, unit_base, inverse_base, gains_ref[0:1])
    grad_embed_ref[...] = grad_embed.astype(low)

    @pl.when(turn == 0)
    def _():
        sums_ref[...] = jnp.zeros_like(sums_ref)

    for row, value in enumerate((gain_base, shift_base, gain_one, shift_one, jnp.sum(gap * gap, axis=0))):
        sums_ref[row : row + 1] += value[None]


def attention_backward(start, steps, scalars, arrays, weights, before):
    rows = arrays[0].shape[0]
    low = jnp.bfloat16

    def at_rows(width):
        return pl.BlockSpec((BLOCK, width), lambda step: (step + start, 0))

    widths = (MODEL_WIDTH, MODEL_WIDTH, 3 * MODEL_WIDTH, MODEL_WIDTH, MODEL_WIDTH)
    count = len(before)

    def body(length_ref, level_ref, *refs):
        attention_back_kernel(start, length_ref, level_ref, *refs[:8], *refs[8 + count :])

    return pl.pallas_call(
        body,
        grid=(steps,),
        in_specs=[pl.BlockSpec(memory_space=pltpu.SMEM)] * 2
        + [at_rows(width) for width in widths]
        + [
            whole((3 * MODEL_WIDTH, MODEL_WIDTH)),
            pl.BlockSpec((MODEL_WIDTH, MODEL_WIDTH), lambda step: (3, 0)),
            whole((6, MODEL_WIDTH)),
        ]
        + [pl.BlockSpec(memory_space=pl.ANY)] * count,
        out_specs=[at_rows(3 * MODEL_WIDTH), at_rows(MODEL_WIDTH), at_rows(MODEL_WIDTH), whole((8, MODEL_WIDTH))],
        out_shape=[
            jax.ShapeDtypeStruct((rows, 3 * MODEL_WIDTH), low),
            jax.ShapeDtypeStruct((rows, MODEL_WIDTH), low),
            jax.ShapeDtypeStruct((rows, MODEL_WIDTH), low),
            jax.ShapeDtypeStruct((8, MODEL_WIDTH), jnp.float32),
        ],
        input_output_aliases={10 + place: place for place in range(count)},
        scratch_shapes=[pltpu.VMEM((BLOCK, MODEL_WIDTH), low)],
        compiler_params=pltpu.CompilerParams(vmem_limit_bytes=VMEM_BYTES),
        cost_estimate=pl.CostEstimate(
            flops=steps * BLOCK * MODEL_WIDTH * MODEL_WIDTH * 40,
            bytes_accessed=steps * BLOCK * MODEL_WIDTH * 24,
            transcendentals=0,
        ),
        name="attention_backward",
    )(*scalars, *arrays, *weights, *before)


FFN_CHUNK = 768


def split_low(value):
    upper = value.astype(jnp.bfloat16)
    return jnp.concatenate([upper, (value - upper.astype(jnp.float32)).astype(jnp.bfloat16)], axis=0)


def ffn_kernel(sizes, length_ref, level_ref, first_ref, teacher_ref, pool_ref, class_ref, logits_ref, gains_ref, index_ref, *refs):
    pieces = refs[: len(sizes)]
    (hidden_ref, grad_before_ref, grad_feed_ref, middle_ref, grad_middle_ref, grad_pool_ref, grad_class_ref, sums_ref) = refs[
        len(sizes) : len(sizes) + 8
    ]
    weights_ref, slope_ref, unit_ref, inverse_ref, pooled_rows_ref, grad_rows_ref, arrivals = refs[len(sizes) + 8 :]
    step = pl.program_id(0)
    blocks = slope_ref.shape[0]
    seqs = BLOCK // L
    low = jnp.bfloat16
    row = lax.broadcasted_iota(jnp.int32, (BLOCK, 1), 0)

    def copies():
        at = 0
        for place, size in enumerate(sizes):
            yield pltpu.make_async_copy(pieces[place], weights_ref.at[pl.ds(at, size)], arrivals.at[place])
            at += size

    @pl.when(step == 0)
    def _():
        for copy in copies():
            copy.start()
        for copy in copies():
            copy.wait()
        sums_ref[...] = jnp.zeros_like(sums_ref)

    @pl.when(step < blocks)
    def _():
        middle, _, _ = norm_forward(first_ref[...], gains_ref[2:3], gains_ref[3:4])
        middle_low = middle.astype(low)
        middle_ref[...] = middle_low
        limit = jnp.full((BLOCK, 1), level_ref[step * seqs])
        for seq in range(1, seqs):
            limit = jnp.where(row >= seq * L, level_ref[step * seqs + seq], limit)
        limit = limit * (FF // LEVELS)
        for at in range(0, FF, FFN_CHUNK):
            columns = slice(at, at + FFN_CHUNK)
            before = dot_nt(middle_low, weights_ref[columns, :MODEL_WIDTH])
            square = before * before
            bend = jnp.tanh(before * (gelu_rate + gelu_rate * gelu_cube * square))
            rise = 0.5 + 0.5 * bend
            value = before * rise
            slope = rise + (0.5 * before) * (1.0 - bend * bend) * (gelu_rate + 3.0 * gelu_rate * gelu_cube * square)
            on = index_ref[:, columns] < limit
            hidden_ref[:, columns] = jnp.where(on, value, 0.0).astype(low)
            slope_ref[step, :, columns] = jnp.where(on, slope, 0.0).astype(low)
        feed = dot_nn(hidden_ref[...], weights_ref[:, MODEL_WIDTH:])
        output, unit, inverse = norm_forward(middle + feed, gains_ref[4:5], gains_ref[5:6])
        unit_ref[step] = unit
        inverse_ref[step] = inverse
        for seq in range(seqs):
            pooled_rows_ref[pl.ds(step * seqs + seq, 1), :] = output[seq * L : seq * L + 1]

    @pl.when(step == blocks)
    def _():
        first_low = pooled_rows_ref[...].astype(low)
        pooled = jnp.tanh(dot_nn(first_low, pool_ref[...]))
        pooled_low = pooled.astype(low)
        gap = dot_nn(pooled_low, class_ref[...]) - logits_ref[...]
        grad_logits = split_low(2.0 * L * gap)
        rows = gap.shape[0]
        grad_class_ref[...] = dot_tn(jnp.concatenate([pooled_low, pooled_low], axis=0), grad_logits)
        grad_pooled = dot_nt(grad_logits, class_ref[...])
        grad_inner = split_low((grad_pooled[:rows] + grad_pooled[rows:]) * (1.0 - pooled * pooled))
        grad_pool_ref[...] = dot_tn(jnp.concatenate([first_low, first_low], axis=0), grad_inner).astype(low)
        grad_rows = dot_nt(grad_inner, pool_ref[...])
        grad_rows_ref[...] = grad_rows[:rows] + grad_rows[rows:]
        sums_ref[3:4, : gap.shape[1]] += L * jnp.sum(gap * gap, axis=0, keepdims=True)

    @pl.when(step > blocks)
    def _():
        block = step - blocks - 1
        unit = unit_ref[block]
        reach = jnp.full((BLOCK, 1), length_ref[block * seqs])
        pooled_grad = jnp.where(row == 0, grad_rows_ref[pl.ds(block * seqs, 1), :], 0.0)
        for seq in range(1, seqs):
            reach = jnp.where(row >= seq * L, length_ref[block * seqs + seq] + seq * L, reach)
            pooled_grad = jnp.where(row == seq * L, grad_rows_ref[pl.ds(block * seqs + seq, 1), :], pooled_grad)
        output = unit * gains_ref[4:5] + gains_ref[5:6]
        gap = jnp.where(row < reach, output - teacher_ref[...].astype(jnp.float32), 0.0)
        grad_second, gain, shift = norm_backward(2.0 * gap + pooled_grad, unit, inverse_ref[block], gains_ref[4:5])
        grad_feed = grad_second.astype(low)
        grad_feed_ref[...] = grad_feed
        for at in range(0, FF, FFN_CHUNK):
            columns = slice(at, at + FFN_CHUNK)
            grad_hidden = dot_nt(grad_feed, weights_ref[columns, MODEL_WIDTH:])
            grad_before_ref[:, columns] = (grad_hidden * slope_ref[block, :, columns].astype(jnp.float32)).astype(low)
        grad_middle_ref[...] = grad_second + dot_nn(grad_before_ref[...], weights_ref[:, :MODEL_WIDTH])
        for place, value in enumerate((gain, shift, jnp.sum(gap * gap, axis=0))):
            sums_ref[place : place + 1] += value[None]


def ffn_layer(scalars, first, teacher, dense_full, class_wide, logits_wide, norm_gains, neuron_index, pieces):
    rows = first.shape[0]
    seqs = rows // L
    blocks = rows // BLOCK
    low = jnp.bfloat16
    sizes = tuple(piece.shape[0] for piece in pieces)

    def going(width):
        return pl.BlockSpec((BLOCK, width), lambda step: (jnp.minimum(step, blocks - 1), 0))

    def coming(width):
        return pl.BlockSpec((BLOCK, width), lambda step: (jnp.maximum(step - blocks - 1, 0), 0))

    return pl.pallas_call(
        lambda *refs: ffn_kernel(sizes, *refs),
        grid=(2 * blocks + 1,),
        in_specs=[
            pl.BlockSpec(memory_space=pltpu.SMEM),
            pl.BlockSpec(memory_space=pltpu.SMEM),
            going(MODEL_WIDTH),
            coming(MODEL_WIDTH),
            pl.BlockSpec((MODEL_WIDTH, MODEL_WIDTH), lambda step: (4, 0)),
            whole(class_wide.shape),
            whole(logits_wide.shape),
            whole((6, MODEL_WIDTH)),
            whole((1, FF)),
        ]
        + [pl.BlockSpec(memory_space=pl.ANY)] * len(sizes),
        out_specs=[
            going(FF),
            coming(FF),
            coming(MODEL_WIDTH),
            going(MODEL_WIDTH),
            coming(MODEL_WIDTH),
            whole((MODEL_WIDTH, MODEL_WIDTH)),
            whole(class_wide.shape),
            whole((8, MODEL_WIDTH)),
        ],
        out_shape=[
            jax.ShapeDtypeStruct((rows, FF), low),
            jax.ShapeDtypeStruct((rows, FF), low),
            jax.ShapeDtypeStruct((rows, MODEL_WIDTH), low),
            jax.ShapeDtypeStruct((rows, MODEL_WIDTH), low),
            jax.ShapeDtypeStruct((rows, MODEL_WIDTH), jnp.float32),
            jax.ShapeDtypeStruct((MODEL_WIDTH, MODEL_WIDTH), low),
            jax.ShapeDtypeStruct(class_wide.shape, jnp.float32),
            jax.ShapeDtypeStruct((8, MODEL_WIDTH), jnp.float32),
        ],
        scratch_shapes=[
            pltpu.VMEM((FF, 2 * MODEL_WIDTH), low),
            pltpu.VMEM((blocks, BLOCK, FF), low),
            pltpu.VMEM((blocks, BLOCK, MODEL_WIDTH), jnp.float32),
            pltpu.VMEM((blocks, BLOCK, 1), jnp.float32),
            pltpu.VMEM((seqs, MODEL_WIDTH), jnp.float32),
            pltpu.VMEM((seqs, MODEL_WIDTH), jnp.float32),
            pltpu.SemaphoreType.DMA((len(sizes),)),
        ],
        compiler_params=pltpu.CompilerParams(vmem_limit_bytes=VMEM_BYTES),
        cost_estimate=pl.CostEstimate(
            flops=rows * MODEL_WIDTH * FF * 16, bytes_accessed=rows * FF * 8, transcendentals=rows * FF
        ),
        name="ffn_layer",
    )(*scalars, first, teacher, dense_full, class_wide, logits_wide, norm_gains, neuron_index, *pieces)


def per_device(
    token_ids,
    replacements,
    replaced,
    lengths,
    widths,
    teacher_embed,
    teacher_hidden,
    teacher_logits,
    embed_table,
    embed_moment,
    embed_square,
    dense_weights,
    dense_moment,
    dense_square,
    feedforward,
    feedforward_moment,
    feedforward_square,
    classifier,
    classifier_moment,
    classifier_square,
    norm_gains,
    norm_moment,
    norm_square,
):
    both = ("dp", "mp")
    mp_count = lax.axis_size("mp")
    mp_index = lax.axis_index("mp")
    n_dev = lax.axis_size("dp") * mp_count
    own_seqs = teacher_logits.shape[0]
    own_rows = own_seqs * L
    table_rows = embed_table.shape[0]
    low = jnp.bfloat16
    by_bits = lax.axis_size("dp") == 8 and mp_count & (mp_count - 1) == 0
    if by_bits:
        dense_steps = gather_mp(dense_weights.astype(low))
        dense_column = jnp.concatenate(
            [lax.select_n(mp_index, *[dense_steps[k ^ z] for z in range(mp_count)]) for k in range(mp_count)],
            axis=0,
        )
    else:
        dense_column = lax.all_gather(dense_weights.astype(low), "mp", axis=0, tiled=True)
    dp_index = lax.axis_index("dp")
    neuron_piece = feedforward.shape[0]
    neuron_slot = jnp.arange(FF)
    if by_bits:
        chunk = neuron_piece * mp_count
        codes = jnp.repeat(jnp.array(piece_codes), chunk, total_repeat_length=FF)
        steps = neuron_slot % chunk // neuron_piece
        neuron_index = (dp_index ^ codes) * chunk + (mp_index ^ steps) * neuron_piece + neuron_slot % neuron_piece
    else:
        neuron_index = neuron_slot
    table_low = embed_table.astype(low)

    depth = -(-(own_rows * 3 // 2) // (n_dev * 16)) * 16
    capacity = depth - 1
    own_start = mp_index * own_seqs
    own_ids = lax.dynamic_slice_in_dim(
        jnp.where(replaced == 1, replacements, token_ids), own_start, own_seqs
    ).reshape(own_rows)
    owner = own_ids // table_rows
    local = own_ids - owner * table_rows
    place = jnp.arange(own_rows)
    first = jnp.min(
        jnp.where(own_ids[:, None] == own_ids[None, :], place[None, :], own_rows), axis=1
    )
    leads = first == place
    slot = jnp.sum(
        (leads[None, :] & (owner[:, None] == owner[None, :]) & (place[None, :] < first[:, None])).astype(
            jnp.int32
        ),
        axis=1,
    )
    deepest = jnp.max(slot)

    def positions(turn):
        rank = slot - turn * capacity
        return jnp.where((rank >= 0) & (rank < capacity), owner * depth + rank, -1)

    def wanted(turn):
        spot = jnp.where(leads, positions(turn), -1)
        hits = spot[:, None] == jnp.arange(n_dev * depth)[None, :]
        rows = jnp.max(jnp.where(hits, local[:, None], -1), axis=0).reshape(n_dev, depth)
        return jnp.where(jnp.arange(depth)[None, :] == capacity, deepest, rows)

    def exchange(blocks):
        return lax.all_to_all(blocks, both, split_axis=0, concat_axis=0)

    def asked_hot(asked):
        flat = jnp.where(jnp.arange(depth)[None, :] < capacity, asked, -1).reshape(-1)
        return (flat[:, None] == jnp.arange(table_rows)[None, :]).astype(low)

    def own_hot(turn):
        return (positions(turn)[:, None] == jnp.arange(n_dev * depth)[None, :]).astype(low)

    def answer(asked, *others):
        rows = jnp.dot(asked_hot(asked), table_low, preferred_element_type=low)
        rows, *others = together(rows.reshape(n_dev, depth, MODEL_WIDTH), *others)
        return exchange(rows).reshape(-1, MODEL_WIDTH), *others

    def place_rows(turn, rows):
        return jnp.dot(own_hot(turn), rows, preferred_element_type=low)

    dense_column, ffn_low = together(dense_column, feedforward.astype(low))
    asked_first = exchange(wanted(0))
    turns = jnp.max(asked_first[:, capacity]) // capacity + 1
    if by_bits:
        ffn_column = jnp.concatenate(gather_mp(ffn_low), axis=0)
        rows_first, ffn_column, *dense_near = answer(asked_first, ffn_column, *gather_near(dense_column))
        ffn_near = gather_near(ffn_column)
        dense_full = assemble(dp_index, gather_far(*dense_near))
        rows_first, dense_full, *ffn_near = together(rows_first, dense_full, *ffn_near)
        ffn_pieces = gather_far(*ffn_near)
    else:
        dense_full = lax.all_gather(dense_column, "dp", axis=0, tiled=True)
        ffn_column = lax.all_gather(ffn_low, "mp", axis=0, tiled=True)
        ffn_pieces = [lax.all_gather(ffn_column, "dp", axis=0, tiled=True)]
        rows_first, = answer(asked_first)
    embedded_low = lax.while_loop(
        lambda state: state[0] < turns,
        lambda state: (
            state[0] + 1,
            state[1] + place_rows(state[0], answer(exchange(wanted(state[0])))[0]),
        ),
        (jnp.int32(1), place_rows(0, rows_first)),
    )[1]

    own_lengths = lax.dynamic_slice_in_dim(lengths, own_start, own_seqs)
    own_levels = lax.dynamic_slice_in_dim(widths, own_start, own_seqs)
    scalars = (own_lengths, own_levels)
    project, head_mixture, first_sum, normed_low = attention_layer(
        own_lengths, own_levels, embedded_low, dense_full, norm_gains
    )
    class_pad = -classifier.shape[1] % 128
    hidden_low, grad_before, grad_feed_low, middle_low, grad_middle, grad_pool_rows, grad_class, ffn_sums = ffn_layer(
        scalars,
        first_sum,
        teacher_hidden.reshape(own_rows, MODEL_WIDTH),
        dense_full,
        jnp.pad(classifier, ((0, 0), (0, class_pad))).astype(low),
        jnp.pad(teacher_logits, ((0, 0), (0, class_pad))),
        norm_gains,
        neuron_index[None, :],
        ffn_pieces,
    )
    grad_class = grad_class[:, : classifier.shape[1]]

    def over_both(rows):
        rows = lax.psum_scatter(rows, "dp", scatter_dimension=0, tiled=True)
        return lax.psum_scatter(rows, "mp", scatter_dimension=0, tiled=True).astype(jnp.float32)

    def weight_sums(left, right):
        half = left.shape[1] // 2
        given = flip(contract_first(left[:, half:], right).astype(low), 1)
        return contract_first(left[:, :half], right).astype(low), given

    def dense_scatter(rows):
        if not by_bits:
            return over_both(rows)
        chunks = rows.reshape(4, 2, rows.shape[0] // 8, rows.shape[1])
        core = dp_index % 2
        place = dp_index // 2
        parts = add_low(
            lax.dynamic_index_in_dim(chunks, core, 1, keepdims=False),
            flip(lax.dynamic_index_in_dim(chunks, 1 - core, 1, keepdims=False), 1),
        )
        half = parts.shape[1] // 2
        parts = [lax.dynamic_index_in_dim(parts, place ^ code, 0, keepdims=False) for code in (0, 1, 3, 2)]
        top = jnp.concatenate([part[:half] for part in parts], axis=0)
        rest = jnp.concatenate([part[half:] for part in parts], axis=0)
        parts = jnp.concatenate(send_last(*send_first(top, rest)), axis=0).reshape(mp_count, -1, rows.shape[1])
        return sum_mp([lax.dynamic_index_in_dim(parts, mp_index ^ step, 0, keepdims=False) for step in range(mp_count)])

    arrays = [
        grad_middle,
        first_sum,
        project,
        embedded_low,
        teacher_embed.reshape(own_rows, MODEL_WIDTH),
    ]
    weights = (dense_full, dense_full, norm_gains)
    blocks = own_rows // BLOCK
    if by_bits:
        down_own, down_given = weight_sums(hidden_low, grad_feed_low)
        up_own, up_given = weight_sums(grad_before, middle_low)
        parts = (add_low(up_own, up_given), add_low(down_own, down_given))
        arrays[0], *parts = together(arrays[0], *parts)
        parts = send_first(*parts)
        before = attention_backward(0, blocks - 2, scalars, arrays, weights, ())
        arrays[0], *flow = together(arrays[0], *before, *parts)
        *before, sums_one = flow[:4]
        parts = send_last(*flow[4:])
        before = attention_backward(blocks - 2, 1, scalars, arrays, weights, before)
        arrays[0], *flow = together(arrays[0], *before, *parts)
        *before, sums_two = flow[:4]
        parts = [part.reshape(mp_count, neuron_piece, MODEL_WIDTH) for part in flow[4:]]
        ffn_grad = sum_mp([jnp.concatenate([part[step] for part in parts], axis=1) for step in range(mp_count)])
        *before, sums_last = attention_backward(blocks - 1, 1, scalars, arrays, weights, before)
        sums = sums_one + sums_two + sums_last
    else:
        ffn_grad = jnp.concatenate(
            [contract_first(grad_before, middle_low), contract_first(hidden_low, grad_feed_low)], axis=1
        ).astype(low)
        ffn_grad = over_both(ffn_grad)
        *before, sums = attention_backward(0, blocks, scalars, arrays, weights, ())
    grad_project, grad_att_low, grad_embed_low = before
    grad_dense = jnp.concatenate(
        [
            contract_first(grad_project, normed_low).astype(low),
            contract_first(head_mixture, grad_att_low).astype(low),
            grad_pool_rows,
        ],
        axis=0,
    )
    grad_embed_low, grad_dense, ffn_grad = together(grad_embed_low, grad_dense, ffn_grad)
    loss_own = jnp.sum(sums[4]) + jnp.sum(ffn_sums[2:4])

    small = jnp.concatenate(
        [
            sums[:4].reshape(-1),
            ffn_sums[:2].reshape(-1),
            grad_class.reshape(-1),
        ]
    )
    share = -(-small.shape[0] // n_dev)
    small_parts = jnp.pad(small, (0, share * n_dev - small.shape[0])).reshape(n_dev, share)
    upper = lax.reduce_precision(small_parts, 8, 7)
    rider = jnp.concatenate([upper, small_parts - upper], axis=1).astype(low)
    rider = jnp.pad(rider, ((0, 0), (0, MODEL_WIDTH - 2 * share)))

    def give_back(turn):
        sums = lax.dot_general(
            own_hot(turn), grad_embed_low, (((0,), (0,)), ((), ())), preferred_element_type=jnp.float32
        )
        return sums.reshape(n_dev, depth, MODEL_WIDTH)

    def collect(asked, returned):
        return lax.dot_general(
            asked_hot(asked),
            returned.reshape(-1, MODEL_WIDTH),
            (((0,), (0,)), ((), ())),
            preferred_element_type=jnp.float32,
        )

    given = give_back(0)
    given = jnp.where(jnp.arange(depth)[None, :, None] == capacity, rider.astype(jnp.float32)[:, None, :], given)
    given = given.astype(low)
    returned = exchange(given)
    dense_grad = dense_scatter(grad_dense)
    table_grad = collect(asked_first, returned)
    table_grad = lax.while_loop(
        lambda state: state[0] < turns,
        lambda state: (
            state[0] + 1,
            state[1]
            + collect(exchange(wanted(state[0])), exchange(give_back(state[0]).astype(low))),
        ),
        (jnp.int32(1), table_grad),
    )[1]
    riders = jnp.sum(returned[:, capacity, : 2 * share].astype(jnp.float32), axis=0)
    small_share = riders[:share] + riders[share:]
    square_sum = (
        jnp.sum(table_grad * table_grad)
        + jnp.sum(dense_grad * dense_grad)
        + jnp.sum(ffn_grad * ffn_grad)
        + jnp.sum(small_share * small_share)
    )
    own_count = jnp.sum(own_lengths).astype(jnp.float32)
    message = jnp.concatenate([small_share, jnp.stack([square_sum, own_count, loss_own])])
    message = jnp.pad(message, (0, -message.shape[0] % 128))
    told = exchange(jnp.broadcast_to(message[None], (n_dev, message.shape[0])))
    scalars = jnp.sum(told[:, share : share + 3], axis=0)
    total_square, token_count, loss_sum = scalars[0], scalars[1], scalars[2]
    small_all = told[:, :share].reshape(-1)
    gains_size = norm_gains.size
    gains_grad = small_all[:gains_size].reshape(norm_gains.shape)
    class_grad = small_all[gains_size : gains_size + classifier.size].reshape(classifier.shape)
    inverse = 1.0 / token_count
    grad_norm = jnp.sqrt(total_square) * inverse
    scaling = inverse * (clip_bound / jnp.maximum(grad_norm, clip_bound))
    table_new = adam_update(
        embed_table, table_grad * scaling, embed_moment, embed_square, weight_decay, learn_rate
    )
    dense_new = adam_update(
        dense_weights, dense_grad * scaling, dense_moment, dense_square, weight_decay, learn_rate
    )
    ffn_new = adam_update(
        feedforward,
        ffn_grad * scaling,
        feedforward_moment,
        feedforward_square,
        weight_decay,
        learn_rate,
    )
    class_new = adam_update(
        classifier,
        class_grad * scaling,
        classifier_moment,
        classifier_square,
        weight_decay,
        learn_rate,
    )
    gains_new = adam_update(
        norm_gains, gains_grad * scaling, norm_moment, norm_square, 0.0, gain_rate
    )
    return (
        loss_sum,
        token_count,
        grad_norm,
        table_new[0],
        table_new[1],
        table_new[2],
        table_new[0].astype(jnp.bfloat16),
        dense_new[0],
        dense_new[1],
        dense_new[2],
        dense_new[0].astype(jnp.bfloat16),
        ffn_new[0],
        ffn_new[1],
        ffn_new[2],
        ffn_new[0].astype(jnp.bfloat16),
        class_new[0],
        class_new[1],
        class_new[2],
        class_new[0].astype(jnp.bfloat16),
        gains_new[0],
        gains_new[1],
        gains_new[2],
    )


def solution(mesh):
    placed = (
        P("dp", None),
        P("dp", None),
        P("dp", None),
        P("dp"),
        P("dp"),
        P(("dp", "mp"), None, None),
        P(("dp", "mp"), None, None),
        P(("dp", "mp"), None),
        P(("dp", "mp"), None),
        P(("dp", "mp"), None),
        P(("dp", "mp"), None),
        P(("dp", "mp"), None),
        P(("dp", "mp"), None),
        P(("dp", "mp"), None),
        P(("dp", "mp"), None),
        P(("dp", "mp"), None),
        P(("dp", "mp"), None),
        P(),
        P(),
        P(),
        P(),
        P(),
        P(),
    )
    return jax.shard_map(
        per_device,
        mesh=mesh,
        in_specs=placed,
        out_specs=(
            P(),
            P(),
            P(),
            P(("dp", "mp"), None),
            P(("dp", "mp"), None),
            P(("dp", "mp"), None),
            P(("dp", "mp"), None),
            P(("dp", "mp"), None),
            P(("dp", "mp"), None),
            P(("dp", "mp"), None),
            P(("dp", "mp"), None),
            P(("dp", "mp"), None),
            P(("dp", "mp"), None),
            P(("dp", "mp"), None),
            P(("dp", "mp"), None),
            P(),
            P(),
            P(),
            P(),
            P(),
            P(),
            P(),
        ),
        check_vma=False,
    )
```

```python
import jax
import jax.numpy as jnp
from jax import lax
from jax.experimental import pallas as pl
from jax.experimental.pallas import tpu as pltpu
from jax.sharding import PartitionSpec as P

MODEL_WIDTH = 768
HEADS = 12
FF = 3072
L = 128
LEVELS = 4
STEP = 10


highest_precision = lax.Precision.HIGHEST
norm_epsilon = 1e-05
learn_rate = 0.05
gain_rate = 0.5
beta_one = 0.9
beta_two = 0.999
adam_epsilon = 1e-08
weight_decay = 0.01
clip_bound = 1.0


def norm_forward(values, gain_row, shift_row):
    center = values - jnp.mean(values, axis=-1, keepdims=True)
    spread = jnp.mean(center * center, axis=-1, keepdims=True)
    inverse = lax.rsqrt(spread + norm_epsilon)
    unit = center * inverse
    return (unit * gain_row + shift_row, unit, inverse)


def norm_backward(grad, unit, inverse, gain_row):
    scaled = grad * gain_row
    level = jnp.mean(scaled, axis=-1, keepdims=True)
    along = jnp.mean(scaled * unit, axis=-1, keepdims=True)
    grad_values = inverse * (scaled - level - unit * along)
    return (grad_values, jnp.sum(grad * unit, axis=0), jnp.sum(grad, axis=0))


gelu_rate = 0.7978845608028654
gelu_cube = 0.044715


def gelu_forward(before):
    bend = jnp.tanh(gelu_rate * (before + gelu_cube * before * before * before))
    return 0.5 * before * (1.0 + bend)


def gelu_slope(before):
    bend = jnp.tanh(gelu_rate * (before + gelu_cube * before * before * before))
    inner = gelu_rate * (1.0 + 3.0 * gelu_cube * before * before)
    return 0.5 * (1.0 + bend) + 0.5 * before * (1.0 - bend * bend) * inner


def adam_update(weight, gradient, first_moment, second, decay_rate, rate):
    first_new = beta_one * first_moment + (1.0 - beta_one) * gradient
    second_new = beta_two * second + (1.0 - beta_two) * gradient * gradient
    direction = (
        first_new
        / (1.0 - beta_one**STEP)
        / (jnp.sqrt(second_new / (1.0 - beta_two**STEP)) + adam_epsilon)
    )
    return (weight - rate * (direction + decay_rate * weight), first_new, second_new)


def contract_last(left, right):
    return lax.dot_general(
        left, right, (((1,), (1,)), ((), ())), preferred_element_type=jnp.float32
    )


def contract_first(left, right):
    return lax.dot_general(
        left, right, (((0,), (0,)), ((), ())), preferred_element_type=jnp.float32
    )


def flip(block, bit):
    size = lax.axis_size("dp")
    return lax.ppermute(block, "dp", [(i, i ^ bit) for i in range(size)])


def add_low(*terms):
    return sum(term.astype(jnp.float32) for term in terms).astype(jnp.bfloat16)


piece_codes = (0, 2, 6, 4, 1, 3, 7, 5)


def gather_near(own):
    return own, flip(own, 2), flip(own, 4)


def far_blocks(along_x, along_y):
    half = along_x.shape[0] // 2
    return flip(along_x[:half], 4), flip(along_y[half:], 2)


def all_blocks(own, along_x, along_y, far_top, far_low):
    mine = [own, along_x, far_top, far_low, along_y]
    return mine + [flip(block, 1) for block in mine]


def assemble_kernel(place_ref, *refs):
    pieces, full_ref, arrivals = refs[:10], refs[10], refs[11]
    chunk = pieces[0].shape[0]
    copies = []
    for block, piece in enumerate(pieces):
        code = (0, 2, 6, 6, 4)[block % 5] + block // 5
        at = (place_ref[0] ^ code) * chunk
        if block % 5 == 3:
            at = at + chunk // 2
        at = pl.multiple_of(at, 16)
        copies.append(
            pltpu.make_async_copy(piece, full_ref.at[pl.ds(at, piece.shape[0])], arrivals.at[block])
        )
    for copy in copies:
        copy.start()
    for copy in copies:
        copy.wait()


def assemble(place, pieces):
    chunk, width = pieces[0].shape
    return pl.pallas_call(
        assemble_kernel,
        in_specs=[pl.BlockSpec(memory_space=pltpu.SMEM)] + [pl.BlockSpec(memory_space=pl.ANY)] * len(pieces),
        out_specs=pl.BlockSpec(memory_space=pltpu.VMEM),
        out_shape=jax.ShapeDtypeStruct((8 * chunk, width), pieces[0].dtype),
        compiler_params=pltpu.CompilerParams(vmem_limit_bytes=VMEM_BYTES),
        scratch_shapes=[pltpu.SemaphoreType.DMA((len(pieces),))],
        cost_estimate=pl.CostEstimate(flops=0, bytes_accessed=32 * chunk * width, transcendentals=0),
        name="assemble",
    )(place.reshape(1), *pieces)


def partner(index, step):
    size = lax.axis_size("mp")
    return index ^ step if size & (size - 1) == 0 else (index + step) % size


def pass_mp(block, step):
    return lax.ppermute(block, "mp", [(i, partner(i, step)) for i in range(lax.axis_size("mp"))])


def gather_mp(rows):
    return [rows] + [pass_mp(rows, step) for step in range(1, lax.axis_size("mp"))]


def sum_mp(blocks):
    total = blocks[0].astype(jnp.float32)
    for step in range(1, lax.axis_size("mp")):
        total = total + pass_mp(blocks[step], step).astype(jnp.float32)
    return total


def send_first(top, low):
    size = top.shape[0] // 4
    from_x = flip(top[size : 3 * size], 2)
    from_y = flip(low[2 * size :], 4)
    late_y = add_low(top[3 * size :], from_x[size:])
    late_x = add_low(low[size : 2 * size], from_y[:size])
    return together(top[:size], low[:size], from_x[:size], from_y[size:], late_y, late_x)


def send_last(top, low, from_x, from_y, late_y, late_x):
    late_y, late_x = flip(late_y, 4), flip(late_x, 2)
    return add_low(top, from_x, late_y), add_low(low, from_y, late_x)


def together(*values):
    return lax.optimization_barrier(values)


PAIR = 2 * (MODEL_WIDTH // HEADS)
PAIRS = HEADS // 2
BLOCK = 2 * L
VMEM_BYTES = 56 * 1024 * 1024


def dot_nt(left, right):
    return lax.dot_general(
        left, right, (((1,), (1,)), ((), ())), preferred_element_type=jnp.float32
    )


def dot_tn(left, right):
    return lax.dot_general(
        left, right, (((0,), (0,)), ((), ())), preferred_element_type=jnp.float32
    )


def dot_nn(left, right):
    return jnp.dot(left, right, preferred_element_type=jnp.float32)


def both_heads(pair, left_half):
    zero = jnp.zeros_like(pair)
    return jnp.concatenate([jnp.where(left_half, pair, zero), jnp.where(left_half, zero, pair)], axis=0)


def pair_attend(queries, keys, key_bias):
    scores = dot_nt(queries, keys) * (MODEL_WIDTH // HEADS) ** (-0.5) + key_bias
    raised = jnp.exp(scores - jnp.max(scores, axis=-1, keepdims=True))
    return raised * (1.0 / jnp.sum(raised, axis=-1, keepdims=True))


def attention_kernel(
    start, length_ref, level_ref, embed_ref, qkv_ref, out_ref, gains_ref, project_ref, mixture_ref, first_ref, normed_ref
):
    step = pl.program_id(0) + start
    normed, _, _ = norm_forward(embed_ref[...].astype(jnp.float32), gains_ref[0:1], gains_ref[1:2])
    normed_low = normed.astype(jnp.bfloat16)
    normed_ref[...] = normed_low
    for part in range(3):
        columns = slice(part * MODEL_WIDTH, (part + 1) * MODEL_WIDTH)
        project_ref[:, columns] = dot_nt(normed_low, qkv_ref[columns]).astype(jnp.bfloat16)
    lane = lax.broadcasted_iota(jnp.int32, (L, PAIR), 1)
    left_half = lane < PAIR // 2
    for seq in range(BLOCK // L):
        rows = slice(seq * L, (seq + 1) * L)
        length = length_ref[step * (BLOCK // L) + seq]
        heads = level_ref[step * (BLOCK // L) + seq] * (HEADS // LEVELS)
        key_bias = jnp.where(lax.broadcasted_iota(jnp.int32, (1, L), 1) < length, 0.0, -1000000000.0)
        for pair in range(PAIRS):
            at = pair * PAIR
            queries = both_heads(project_ref[rows, at : at + PAIR], left_half)
            keys = project_ref[rows, MODEL_WIDTH + at : MODEL_WIDTH + at + PAIR]
            values = project_ref[rows, 2 * MODEL_WIDTH + at : 2 * MODEL_WIDTH + at + PAIR]
            attend = pair_attend(queries, keys, key_bias).astype(jnp.bfloat16)
            mixed = dot_nn(attend, values)
            mixed = jnp.where(left_half, mixed[:L], mixed[L:])
            head = 2 * pair + (lane >= PAIR // 2).astype(jnp.int32)
            mixture_ref[rows, at : at + PAIR] = jnp.where(head < heads, mixed, 0.0).astype(jnp.bfloat16)
    first_ref[...] = normed + dot_nn(mixture_ref[...], out_ref[...])


def whole(shape):
    return pl.BlockSpec(shape, lambda step: (0,) * len(shape))


def by_rows(width):
    return pl.BlockSpec((BLOCK, width), lambda step: (step, 0))


def attention_layer(start, steps, scalars, embedded, dense_full, norm_gains, before):
    rows = embedded.shape[0]
    low = jnp.bfloat16
    count = len(before)

    def at_rows(width):
        return pl.BlockSpec((BLOCK, width), lambda step: (step + start, 0))

    def body(length_ref, level_ref, *refs):
        attention_kernel(start, length_ref, level_ref, *refs[:4], *refs[4 + count :])

    return pl.pallas_call(
        body,
        grid=(steps,),
        in_specs=[
            pl.BlockSpec(memory_space=pltpu.SMEM),
            pl.BlockSpec(memory_space=pltpu.SMEM),
            at_rows(MODEL_WIDTH),
            whole((3 * MODEL_WIDTH, MODEL_WIDTH)),
            pl.BlockSpec((MODEL_WIDTH, MODEL_WIDTH), lambda step: (3, 0)),
            whole((6, MODEL_WIDTH)),
        ]
        + [pl.BlockSpec(memory_space=pl.ANY)] * count,
        out_specs=[at_rows(3 * MODEL_WIDTH), at_rows(MODEL_WIDTH), at_rows(MODEL_WIDTH), at_rows(MODEL_WIDTH)],
        out_shape=[
            jax.ShapeDtypeStruct((rows, 3 * MODEL_WIDTH), low),
            jax.ShapeDtypeStruct((rows, MODEL_WIDTH), low),
            jax.ShapeDtypeStruct((rows, MODEL_WIDTH), jnp.float32),
            jax.ShapeDtypeStruct((rows, MODEL_WIDTH), low),
        ],
        input_output_aliases={6 + place: place for place in range(count)},
        compiler_params=pltpu.CompilerParams(vmem_limit_bytes=VMEM_BYTES),
        cost_estimate=pl.CostEstimate(
            flops=steps * BLOCK * MODEL_WIDTH * MODEL_WIDTH * 20,
            bytes_accessed=steps * BLOCK * MODEL_WIDTH * 16,
            transcendentals=0,
        ),
        name="attention_layer",
    )(*scalars, embedded, dense_full, dense_full, norm_gains, *before)


def give_kernel(depth, spots_ref, grad_ref, rider_ref, sums_ref):
    rows = sums_ref.shape[0]
    row = pl.program_id(0) * rows + lax.broadcasted_iota(jnp.int32, (rows, 1), 0)
    last = lax.broadcasted_iota(jnp.int32, (1, rider_ref.shape[0]), 1) * depth + depth - 1
    own = (row == spots_ref[...]).astype(jnp.float32).astype(jnp.bfloat16)
    ride = (row == last).astype(jnp.float32).astype(jnp.bfloat16)
    sums_ref[...] = (dot_nn(own, grad_ref[...]) + dot_nn(ride, rider_ref[...])).astype(jnp.bfloat16)


def give_rows(spots, grads, rider, depth):
    total = rider.shape[0] * depth
    size = 512 if total % 512 == 0 else total
    return pl.pallas_call(
        lambda *refs: give_kernel(depth, *refs),
        grid=(total // size,),
        in_specs=[whole((1, spots.shape[0])), whole(grads.shape), whole(rider.shape)],
        out_specs=pl.BlockSpec((size, MODEL_WIDTH), lambda step: (step, 0)),
        out_shape=jax.ShapeDtypeStruct((total, MODEL_WIDTH), jnp.bfloat16),
        compiler_params=pltpu.CompilerParams(vmem_limit_bytes=VMEM_BYTES),
        cost_estimate=pl.CostEstimate(
            flops=2 * total * spots.shape[0] * MODEL_WIDTH, bytes_accessed=4 * total * MODEL_WIDTH, transcendentals=0
        ),
        name="give_rows",
    )(spots[None, :], grads, rider)


def collect_kernel(ids_ref, returned_ref, sums_ref, squares_ref):
    step = pl.program_id(0)
    rows = sums_ref.shape[0]
    row = step * rows + lax.broadcasted_iota(jnp.int32, (rows, 1), 0)
    hot = (row == ids_ref[...]).astype(jnp.float32).astype(jnp.bfloat16)
    sums = dot_nn(hot, returned_ref[...])
    sums_ref[...] = sums

    @pl.when(step == 0)
    def _():
        squares_ref[...] = jnp.zeros_like(squares_ref)

    squares_ref[0:1] += jnp.sum(sums * sums, axis=0, keepdims=True)


def collect_rows(ids, returned, table_rows):
    size = 240
    return pl.pallas_call(
        collect_kernel,
        grid=(-(-table_rows // size),),
        in_specs=[whole((1, ids.shape[0])), whole(returned.shape)],
        out_specs=[pl.BlockSpec((size, MODEL_WIDTH), lambda step: (step, 0)), whole((8, MODEL_WIDTH))],
        out_shape=[
            jax.ShapeDtypeStruct((table_rows, MODEL_WIDTH), jnp.float32),
            jax.ShapeDtypeStruct((8, MODEL_WIDTH), jnp.float32),
        ],
        compiler_params=pltpu.CompilerParams(vmem_limit_bytes=VMEM_BYTES),
        cost_estimate=pl.CostEstimate(
            flops=2 * table_rows * ids.shape[0] * MODEL_WIDTH, bytes_accessed=8 * table_rows * MODEL_WIDTH, transcendentals=0
        ),
        name="collect_rows",
    )(ids[None, :], returned)


def attention_back_kernel(
    start,
    length_ref,
    level_ref,
    grad_ref,
    first_ref,
    project_ref,
    embed_ref,
    teacher_ref,
    qkv_ref,
    out_ref,
    gains_ref,
    grad_project_ref,
    grad_att_ref,
    grad_embed_ref,
    sums_ref,
    grad_mixture_ref,
):
    turn = pl.program_id(0)
    step = turn + start
    low = jnp.bfloat16
    _, unit_one, inverse_one = norm_forward(first_ref[...], gains_ref[2:3], gains_ref[3:4])
    grad_first, gain_one, shift_one = norm_backward(grad_ref[...], unit_one, inverse_one, gains_ref[2:3])
    grad_att = grad_first.astype(low)
    grad_att_ref[...] = grad_att
    grad_mixture_ref[...] = dot_nt(grad_att, out_ref[...]).astype(low)
    lane = lax.broadcasted_iota(jnp.int32, (L, PAIR), 1)
    left_half = lane < PAIR // 2
    scaling = (MODEL_WIDTH // HEADS) ** (-0.5)
    usable = []
    for seq in range(BLOCK // L):
        rows = slice(seq * L, (seq + 1) * L)
        length = length_ref[step * (BLOCK // L) + seq]
        heads = level_ref[step * (BLOCK // L) + seq] * (HEADS // LEVELS)
        usable.append((lax.broadcasted_iota(jnp.int32, (L, 1), 0) < length).astype(jnp.float32))
        key_bias = jnp.where(lax.broadcasted_iota(jnp.int32, (L, 1), 0) < length, 0.0, -1000000000.0)
        for pair in range(PAIRS):
            at = pair * PAIR
            queries = both_heads(project_ref[rows, at : at + PAIR], left_half)
            keys = project_ref[rows, MODEL_WIDTH + at : MODEL_WIDTH + at + PAIR]
            values = project_ref[rows, 2 * MODEL_WIDTH + at : 2 * MODEL_WIDTH + at + PAIR]
            scores = dot_nt(keys, queries) * scaling + key_bias
            raised = jnp.exp(scores - jnp.max(scores, axis=0, keepdims=True))
            attend = raised * (1.0 / jnp.sum(raised, axis=0, keepdims=True))
            head = 2 * pair + (lane >= PAIR // 2).astype(jnp.int32)
            mixture = grad_mixture_ref[rows, at : at + PAIR]
            mixture = both_heads(jnp.where(head < heads, mixture, jnp.zeros_like(mixture)), left_half)
            grad_values = dot_nn(attend.astype(low), mixture)
            grad_attend = dot_nt(values, mixture)
            level = jnp.sum(grad_attend * attend, axis=0, keepdims=True)
            grad_scores = (attend * (grad_attend - level)).astype(low)
            grad_keys = dot_nn(grad_scores, queries) * scaling
            grad_queries = dot_tn(grad_scores, keys) * scaling
            grad_queries = jnp.where(left_half, grad_queries[:L], grad_queries[L:])
            grad_project_ref[rows, at : at + PAIR] = grad_queries.astype(low)
            grad_project_ref[rows, MODEL_WIDTH + at : MODEL_WIDTH + at + PAIR] = grad_keys.astype(low)
            grad_project_ref[rows, 2 * MODEL_WIDTH + at : 2 * MODEL_WIDTH + at + PAIR] = grad_values.astype(low)
    normed, unit_base, inverse_base = norm_forward(
        embed_ref[...].astype(jnp.float32), gains_ref[0:1], gains_ref[1:2]
    )
    usable = jnp.concatenate(usable, axis=0)
    gap = usable * (normed - teacher_ref[...].astype(jnp.float32))
    grad_normed = grad_first + 2.0 * gap + dot_nn(grad_project_ref[...], qkv_ref[...])
    grad_embed, gain_base, shift_base = norm_backward(grad_normed, unit_base, inverse_base, gains_ref[0:1])
    grad_embed_ref[...] = grad_embed.astype(low)

    @pl.when(turn == 0)
    def _():
        sums_ref[...] = jnp.zeros_like(sums_ref)

    for row, value in enumerate((gain_base, shift_base, gain_one, shift_one, jnp.sum(gap * gap, axis=0))):
        sums_ref[row : row + 1] += value[None]


def attention_backward(start, steps, scalars, arrays, weights, before):
    rows = arrays[0].shape[0]
    low = jnp.bfloat16

    def at_rows(width):
        return pl.BlockSpec((BLOCK, width), lambda step: (step + start, 0))

    widths = (MODEL_WIDTH, MODEL_WIDTH, 3 * MODEL_WIDTH, MODEL_WIDTH, MODEL_WIDTH)
    count = len(before)

    def body(length_ref, level_ref, *refs):
        attention_back_kernel(start, length_ref, level_ref, *refs[:8], *refs[8 + count :])

    return pl.pallas_call(
        body,
        grid=(steps,),
        in_specs=[pl.BlockSpec(memory_space=pltpu.SMEM)] * 2
        + [at_rows(width) for width in widths]
        + [
            whole((3 * MODEL_WIDTH, MODEL_WIDTH)),
            pl.BlockSpec((MODEL_WIDTH, MODEL_WIDTH), lambda step: (3, 0)),
            whole((6, MODEL_WIDTH)),
        ]
        + [pl.BlockSpec(memory_space=pl.ANY)] * count,
        out_specs=[at_rows(3 * MODEL_WIDTH), at_rows(MODEL_WIDTH), at_rows(MODEL_WIDTH), whole((8, MODEL_WIDTH))],
        out_shape=[
            jax.ShapeDtypeStruct((rows, 3 * MODEL_WIDTH), low),
            jax.ShapeDtypeStruct((rows, MODEL_WIDTH), low),
            jax.ShapeDtypeStruct((rows, MODEL_WIDTH), low),
            jax.ShapeDtypeStruct((8, MODEL_WIDTH), jnp.float32),
        ],
        input_output_aliases={10 + place: place for place in range(count)},
        scratch_shapes=[pltpu.VMEM((BLOCK, MODEL_WIDTH), low)],
        compiler_params=pltpu.CompilerParams(vmem_limit_bytes=VMEM_BYTES),
        cost_estimate=pl.CostEstimate(
            flops=steps * BLOCK * MODEL_WIDTH * MODEL_WIDTH * 40,
            bytes_accessed=steps * BLOCK * MODEL_WIDTH * 24,
            transcendentals=0,
        ),
        name="attention_backward",
    )(*scalars, *arrays, *weights, *before)


FFN_CHUNK = 768


def split_low(value):
    upper = value.astype(jnp.bfloat16)
    return jnp.concatenate([upper, (value - upper.astype(jnp.float32)).astype(jnp.bfloat16)], axis=0)


def ffn_kernel(sizes, length_ref, level_ref, first_ref, teacher_ref, pool_ref, class_ref, logits_ref, gains_ref, index_ref, *refs):
    pieces = refs[: len(sizes)]
    (hidden_ref, grad_before_ref, grad_feed_ref, middle_ref, grad_middle_ref, grad_pool_ref, grad_class_ref, sums_ref) = refs[
        len(sizes) : len(sizes) + 8
    ]
    weights_ref, slope_ref, unit_ref, inverse_ref, pooled_rows_ref, grad_rows_ref, arrivals = refs[len(sizes) + 8 :]
    step = pl.program_id(0)
    blocks = slope_ref.shape[0]
    seqs = BLOCK // L
    low = jnp.bfloat16
    row = lax.broadcasted_iota(jnp.int32, (BLOCK, 1), 0)

    def copies():
        at = 0
        for place, size in enumerate(sizes):
            yield pltpu.make_async_copy(pieces[place], weights_ref.at[pl.ds(at, size)], arrivals.at[place])
            at += size

    @pl.when(step == 0)
    def _():
        for copy in copies():
            copy.start()
        for copy in copies():
            copy.wait()
        sums_ref[...] = jnp.zeros_like(sums_ref)

    @pl.when(step < blocks)
    def _():
        middle, _, _ = norm_forward(first_ref[...], gains_ref[2:3], gains_ref[3:4])
        middle_low = middle.astype(low)
        middle_ref[...] = middle_low
        limit = jnp.full((BLOCK, 1), level_ref[step * seqs])
        for seq in range(1, seqs):
            limit = jnp.where(row >= seq * L, level_ref[step * seqs + seq], limit)
        limit = limit * (FF // LEVELS)
        for at in range(0, FF, FFN_CHUNK):
            columns = slice(at, at + FFN_CHUNK)
            before = dot_nt(middle_low, weights_ref[columns, :MODEL_WIDTH])
            square = before * before
            bend = jnp.tanh(before * (gelu_rate + gelu_rate * gelu_cube * square))
            rise = 0.5 + 0.5 * bend
            value = before * rise
            slope = rise + (0.5 * before) * (1.0 - bend * bend) * (gelu_rate + 3.0 * gelu_rate * gelu_cube * square)
            on = index_ref[:, columns] < limit
            hidden_ref[:, columns] = jnp.where(on, value, 0.0).astype(low)
            slope_ref[step, :, columns] = jnp.where(on, slope, 0.0).astype(low)
        feed = dot_nn(hidden_ref[...], weights_ref[:, MODEL_WIDTH:])
        output, unit, inverse = norm_forward(middle + feed, gains_ref[4:5], gains_ref[5:6])
        unit_ref[step] = unit
        inverse_ref[step] = inverse
        for seq in range(seqs):
            pooled_rows_ref[pl.ds(step * seqs + seq, 1), :] = output[seq * L : seq * L + 1]

    @pl.when(step == blocks)
    def _():
        first_low = pooled_rows_ref[...].astype(low)
        pooled = jnp.tanh(dot_nn(first_low, pool_ref[...]))
        pooled_low = pooled.astype(low)
        gap = dot_nn(pooled_low, class_ref[...]) - logits_ref[...]
        grad_logits = split_low(2.0 * L * gap)
        rows = gap.shape[0]
        grad_class = dot_tn(grad_logits, jnp.concatenate([pooled_low, pooled_low], axis=0))
        grad_class_ref[...] = grad_class[: grad_class_ref.shape[0]]
        grad_pooled = dot_nt(grad_logits, class_ref[...])
        grad_inner = split_low((grad_pooled[:rows] + grad_pooled[rows:]) * (1.0 - pooled * pooled))
        grad_pool_ref[...] = dot_tn(jnp.concatenate([first_low, first_low], axis=0), grad_inner).astype(low)
        grad_rows = dot_nt(grad_inner, pool_ref[...])
        grad_rows_ref[...] = grad_rows[:rows] + grad_rows[rows:]
        sums_ref[3:4, : gap.shape[1]] += L * jnp.sum(gap * gap, axis=0, keepdims=True)

    @pl.when(step > blocks)
    def _():
        block = step - blocks - 1
        unit = unit_ref[block]
        reach = jnp.full((BLOCK, 1), length_ref[block * seqs])
        pooled_grad = jnp.where(row == 0, grad_rows_ref[pl.ds(block * seqs, 1), :], 0.0)
        for seq in range(1, seqs):
            reach = jnp.where(row >= seq * L, length_ref[block * seqs + seq] + seq * L, reach)
            pooled_grad = jnp.where(row == seq * L, grad_rows_ref[pl.ds(block * seqs + seq, 1), :], pooled_grad)
        output = unit * gains_ref[4:5] + gains_ref[5:6]
        gap = jnp.where(row < reach, output - teacher_ref[...].astype(jnp.float32), 0.0)
        grad_second, gain, shift = norm_backward(2.0 * gap + pooled_grad, unit, inverse_ref[block], gains_ref[4:5])
        grad_feed = grad_second.astype(low)
        grad_feed_ref[...] = grad_feed
        for at in range(0, FF, FFN_CHUNK):
            columns = slice(at, at + FFN_CHUNK)
            grad_hidden = dot_nt(grad_feed, weights_ref[columns, MODEL_WIDTH:])
            grad_before_ref[:, columns] = (grad_hidden * slope_ref[block, :, columns].astype(jnp.float32)).astype(low)
        grad_middle_ref[...] = grad_second + dot_nn(grad_before_ref[...], weights_ref[:, :MODEL_WIDTH])
        for place, value in enumerate((gain, shift, jnp.sum(gap * gap, axis=0))):
            sums_ref[place : place + 1] += value[None]


def ffn_layer(scalars, first, teacher, dense_full, class_wide, logits_wide, norm_gains, neuron_index, pieces):
    rows = first.shape[0]
    seqs = rows // L
    blocks = rows // BLOCK
    low = jnp.bfloat16
    sizes = tuple(piece.shape[0] for piece in pieces)

    def going(width):
        return pl.BlockSpec((BLOCK, width), lambda step: (jnp.minimum(step, blocks - 1), 0))

    def coming(width):
        return pl.BlockSpec((BLOCK, width), lambda step: (jnp.maximum(step - blocks - 1, 0), 0))

    return pl.pallas_call(
        lambda *refs: ffn_kernel(sizes, *refs),
        grid=(2 * blocks + 1,),
        in_specs=[
            pl.BlockSpec(memory_space=pltpu.SMEM),
            pl.BlockSpec(memory_space=pltpu.SMEM),
            going(MODEL_WIDTH),
            coming(MODEL_WIDTH),
            pl.BlockSpec((MODEL_WIDTH, MODEL_WIDTH), lambda step: (4, 0)),
            whole(class_wide.shape),
            whole(logits_wide.shape),
            whole((6, MODEL_WIDTH)),
            whole((1, FF)),
        ]
        + [pl.BlockSpec(memory_space=pl.ANY)] * len(sizes),
        out_specs=[
            going(FF),
            coming(FF),
            coming(MODEL_WIDTH),
            going(MODEL_WIDTH),
            coming(MODEL_WIDTH),
            whole((MODEL_WIDTH, MODEL_WIDTH)),
            whole((8, MODEL_WIDTH)),
            whole((8, MODEL_WIDTH)),
        ],
        out_shape=[
            jax.ShapeDtypeStruct((rows, FF), low),
            jax.ShapeDtypeStruct((rows, FF), low),
            jax.ShapeDtypeStruct((rows, MODEL_WIDTH), low),
            jax.ShapeDtypeStruct((rows, MODEL_WIDTH), low),
            jax.ShapeDtypeStruct((rows, MODEL_WIDTH), jnp.float32),
            jax.ShapeDtypeStruct((MODEL_WIDTH, MODEL_WIDTH), low),
            jax.ShapeDtypeStruct((8, MODEL_WIDTH), jnp.float32),
            jax.ShapeDtypeStruct((8, MODEL_WIDTH), jnp.float32),
        ],
        scratch_shapes=[
            pltpu.VMEM((FF, 2 * MODEL_WIDTH), low),
            pltpu.VMEM((blocks, BLOCK, FF), low),
            pltpu.VMEM((blocks, BLOCK, MODEL_WIDTH), jnp.float32),
            pltpu.VMEM((blocks, BLOCK, 1), jnp.float32),
            pltpu.VMEM((seqs, MODEL_WIDTH), jnp.float32),
            pltpu.VMEM((seqs, MODEL_WIDTH), jnp.float32),
            pltpu.SemaphoreType.DMA((len(sizes),)),
        ],
        compiler_params=pltpu.CompilerParams(vmem_limit_bytes=VMEM_BYTES),
        cost_estimate=pl.CostEstimate(
            flops=rows * MODEL_WIDTH * FF * 16, bytes_accessed=rows * FF * 8, transcendentals=rows * FF
        ),
        name="ffn_layer",
    )(*scalars, first, teacher, dense_full, class_wide, logits_wide, norm_gains, neuron_index, *pieces)


def per_device(
    token_ids,
    replacements,
    replaced,
    lengths,
    widths,
    teacher_embed,
    teacher_hidden,
    teacher_logits,
    embed_table,
    embed_moment,
    embed_square,
    dense_weights,
    dense_moment,
    dense_square,
    feedforward,
    feedforward_moment,
    feedforward_square,
    classifier,
    classifier_moment,
    classifier_square,
    norm_gains,
    norm_moment,
    norm_square,
):
    both = ("dp", "mp")
    mp_count = lax.axis_size("mp")
    mp_index = lax.axis_index("mp")
    n_dev = lax.axis_size("dp") * mp_count
    own_seqs = teacher_logits.shape[0]
    own_rows = own_seqs * L
    table_rows = embed_table.shape[0]
    low = jnp.bfloat16
    by_bits = lax.axis_size("dp") == 8 and mp_count & (mp_count - 1) == 0
    if by_bits:
        dense_steps = gather_mp(dense_weights.astype(low))
        dense_column = jnp.concatenate(
            [lax.select_n(mp_index, *[dense_steps[k ^ z] for z in range(mp_count)]) for k in range(mp_count)],
            axis=0,
        )
    else:
        dense_column = lax.all_gather(dense_weights.astype(low), "mp", axis=0, tiled=True)
    dp_index = lax.axis_index("dp")
    neuron_piece = feedforward.shape[0]
    neuron_slot = jnp.arange(FF)
    if by_bits:
        chunk = neuron_piece * mp_count
        codes = jnp.repeat(jnp.array(piece_codes), chunk, total_repeat_length=FF)
        steps = neuron_slot % chunk // neuron_piece
        neuron_index = (dp_index ^ codes) * chunk + (mp_index ^ steps) * neuron_piece + neuron_slot % neuron_piece
    else:
        neuron_index = neuron_slot

    depth = -(-(own_rows * 3 // 2) // (n_dev * 16)) * 16
    capacity = depth - 1
    own_start = mp_index * own_seqs
    own_ids = lax.dynamic_slice_in_dim(
        jnp.where(replaced == 1, replacements, token_ids), own_start, own_seqs
    ).reshape(own_rows)
    owner = own_ids // table_rows
    local = own_ids - owner * table_rows
    place = jnp.arange(own_rows)
    first = jnp.min(
        jnp.where(own_ids[:, None] == own_ids[None, :], place[None, :], own_rows), axis=1
    )
    leads = first == place
    slot = jnp.sum(
        (leads[None, :] & (owner[:, None] == owner[None, :]) & (place[None, :] < first[:, None])).astype(
            jnp.int32
        ),
        axis=1,
    )
    deepest = jnp.max(slot)

    def positions(turn):
        rank = slot - turn * capacity
        return jnp.where((rank >= 0) & (rank < capacity), owner * depth + rank, -1)

    def wanted(turn):
        spot = jnp.where(leads, positions(turn), -1)
        hits = spot[:, None] == jnp.arange(n_dev * depth)[None, :]
        rows = jnp.max(jnp.where(hits, local[:, None], -1), axis=0).reshape(n_dev, depth)
        return jnp.where(jnp.arange(depth)[None, :] == capacity, deepest, rows)

    def exchange(blocks):
        return lax.all_to_all(blocks, both, split_axis=0, concat_axis=0)

    def asked_hot(asked):
        flat = jnp.where(jnp.arange(depth)[None, :] < capacity, asked, -1).reshape(-1)
        return (flat[:, None] == jnp.arange(table_rows)[None, :]).astype(low)

    def own_hot(turn):
        return (positions(turn)[:, None] == jnp.arange(n_dev * depth)[None, :]).astype(low)

    def answer(asked, table):
        rows = jnp.dot(asked_hot(asked), table.astype(low), preferred_element_type=low)
        return rows.reshape(n_dev, depth, MODEL_WIDTH)

    def place_rows(turn, rows):
        return jnp.dot(own_hot(turn), rows.reshape(-1, MODEL_WIDTH), preferred_element_type=low)

    asked_first = exchange(wanted(0))
    ffn_low = feedforward.astype(low)
    if by_bits:
        dense_column, ffn_low = together(dense_column, ffn_low)
        dense_near = gather_near(dense_column)
        ffn_column = jnp.concatenate(gather_mp(ffn_low), axis=0)
        rows_first, ffn_column, *dense_near = together(answer(asked_first, embed_table), ffn_column, *dense_near)
    else:
        rows_first = answer(asked_first, embed_table)
    turns = jnp.max(asked_first[:, capacity]) // capacity + 1
    extra_rows = lax.while_loop(
        lambda state: state[0] < turns,
        lambda state: (
            state[0] + 1,
            state[1] + place_rows(state[0], exchange(answer(exchange(wanted(state[0])), embed_table))),
        ),
        (jnp.int32(1), jnp.zeros((own_rows, MODEL_WIDTH), low)),
    )[1]
    rows_first, extra_rows = together(rows_first, extra_rows)
    rows_first = exchange(rows_first)
    if by_bits:
        dense_full = assemble(dp_index, all_blocks(*dense_near, *far_blocks(*dense_near[1:])))
        half = ffn_column.shape[0] // 2
        top, rest = ffn_column[:half], ffn_column[half:]
        x_top, y_rest = flip(top, 2), flip(rest, 4)
        x_rest, y_top = flip(rest, 2), flip(top, 4)
        rows_first, dense_full = together(rows_first, dense_full)
    else:
        dense_full = lax.all_gather(dense_column, "dp", axis=0, tiled=True)
        ffn_column = lax.all_gather(ffn_low, "mp", axis=0, tiled=True)
        ffn_pieces = [lax.all_gather(ffn_column, "dp", axis=0, tiled=True)]
    embedded_low = place_rows(0, rows_first) + extra_rows

    own_lengths = lax.dynamic_slice_in_dim(lengths, own_start, own_seqs)
    own_levels = lax.dynamic_slice_in_dim(widths, own_start, own_seqs)
    scalars = (own_lengths, own_levels)
    blocks = own_rows // BLOCK
    if by_bits:
        layer = attention_layer(0, blocks // 2, scalars, embedded_low, dense_full, norm_gains, ())
        *layer, x_top, y_rest = together(*layer, x_top, y_rest)
        far = flip(x_top, 4), flip(y_rest, 2)
        layer = attention_layer(
            blocks // 2, blocks - blocks // 2, scalars, embedded_low, dense_full, norm_gains, layer
        )
        near = [top, rest, x_top, x_rest, y_top, y_rest]
        near = near + [flip(block, 1) for block in near]
        flow = together(*layer, *near, *far)
        layer, near, far = flow[:4], flow[4:16], flow[16:]
        far = [*far, flip(far[0], 1), flip(far[1], 1)]
        ffn_pieces = [*near[:4], *far[:2], *near[4:10], *far[2:], *near[10:]]
    else:
        layer = attention_layer(0, blocks, scalars, embedded_low, dense_full, norm_gains, ())
    project, head_mixture, first_sum, normed_low = layer
    class_pad = -classifier.shape[1] % 128
    hidden_low, grad_before, grad_feed_low, middle_low, grad_middle, grad_pool_rows, grad_class, ffn_sums = ffn_layer(
        scalars,
        first_sum,
        teacher_hidden.reshape(own_rows, MODEL_WIDTH),
        dense_full,
        jnp.pad(classifier, ((0, 0), (0, class_pad))).astype(low),
        jnp.pad(teacher_logits, ((0, 0), (0, class_pad))),
        norm_gains,
        neuron_index[None, :],
        ffn_pieces,
    )
    grad_class = grad_class[: classifier.shape[1]]

    def over_both(rows):
        rows = lax.psum_scatter(rows, "dp", scatter_dimension=0, tiled=True)
        return lax.psum_scatter(rows, "mp", scatter_dimension=0, tiled=True).astype(jnp.float32)

    def weight_sums(left, right):
        half = left.shape[1] // 2
        given = flip(contract_first(left[:, half:], right).astype(low), 1)
        return contract_first(left[:, :half], right).astype(low), given

    def dense_scatter(rows):
        if not by_bits:
            return over_both(rows)
        chunks = rows.reshape(4, 2, rows.shape[0] // 8, rows.shape[1])
        core = dp_index % 2
        place = dp_index // 2
        parts = add_low(
            lax.dynamic_index_in_dim(chunks, core, 1, keepdims=False),
            flip(lax.dynamic_index_in_dim(chunks, 1 - core, 1, keepdims=False), 1),
        )
        half = parts.shape[1] // 2
        parts = [lax.dynamic_index_in_dim(parts, place ^ code, 0, keepdims=False) for code in (0, 1, 3, 2)]
        top = jnp.concatenate([part[:half] for part in parts], axis=0)
        rest = jnp.concatenate([part[half:] for part in parts], axis=0)
        parts = send_last(*send_first(top, rest))
        parts = jnp.concatenate(parts, axis=0).reshape(mp_count, -1, rows.shape[1])
        return sum_mp([lax.dynamic_index_in_dim(parts, mp_index ^ step, 0, keepdims=False) for step in range(mp_count)])

    arrays = [
        grad_middle,
        first_sum,
        project,
        embedded_low,
        teacher_embed.reshape(own_rows, MODEL_WIDTH),
    ]
    weights = (dense_full, dense_full, norm_gains)
    if by_bits:
        down_own, down_given = weight_sums(hidden_low, grad_feed_low)
        up_own, up_given = weight_sums(grad_before, middle_low)
        parts = (add_low(up_own, up_given), add_low(down_own, down_given))
        arrays[0], *parts = together(arrays[0], *parts)
        parts = send_first(*parts)
        before = attention_backward(0, blocks - 1, scalars, arrays, weights, ())
        arrays[0], *flow = together(arrays[0], *before, *parts)
        *before, sums_one = flow[:4]
        parts = send_last(*flow[4:])
        before = attention_backward(blocks - 1, 1, scalars, arrays, weights, before)
        flow = together(*before, *parts)
        *before, sums_last = flow[:4]
        parts = [part.reshape(mp_count, neuron_piece, MODEL_WIDTH) for part in flow[4:]]
        ffn_grad = sum_mp([jnp.concatenate([part[step] for part in parts], axis=1) for step in range(mp_count)])
        sums = sums_one + sums_last
    else:
        ffn_grad = jnp.concatenate(
            [contract_first(grad_before, middle_low), contract_first(hidden_low, grad_feed_low)], axis=1
        ).astype(low)
        ffn_grad = over_both(ffn_grad)
        *before, sums = attention_backward(0, blocks, scalars, arrays, weights, ())
    grad_project, grad_att_low, grad_embed_low = before
    grad_dense = jnp.concatenate(
        [
            contract_first(grad_project, normed_low).astype(low),
            contract_first(head_mixture, grad_att_low).astype(low),
            grad_pool_rows,
        ],
        axis=0,
    )
    loss_own = jnp.sum(sums[4]) + jnp.sum(ffn_sums[2:4])

    small = jnp.concatenate([sums[:4], ffn_sums[:2], grad_class], axis=0)
    small_rows = small.shape[0]
    upper = lax.reduce_precision(small, 8, 7)
    rider = jnp.concatenate([upper, small - upper], axis=0).astype(low)
    rider = jnp.pad(rider, ((0, n_dev - 2 * small_rows), (0, 0)))

    def give_back(turn, rider):
        return give_rows(positions(turn), grad_embed_low, rider, depth).reshape(n_dev, depth, MODEL_WIDTH)

    def collect(asked, returned):
        ids = jnp.where(jnp.arange(depth)[None, :] < capacity, asked, -1).reshape(-1)
        return collect_rows(ids, returned.reshape(-1, MODEL_WIDTH), table_rows)

    def collect_more(state):
        turn, total, _ = state
        total = total + collect(exchange(wanted(turn)), exchange(give_back(turn, jnp.zeros_like(rider))))[0]
        return turn + 1, total, jnp.zeros((8, MODEL_WIDTH)).at[0].set(jnp.sum(total * total, axis=0))

    given = give_back(0, rider)
    given, grad_dense, ffn_grad = together(given, grad_dense, ffn_grad)
    returned = exchange(given)
    dense_grad = dense_scatter(grad_dense)
    _, table_grad, table_squares = lax.while_loop(
        lambda state: state[0] < turns, collect_more, (jnp.int32(1), *collect(asked_first, returned))
    )
    small_row = jnp.sum(returned[:, capacity].astype(jnp.float32), axis=0)
    square_sum = jnp.sum(table_squares) + jnp.sum(dense_grad * dense_grad) + jnp.sum(ffn_grad * ffn_grad)
    own_count = jnp.sum(own_lengths).astype(jnp.float32)
    message = jnp.concatenate([small_row, jnp.stack([square_sum, own_count, loss_own])])
    message = jnp.pad(message, (0, -message.shape[0] % 128))
    told = exchange(jnp.broadcast_to(message[None], (n_dev, message.shape[0])))
    scalars = jnp.sum(told[:, MODEL_WIDTH : MODEL_WIDTH + 128], axis=0)
    token_count, loss_sum = scalars[1], scalars[2]
    small = told[:small_rows, :MODEL_WIDTH] + told[small_rows : 2 * small_rows, :MODEL_WIDTH]
    total_square = scalars[0] + jnp.sum(small * small)
    gains_grad, class_grad = small[:6], small[6:].T
    inverse = 1.0 / token_count
    grad_norm = jnp.sqrt(total_square) * inverse
    scaling = inverse * (clip_bound / jnp.maximum(grad_norm, clip_bound))
    table_new = adam_update(
        embed_table, table_grad * scaling, embed_moment, embed_square, weight_decay, learn_rate
    )
    dense_new = adam_update(
        dense_weights, dense_grad * scaling, dense_moment, dense_square, weight_decay, learn_rate
    )
    ffn_new = adam_update(
        feedforward,
        ffn_grad * scaling,
        feedforward_moment,
        feedforward_square,
        weight_decay,
        learn_rate,
    )
    class_new = adam_update(
        classifier,
        class_grad * scaling,
        classifier_moment,
        classifier_square,
        weight_decay,
        learn_rate,
    )
    gains_new = adam_update(
        norm_gains, gains_grad * scaling, norm_moment, norm_square, 0.0, gain_rate
    )
    return (
        loss_sum,
        token_count,
        grad_norm,
        table_new[0],
        table_new[1],
        table_new[2],
        table_new[0].astype(jnp.bfloat16),
        dense_new[0],
        dense_new[1],
        dense_new[2],
        dense_new[0].astype(jnp.bfloat16),
        ffn_new[0],
        ffn_new[1],
        ffn_new[2],
        ffn_new[0].astype(jnp.bfloat16),
        class_new[0],
        class_new[1],
        class_new[2],
        class_new[0].astype(jnp.bfloat16),
        gains_new[0],
        gains_new[1],
        gains_new[2],
    )


def solution(mesh):
    placed = (
        P("dp", None),
        P("dp", None),
        P("dp", None),
        P("dp"),
        P("dp"),
        P(("dp", "mp"), None, None),
        P(("dp", "mp"), None, None),
        P(("dp", "mp"), None),
        P(("dp", "mp"), None),
        P(("dp", "mp"), None),
        P(("dp", "mp"), None),
        P(("dp", "mp"), None),
        P(("dp", "mp"), None),
        P(("dp", "mp"), None),
        P(("dp", "mp"), None),
        P(("dp", "mp"), None),
        P(("dp", "mp"), None),
        P(),
        P(),
        P(),
        P(),
        P(),
        P(),
    )
    return jax.shard_map(
        per_device,
        mesh=mesh,
        in_specs=placed,
        out_specs=(
            P(),
            P(),
            P(),
            P(("dp", "mp"), None),
            P(("dp", "mp"), None),
            P(("dp", "mp"), None),
            P(("dp", "mp"), None),
            P(("dp", "mp"), None),
            P(("dp", "mp"), None),
            P(("dp", "mp"), None),
            P(("dp", "mp"), None),
            P(("dp", "mp"), None),
            P(("dp", "mp"), None),
            P(("dp", "mp"), None),
            P(("dp", "mp"), None),
            P(),
            P(),
            P(),
            P(),
            P(),
            P(),
            P(),
        ),
        check_vma=False,
    )
```

```python
import jax
import jax.numpy as jnp
from jax import lax
from jax.experimental import pallas as pl
from jax.experimental.pallas import tpu as pltpu
from jax.sharding import PartitionSpec as P

MODEL_WIDTH = 768
HEADS = 12
FF = 3072
L = 128
LEVELS = 4
STEP = 10


highest_precision = lax.Precision.HIGHEST
norm_epsilon = 1e-05
learn_rate = 0.05
gain_rate = 0.5
beta_one = 0.9
beta_two = 0.999
adam_epsilon = 1e-08
weight_decay = 0.01
clip_bound = 1.0


def norm_forward(values, gain_row, shift_row):
    center = values - jnp.mean(values, axis=-1, keepdims=True)
    spread = jnp.mean(center * center, axis=-1, keepdims=True)
    inverse = lax.rsqrt(spread + norm_epsilon)
    unit = center * inverse
    return (unit * gain_row + shift_row, unit, inverse)


def norm_backward(grad, unit, inverse, gain_row):
    scaled = grad * gain_row
    level = jnp.mean(scaled, axis=-1, keepdims=True)
    along = jnp.mean(scaled * unit, axis=-1, keepdims=True)
    grad_values = inverse * (scaled - level - unit * along)
    return (grad_values, jnp.sum(grad * unit, axis=0), jnp.sum(grad, axis=0))


gelu_rate = 0.7978845608028654
gelu_cube = 0.044715


def gelu_forward(before):
    bend = jnp.tanh(gelu_rate * (before + gelu_cube * before * before * before))
    return 0.5 * before * (1.0 + bend)


def gelu_slope(before):
    bend = jnp.tanh(gelu_rate * (before + gelu_cube * before * before * before))
    inner = gelu_rate * (1.0 + 3.0 * gelu_cube * before * before)
    return 0.5 * (1.0 + bend) + 0.5 * before * (1.0 - bend * bend) * inner


def adam_update(weight, gradient, first_moment, second, decay_rate, rate):
    first_new = beta_one * first_moment + (1.0 - beta_one) * gradient
    second_new = beta_two * second + (1.0 - beta_two) * gradient * gradient
    direction = (
        first_new
        / (1.0 - beta_one**STEP)
        / (jnp.sqrt(second_new / (1.0 - beta_two**STEP)) + adam_epsilon)
    )
    return (weight - rate * (direction + decay_rate * weight), first_new, second_new)


def contract_last(left, right):
    return lax.dot_general(
        left, right, (((1,), (1,)), ((), ())), preferred_element_type=jnp.float32
    )


def contract_first(left, right):
    return lax.dot_general(
        left, right, (((0,), (0,)), ((), ())), preferred_element_type=jnp.float32
    )


def flip(block, bit):
    size = lax.axis_size("dp")
    return lax.ppermute(block, "dp", [(i, i ^ bit) for i in range(size)])


def add_low(*terms):
    return sum(term.astype(jnp.float32) for term in terms).astype(jnp.bfloat16)


piece_codes = (0, 2, 6, 4, 1, 3, 7, 5)


def gather_near(own):
    return own, flip(own, 2), flip(own, 4)


def far_blocks(along_x, along_y):
    half = along_x.shape[0] // 2
    return flip(along_x[:half], 4), flip(along_y[half:], 2)


def all_blocks(own, along_x, along_y, far_top, far_low):
    mine = [own, along_x, far_top, far_low, along_y]
    return mine + [flip(block, 1) for block in mine]


def assemble_kernel(place_ref, *refs):
    pieces, full_ref, arrivals = refs[:10], refs[10], refs[11]
    chunk = pieces[0].shape[0]
    copies = []
    for block, piece in enumerate(pieces):
        code = (0, 2, 6, 6, 4)[block % 5] + block // 5
        at = (place_ref[0] ^ code) * chunk
        if block % 5 == 3:
            at = at + chunk // 2
        at = pl.multiple_of(at, 16)
        copies.append(
            pltpu.make_async_copy(piece, full_ref.at[pl.ds(at, piece.shape[0])], arrivals.at[block])
        )
    for copy in copies:
        copy.start()
    for copy in copies:
        copy.wait()


def assemble(place, pieces):
    chunk, width = pieces[0].shape
    return pl.pallas_call(
        assemble_kernel,
        in_specs=[pl.BlockSpec(memory_space=pltpu.SMEM)] + [pl.BlockSpec(memory_space=pl.ANY)] * len(pieces),
        out_specs=pl.BlockSpec(memory_space=pltpu.VMEM),
        out_shape=jax.ShapeDtypeStruct((8 * chunk, width), pieces[0].dtype),
        compiler_params=pltpu.CompilerParams(vmem_limit_bytes=VMEM_BYTES),
        scratch_shapes=[pltpu.SemaphoreType.DMA((len(pieces),))],
        cost_estimate=pl.CostEstimate(flops=0, bytes_accessed=32 * chunk * width, transcendentals=0),
        name="assemble",
    )(place.reshape(1), *pieces)


def partner(index, step):
    size = lax.axis_size("mp")
    return index ^ step if size & (size - 1) == 0 else (index + step) % size


def pass_mp(block, step):
    return lax.ppermute(block, "mp", [(i, partner(i, step)) for i in range(lax.axis_size("mp"))])


def gather_mp(rows):
    return [rows] + [pass_mp(rows, step) for step in range(1, lax.axis_size("mp"))]


def send_first(top, low):
    size = top.shape[0] // 4
    from_x = flip(top[size : 3 * size], 2)
    from_y = flip(low[2 * size :], 4)
    late_y = add_low(top[3 * size :], from_x[size:])
    late_x = add_low(low[size : 2 * size], from_y[:size])
    return together(top[:size], low[:size], from_x[:size], from_y[size:], late_y, late_x)


def send_last(top, low, from_x, from_y, late_y, late_x):
    late_y, late_x = flip(late_y, 4), flip(late_x, 2)
    return add_low(top, from_x, late_y), add_low(low, from_y, late_x)


def together(*values):
    return lax.optimization_barrier(values)


PAIR = 2 * (MODEL_WIDTH // HEADS)
PAIRS = HEADS // 2
BLOCK = 2 * L
VMEM_BYTES = 56 * 1024 * 1024


def dot_nt(left, right):
    return lax.dot_general(
        left, right, (((1,), (1,)), ((), ())), preferred_element_type=jnp.float32
    )


def dot_tn(left, right):
    return lax.dot_general(
        left, right, (((0,), (0,)), ((), ())), preferred_element_type=jnp.float32
    )


def dot_nn(left, right):
    return jnp.dot(left, right, preferred_element_type=jnp.float32)


def both_heads(pair, left_half):
    zero = jnp.zeros_like(pair)
    return jnp.concatenate([jnp.where(left_half, pair, zero), jnp.where(left_half, zero, pair)], axis=0)


def pair_attend(queries, keys, key_bias):
    scores = dot_nt(queries, keys) * (MODEL_WIDTH // HEADS) ** (-0.5) + key_bias
    raised = jnp.exp(scores - jnp.max(scores, axis=-1, keepdims=True))
    return raised * (1.0 / jnp.sum(raised, axis=-1, keepdims=True))


def attention_kernel(
    start, length_ref, level_ref, embed_ref, qkv_ref, out_ref, gains_ref, project_ref, mixture_ref, first_ref, normed_ref
):
    step = pl.program_id(0) + start
    normed, _, _ = norm_forward(embed_ref[...].astype(jnp.float32), gains_ref[0:1], gains_ref[1:2])
    normed_low = normed.astype(jnp.bfloat16)
    normed_ref[...] = normed_low
    for part in range(3):
        columns = slice(part * MODEL_WIDTH, (part + 1) * MODEL_WIDTH)
        project_ref[:, columns] = dot_nt(normed_low, qkv_ref[columns]).astype(jnp.bfloat16)
    lane = lax.broadcasted_iota(jnp.int32, (L, PAIR), 1)
    left_half = lane < PAIR // 2
    for seq in range(BLOCK // L):
        rows = slice(seq * L, (seq + 1) * L)
        length = length_ref[step * (BLOCK // L) + seq]
        heads = level_ref[step * (BLOCK // L) + seq] * (HEADS // LEVELS)
        key_bias = jnp.where(lax.broadcasted_iota(jnp.int32, (1, L), 1) < length, 0.0, -1000000000.0)
        for pair in range(PAIRS):
            at = pair * PAIR
            queries = both_heads(project_ref[rows, at : at + PAIR], left_half)
            keys = project_ref[rows, MODEL_WIDTH + at : MODEL_WIDTH + at + PAIR]
            values = project_ref[rows, 2 * MODEL_WIDTH + at : 2 * MODEL_WIDTH + at + PAIR]
            attend = pair_attend(queries, keys, key_bias).astype(jnp.bfloat16)
            mixed = dot_nn(attend, values)
            mixed = jnp.where(left_half, mixed[:L], mixed[L:])
            head = 2 * pair + (lane >= PAIR // 2).astype(jnp.int32)
            mixture_ref[rows, at : at + PAIR] = jnp.where(head < heads, mixed, 0.0).astype(jnp.bfloat16)
    first_ref[...] = normed + dot_nn(mixture_ref[...], out_ref[...])


def whole(shape):
    return pl.BlockSpec(shape, lambda step: (0,) * len(shape))


def by_rows(width):
    return pl.BlockSpec((BLOCK, width), lambda step: (step, 0))


def attention_layer(start, steps, scalars, embedded, dense_full, norm_gains, before):
    rows = embedded.shape[0]
    low = jnp.bfloat16
    count = len(before)

    def at_rows(width):
        return pl.BlockSpec((BLOCK, width), lambda step: (step + start, 0))

    def body(length_ref, level_ref, *refs):
        attention_kernel(start, length_ref, level_ref, *refs[:4], *refs[4 + count :])

    return pl.pallas_call(
        body,
        grid=(steps,),
        in_specs=[
            pl.BlockSpec(memory_space=pltpu.SMEM),
            pl.BlockSpec(memory_space=pltpu.SMEM),
            at_rows(MODEL_WIDTH),
            whole((3 * MODEL_WIDTH, MODEL_WIDTH)),
            pl.BlockSpec((MODEL_WIDTH, MODEL_WIDTH), lambda step: (3, 0)),
            whole((6, MODEL_WIDTH)),
        ]
        + [pl.BlockSpec(memory_space=pl.ANY)] * count,
        out_specs=[at_rows(3 * MODEL_WIDTH), at_rows(MODEL_WIDTH), at_rows(MODEL_WIDTH), at_rows(MODEL_WIDTH)],
        out_shape=[
            jax.ShapeDtypeStruct((rows, 3 * MODEL_WIDTH), low),
            jax.ShapeDtypeStruct((rows, MODEL_WIDTH), low),
            jax.ShapeDtypeStruct((rows, MODEL_WIDTH), jnp.float32),
            jax.ShapeDtypeStruct((rows, MODEL_WIDTH), low),
        ],
        input_output_aliases={6 + place: place for place in range(count)},
        compiler_params=pltpu.CompilerParams(vmem_limit_bytes=VMEM_BYTES),
        cost_estimate=pl.CostEstimate(
            flops=steps * BLOCK * MODEL_WIDTH * MODEL_WIDTH * 20,
            bytes_accessed=steps * BLOCK * MODEL_WIDTH * 16,
            transcendentals=0,
        ),
        name="attention_layer",
    )(*scalars, embedded, dense_full, dense_full, norm_gains, *before)


def give_kernel(depth, spots_ref, grad_ref, rider_ref, sums_ref):
    rows = sums_ref.shape[0]
    row = pl.program_id(0) * rows + lax.broadcasted_iota(jnp.int32, (rows, 1), 0)
    last = lax.broadcasted_iota(jnp.int32, (1, rider_ref.shape[0]), 1) * depth + depth - 1
    own = (row == spots_ref[...]).astype(jnp.float32).astype(jnp.bfloat16)
    ride = (row == last).astype(jnp.float32).astype(jnp.bfloat16)
    sums_ref[...] = (dot_nn(own, grad_ref[...]) + dot_nn(ride, rider_ref[...])).astype(jnp.bfloat16)


def give_rows(spots, grads, rider, depth):
    total = rider.shape[0] * depth
    size = 512 if total % 512 == 0 else total
    return pl.pallas_call(
        lambda *refs: give_kernel(depth, *refs),
        grid=(total // size,),
        in_specs=[whole((1, spots.shape[0])), whole(grads.shape), whole(rider.shape)],
        out_specs=pl.BlockSpec((size, MODEL_WIDTH), lambda step: (step, 0)),
        out_shape=jax.ShapeDtypeStruct((total, MODEL_WIDTH), jnp.bfloat16),
        compiler_params=pltpu.CompilerParams(vmem_limit_bytes=VMEM_BYTES),
        cost_estimate=pl.CostEstimate(
            flops=2 * total * spots.shape[0] * MODEL_WIDTH, bytes_accessed=4 * total * MODEL_WIDTH, transcendentals=0
        ),
        name="give_rows",
    )(spots[None, :], grads, rider)


def collect_kernel(ids_ref, returned_ref, sums_ref, squares_ref):
    step = pl.program_id(0)
    rows = sums_ref.shape[0]
    row = step * rows + lax.broadcasted_iota(jnp.int32, (rows, 1), 0)
    hot = (row == ids_ref[...]).astype(jnp.float32).astype(jnp.bfloat16)
    sums = dot_nn(hot, returned_ref[...])
    sums_ref[...] = sums

    @pl.when(step == 0)
    def _():
        squares_ref[...] = jnp.zeros_like(squares_ref)

    squares_ref[0:1] += jnp.sum(sums * sums, axis=0, keepdims=True)


def collect_rows(ids, returned, table_rows):
    size = 240
    return pl.pallas_call(
        collect_kernel,
        grid=(-(-table_rows // size),),
        in_specs=[whole((1, ids.shape[0])), whole(returned.shape)],
        out_specs=[pl.BlockSpec((size, MODEL_WIDTH), lambda step: (step, 0)), whole((8, MODEL_WIDTH))],
        out_shape=[
            jax.ShapeDtypeStruct((table_rows, MODEL_WIDTH), jnp.float32),
            jax.ShapeDtypeStruct((8, MODEL_WIDTH), jnp.float32),
        ],
        compiler_params=pltpu.CompilerParams(vmem_limit_bytes=VMEM_BYTES),
        cost_estimate=pl.CostEstimate(
            flops=2 * table_rows * ids.shape[0] * MODEL_WIDTH, bytes_accessed=8 * table_rows * MODEL_WIDTH, transcendentals=0
        ),
        name="collect_rows",
    )(ids[None, :], returned)


def attention_back_kernel(
    start,
    length_ref,
    level_ref,
    grad_ref,
    first_ref,
    project_ref,
    embed_ref,
    teacher_ref,
    qkv_ref,
    out_ref,
    gains_ref,
    grad_project_ref,
    grad_att_ref,
    grad_embed_ref,
    sums_ref,
    grad_mixture_ref,
):
    turn = pl.program_id(0)
    step = turn + start
    low = jnp.bfloat16
    _, unit_one, inverse_one = norm_forward(first_ref[...], gains_ref[2:3], gains_ref[3:4])
    grad_first, gain_one, shift_one = norm_backward(grad_ref[...], unit_one, inverse_one, gains_ref[2:3])
    grad_att = grad_first.astype(low)
    grad_att_ref[...] = grad_att
    grad_mixture_ref[...] = dot_nt(grad_att, out_ref[...]).astype(low)
    lane = lax.broadcasted_iota(jnp.int32, (L, PAIR), 1)
    left_half = lane < PAIR // 2
    scaling = (MODEL_WIDTH // HEADS) ** (-0.5)
    usable = []
    for seq in range(BLOCK // L):
        rows = slice(seq * L, (seq + 1) * L)
        length = length_ref[step * (BLOCK // L) + seq]
        heads = level_ref[step * (BLOCK // L) + seq] * (HEADS // LEVELS)
        usable.append((lax.broadcasted_iota(jnp.int32, (L, 1), 0) < length).astype(jnp.float32))
        key_bias = jnp.where(lax.broadcasted_iota(jnp.int32, (L, 1), 0) < length, 0.0, -1000000000.0)
        for pair in range(PAIRS):
            at = pair * PAIR
            queries = both_heads(project_ref[rows, at : at + PAIR], left_half)
            keys = project_ref[rows, MODEL_WIDTH + at : MODEL_WIDTH + at + PAIR]
            values = project_ref[rows, 2 * MODEL_WIDTH + at : 2 * MODEL_WIDTH + at + PAIR]
            scores = dot_nt(keys, queries) * scaling + key_bias
            raised = jnp.exp(scores - jnp.max(scores, axis=0, keepdims=True))
            attend = raised * (1.0 / jnp.sum(raised, axis=0, keepdims=True))
            head = 2 * pair + (lane >= PAIR // 2).astype(jnp.int32)
            mixture = grad_mixture_ref[rows, at : at + PAIR]
            mixture = both_heads(jnp.where(head < heads, mixture, jnp.zeros_like(mixture)), left_half)
            grad_values = dot_nn(attend.astype(low), mixture)
            grad_attend = dot_nt(values, mixture)
            level = jnp.sum(grad_attend * attend, axis=0, keepdims=True)
            grad_scores = (attend * (grad_attend - level)).astype(low)
            grad_keys = dot_nn(grad_scores, queries) * scaling
            grad_queries = dot_tn(grad_scores, keys) * scaling
            grad_queries = jnp.where(left_half, grad_queries[:L], grad_queries[L:])
            grad_project_ref[rows, at : at + PAIR] = grad_queries.astype(low)
            grad_project_ref[rows, MODEL_WIDTH + at : MODEL_WIDTH + at + PAIR] = grad_keys.astype(low)
            grad_project_ref[rows, 2 * MODEL_WIDTH + at : 2 * MODEL_WIDTH + at + PAIR] = grad_values.astype(low)
    normed, unit_base, inverse_base = norm_forward(
        embed_ref[...].astype(jnp.float32), gains_ref[0:1], gains_ref[1:2]
    )
    usable = jnp.concatenate(usable, axis=0)
    gap = usable * (normed - teacher_ref[...].astype(jnp.float32))
    grad_normed = grad_first + 2.0 * gap + dot_nn(grad_project_ref[...], qkv_ref[...])
    grad_embed, gain_base, shift_base = norm_backward(grad_normed, unit_base, inverse_base, gains_ref[0:1])
    grad_embed_ref[...] = grad_embed.astype(low)

    @pl.when(turn == 0)
    def _():
        sums_ref[...] = jnp.zeros_like(sums_ref)

    for row, value in enumerate((gain_base, shift_base, gain_one, shift_one, jnp.sum(gap * gap, axis=0))):
        sums_ref[row : row + 1] += value[None]


def attention_backward(start, steps, scalars, arrays, weights, before):
    rows = arrays[0].shape[0]
    low = jnp.bfloat16

    def at_rows(width):
        return pl.BlockSpec((BLOCK, width), lambda step: (step + start, 0))

    widths = (MODEL_WIDTH, MODEL_WIDTH, 3 * MODEL_WIDTH, MODEL_WIDTH, MODEL_WIDTH)
    count = len(before)

    def body(length_ref, level_ref, *refs):
        attention_back_kernel(start, length_ref, level_ref, *refs[:8], *refs[8 + count :])

    return pl.pallas_call(
        body,
        grid=(steps,),
        in_specs=[pl.BlockSpec(memory_space=pltpu.SMEM)] * 2
        + [at_rows(width) for width in widths]
        + [
            whole((3 * MODEL_WIDTH, MODEL_WIDTH)),
            pl.BlockSpec((MODEL_WIDTH, MODEL_WIDTH), lambda step: (3, 0)),
            whole((6, MODEL_WIDTH)),
        ]
        + [pl.BlockSpec(memory_space=pl.ANY)] * count,
        out_specs=[at_rows(3 * MODEL_WIDTH), at_rows(MODEL_WIDTH), at_rows(MODEL_WIDTH), whole((8, MODEL_WIDTH))],
        out_shape=[
            jax.ShapeDtypeStruct((rows, 3 * MODEL_WIDTH), low),
            jax.ShapeDtypeStruct((rows, MODEL_WIDTH), low),
            jax.ShapeDtypeStruct((rows, MODEL_WIDTH), low),
            jax.ShapeDtypeStruct((8, MODEL_WIDTH), jnp.float32),
        ],
        input_output_aliases={10 + place: place for place in range(count)},
        scratch_shapes=[pltpu.VMEM((BLOCK, MODEL_WIDTH), low)],
        compiler_params=pltpu.CompilerParams(vmem_limit_bytes=VMEM_BYTES),
        cost_estimate=pl.CostEstimate(
            flops=steps * BLOCK * MODEL_WIDTH * MODEL_WIDTH * 40,
            bytes_accessed=steps * BLOCK * MODEL_WIDTH * 24,
            transcendentals=0,
        ),
        name="attention_backward",
    )(*scalars, *arrays, *weights, *before)


FFN_CHUNK = 768


def split_low(value):
    upper = value.astype(jnp.bfloat16)
    return jnp.concatenate([upper, (value - upper.astype(jnp.float32)).astype(jnp.bfloat16)], axis=0)


def ffn_kernel(sizes, length_ref, level_ref, first_ref, teacher_ref, pool_ref, class_ref, logits_ref, gains_ref, index_ref, *refs):
    pieces = refs[: len(sizes)]
    (hidden_ref, grad_before_ref, grad_feed_ref, middle_ref, grad_middle_ref, grad_pool_ref, grad_class_ref, sums_ref) = refs[
        len(sizes) : len(sizes) + 8
    ]
    weights_ref, slope_ref, unit_ref, inverse_ref, pooled_rows_ref, grad_rows_ref, arrivals = refs[len(sizes) + 8 :]
    step = pl.program_id(0)
    blocks = slope_ref.shape[0]
    seqs = BLOCK // L
    low = jnp.bfloat16
    row = lax.broadcasted_iota(jnp.int32, (BLOCK, 1), 0)

    def copies():
        at = 0
        for place, size in enumerate(sizes):
            yield pltpu.make_async_copy(pieces[place], weights_ref.at[pl.ds(at, size)], arrivals.at[place])
            at += size

    @pl.when(step == 0)
    def _():
        for copy in copies():
            copy.start()
        for copy in copies():
            copy.wait()
        sums_ref[...] = jnp.zeros_like(sums_ref)

    @pl.when(step < blocks)
    def _():
        middle, _, _ = norm_forward(first_ref[...], gains_ref[2:3], gains_ref[3:4])
        middle_low = middle.astype(low)
        middle_ref[...] = middle_low
        limit = jnp.full((BLOCK, 1), level_ref[step * seqs])
        for seq in range(1, seqs):
            limit = jnp.where(row >= seq * L, level_ref[step * seqs + seq], limit)
        limit = limit * (FF // LEVELS)
        for at in range(0, FF, FFN_CHUNK):
            columns = slice(at, at + FFN_CHUNK)
            before = dot_nt(middle_low, weights_ref[columns, :MODEL_WIDTH])
            square = before * before
            bend = jnp.tanh(before * (gelu_rate + gelu_rate * gelu_cube * square))
            rise = 0.5 + 0.5 * bend
            value = before * rise
            slope = rise + (0.5 * before) * (1.0 - bend * bend) * (gelu_rate + 3.0 * gelu_rate * gelu_cube * square)
            on = index_ref[:, columns] < limit
            hidden_ref[:, columns] = jnp.where(on, value, 0.0).astype(low)
            slope_ref[step, :, columns] = jnp.where(on, slope, 0.0).astype(low)
        feed = dot_nn(hidden_ref[...], weights_ref[:, MODEL_WIDTH:])
        output, unit, inverse = norm_forward(middle + feed, gains_ref[4:5], gains_ref[5:6])
        unit_ref[step] = unit
        inverse_ref[step] = inverse
        for seq in range(seqs):
            pooled_rows_ref[pl.ds(step * seqs + seq, 1), :] = output[seq * L : seq * L + 1]

    @pl.when(step == blocks)
    def _():
        first_low = pooled_rows_ref[...].astype(low)
        pooled = jnp.tanh(dot_nn(first_low, pool_ref[...]))
        pooled_low = pooled.astype(low)
        gap = dot_nn(pooled_low, class_ref[...]) - logits_ref[...]
        grad_logits = split_low(2.0 * L * gap)
        rows = gap.shape[0]
        grad_class = dot_tn(grad_logits, jnp.concatenate([pooled_low, pooled_low], axis=0))
        grad_class_ref[...] = grad_class[: grad_class_ref.shape[0]]
        grad_pooled = dot_nt(grad_logits, class_ref[...])
        grad_inner = split_low((grad_pooled[:rows] + grad_pooled[rows:]) * (1.0 - pooled * pooled))
        grad_pool_ref[...] = dot_tn(jnp.concatenate([first_low, first_low], axis=0), grad_inner).astype(low)
        grad_rows = dot_nt(grad_inner, pool_ref[...])
        grad_rows_ref[...] = grad_rows[:rows] + grad_rows[rows:]
        sums_ref[3:4, : gap.shape[1]] += L * jnp.sum(gap * gap, axis=0, keepdims=True)

    @pl.when(step > blocks)
    def _():
        block = step - blocks - 1
        unit = unit_ref[block]
        reach = jnp.full((BLOCK, 1), length_ref[block * seqs])
        pooled_grad = jnp.where(row == 0, grad_rows_ref[pl.ds(block * seqs, 1), :], 0.0)
        for seq in range(1, seqs):
            reach = jnp.where(row >= seq * L, length_ref[block * seqs + seq] + seq * L, reach)
            pooled_grad = jnp.where(row == seq * L, grad_rows_ref[pl.ds(block * seqs + seq, 1), :], pooled_grad)
        output = unit * gains_ref[4:5] + gains_ref[5:6]
        gap = jnp.where(row < reach, output - teacher_ref[...].astype(jnp.float32), 0.0)
        grad_second, gain, shift = norm_backward(2.0 * gap + pooled_grad, unit, inverse_ref[block], gains_ref[4:5])
        grad_feed = grad_second.astype(low)
        grad_feed_ref[...] = grad_feed
        for at in range(0, FF, FFN_CHUNK):
            columns = slice(at, at + FFN_CHUNK)
            grad_hidden = dot_nt(grad_feed, weights_ref[columns, MODEL_WIDTH:])
            grad_before_ref[:, columns] = (grad_hidden * slope_ref[block, :, columns].astype(jnp.float32)).astype(low)
        grad_middle_ref[...] = grad_second + dot_nn(grad_before_ref[...], weights_ref[:, :MODEL_WIDTH])
        for place, value in enumerate((gain, shift, jnp.sum(gap * gap, axis=0))):
            sums_ref[place : place + 1] += value[None]


def ffn_layer(scalars, first, teacher, dense_full, class_wide, logits_wide, norm_gains, neuron_index, pieces):
    rows = first.shape[0]
    seqs = rows // L
    blocks = rows // BLOCK
    low = jnp.bfloat16
    sizes = tuple(piece.shape[0] for piece in pieces)

    def going(width):
        return pl.BlockSpec((BLOCK, width), lambda step: (jnp.minimum(step, blocks - 1), 0))

    def coming(width):
        return pl.BlockSpec((BLOCK, width), lambda step: (jnp.maximum(step - blocks - 1, 0), 0))

    return pl.pallas_call(
        lambda *refs: ffn_kernel(sizes, *refs),
        grid=(2 * blocks + 1,),
        in_specs=[
            pl.BlockSpec(memory_space=pltpu.SMEM),
            pl.BlockSpec(memory_space=pltpu.SMEM),
            going(MODEL_WIDTH),
            coming(MODEL_WIDTH),
            pl.BlockSpec((MODEL_WIDTH, MODEL_WIDTH), lambda step: (4, 0)),
            whole(class_wide.shape),
            whole(logits_wide.shape),
            whole((6, MODEL_WIDTH)),
            whole((1, FF)),
        ]
        + [pl.BlockSpec(memory_space=pl.ANY)] * len(sizes),
        out_specs=[
            going(FF),
            coming(FF),
            coming(MODEL_WIDTH),
            going(MODEL_WIDTH),
            coming(MODEL_WIDTH),
            whole((MODEL_WIDTH, MODEL_WIDTH)),
            whole((8, MODEL_WIDTH)),
            whole((8, MODEL_WIDTH)),
        ],
        out_shape=[
            jax.ShapeDtypeStruct((rows, FF), low),
            jax.ShapeDtypeStruct((rows, FF), low),
            jax.ShapeDtypeStruct((rows, MODEL_WIDTH), low),
            jax.ShapeDtypeStruct((rows, MODEL_WIDTH), low),
            jax.ShapeDtypeStruct((rows, MODEL_WIDTH), jnp.float32),
            jax.ShapeDtypeStruct((MODEL_WIDTH, MODEL_WIDTH), low),
            jax.ShapeDtypeStruct((8, MODEL_WIDTH), jnp.float32),
            jax.ShapeDtypeStruct((8, MODEL_WIDTH), jnp.float32),
        ],
        scratch_shapes=[
            pltpu.VMEM((FF, 2 * MODEL_WIDTH), low),
            pltpu.VMEM((blocks, BLOCK, FF), low),
            pltpu.VMEM((blocks, BLOCK, MODEL_WIDTH), jnp.float32),
            pltpu.VMEM((blocks, BLOCK, 1), jnp.float32),
            pltpu.VMEM((seqs, MODEL_WIDTH), jnp.float32),
            pltpu.VMEM((seqs, MODEL_WIDTH), jnp.float32),
            pltpu.SemaphoreType.DMA((len(sizes),)),
        ],
        compiler_params=pltpu.CompilerParams(vmem_limit_bytes=VMEM_BYTES),
        cost_estimate=pl.CostEstimate(
            flops=rows * MODEL_WIDTH * FF * 16, bytes_accessed=rows * FF * 8, transcendentals=rows * FF
        ),
        name="ffn_layer",
    )(*scalars, first, teacher, dense_full, class_wide, logits_wide, norm_gains, neuron_index, *pieces)


def per_device(
    token_ids,
    replacements,
    replaced,
    lengths,
    widths,
    teacher_embed,
    teacher_hidden,
    teacher_logits,
    embed_table,
    embed_moment,
    embed_square,
    dense_weights,
    dense_moment,
    dense_square,
    feedforward,
    feedforward_moment,
    feedforward_square,
    classifier,
    classifier_moment,
    classifier_square,
    norm_gains,
    norm_moment,
    norm_square,
):
    both = ("dp", "mp")
    mp_count = lax.axis_size("mp")
    mp_index = lax.axis_index("mp")
    n_dev = lax.axis_size("dp") * mp_count
    own_seqs = teacher_logits.shape[0]
    own_rows = own_seqs * L
    table_rows = embed_table.shape[0]
    low = jnp.bfloat16
    by_bits = lax.axis_size("dp") == 8 and mp_count & (mp_count - 1) == 0
    if by_bits:
        dense_steps = gather_mp(dense_weights.astype(low))
        dense_column = jnp.concatenate(
            [lax.select_n(mp_index, *[dense_steps[k ^ z] for z in range(mp_count)]) for k in range(mp_count)],
            axis=0,
        )
    else:
        dense_column = lax.all_gather(dense_weights.astype(low), "mp", axis=0, tiled=True)
    dp_index = lax.axis_index("dp")
    neuron_piece = feedforward.shape[0]
    neuron_slot = jnp.arange(FF)
    if by_bits:
        chunk = neuron_piece * mp_count
        codes = jnp.repeat(jnp.array(piece_codes), chunk, total_repeat_length=FF)
        steps = neuron_slot % chunk // neuron_piece
        neuron_index = (dp_index ^ codes) * chunk + (mp_index ^ steps) * neuron_piece + neuron_slot % neuron_piece
    else:
        neuron_index = neuron_slot

    depth = -(-(own_rows * 3 // 2) // (n_dev * 16)) * 16
    capacity = depth - 1
    own_start = mp_index * own_seqs
    own_ids = lax.dynamic_slice_in_dim(
        jnp.where(replaced == 1, replacements, token_ids), own_start, own_seqs
    ).reshape(own_rows)
    owner = own_ids // table_rows
    local = own_ids - owner * table_rows
    place = jnp.arange(own_rows)
    first = jnp.min(
        jnp.where(own_ids[:, None] == own_ids[None, :], place[None, :], own_rows), axis=1
    )
    leads = first == place
    slot = jnp.sum(
        (leads[None, :] & (owner[:, None] == owner[None, :]) & (place[None, :] < first[:, None])).astype(
            jnp.int32
        ),
        axis=1,
    )
    deepest = jnp.max(slot)

    def positions(turn):
        rank = slot - turn * capacity
        return jnp.where((rank >= 0) & (rank < capacity), owner * depth + rank, -1)

    def wanted(turn):
        spot = jnp.where(leads, positions(turn), -1)
        hits = spot[:, None] == jnp.arange(n_dev * depth)[None, :]
        rows = jnp.max(jnp.where(hits, local[:, None], -1), axis=0).reshape(n_dev, depth)
        return jnp.where(jnp.arange(depth)[None, :] == capacity, deepest, rows)

    def exchange(blocks):
        return lax.all_to_all(blocks, both, split_axis=0, concat_axis=0)

    def asked_hot(asked):
        flat = jnp.where(jnp.arange(depth)[None, :] < capacity, asked, -1).reshape(-1)
        return (flat[:, None] == jnp.arange(table_rows)[None, :]).astype(low)

    def own_hot(turn):
        return (positions(turn)[:, None] == jnp.arange(n_dev * depth)[None, :]).astype(low)

    def answer(asked, table):
        rows = jnp.dot(asked_hot(asked), table.astype(low), preferred_element_type=low)
        return rows.reshape(n_dev, depth, MODEL_WIDTH)

    def place_rows(turn, rows):
        return jnp.dot(own_hot(turn), rows.reshape(-1, MODEL_WIDTH), preferred_element_type=low)

    own_lengths = lax.dynamic_slice_in_dim(lengths, own_start, own_seqs)
    own_levels = lax.dynamic_slice_in_dim(widths, own_start, own_seqs)
    own_count = jnp.sum(own_lengths).astype(jnp.float32)
    asked_first = exchange(wanted(0))
    ffn_low = feedforward.astype(low)
    if by_bits:
        dense_column, ffn_low = together(dense_column, ffn_low)
        dense_near = gather_near(dense_column)
        ffn_column = jnp.concatenate(gather_mp(ffn_low), axis=0)
        dense_far = far_blocks(*dense_near[1:])
        rows_first, ffn_column, *dense_blocks = together(
            answer(asked_first, embed_table), ffn_column, *dense_near, *dense_far
        )
    else:
        rows_first = answer(asked_first, embed_table)
    turns = jnp.max(asked_first[:, capacity]) // capacity + 1
    extra_rows = lax.while_loop(
        lambda state: state[0] < turns,
        lambda state: (
            state[0] + 1,
            state[1] + place_rows(state[0], exchange(answer(exchange(wanted(state[0])), embed_table))),
        ),
        (jnp.int32(1), jnp.zeros((own_rows, MODEL_WIDTH), low)),
    )[1]
    rows_first, extra_rows = together(rows_first, extra_rows)
    rows_first = exchange(rows_first)
    if by_bits:
        dense_full = assemble(dp_index, all_blocks(*dense_blocks))
        half = ffn_column.shape[0] // 2
        top, rest = ffn_column[:half], ffn_column[half:]
        x_top, y_rest = flip(top, 2), flip(rest, 4)
        x_rest, y_top = flip(rest, 2), flip(top, 4)
        own_lengths, own_levels, own_count, dense_full, *near = together(
            own_lengths, own_levels, own_count, dense_full, top, rest, x_top, x_rest, y_top, y_rest
        )
        far = flip(near[2], 4), flip(near[5], 2)
        near = near + [flip(block, 1) for block in near]
    else:
        dense_full = lax.all_gather(dense_column, "dp", axis=0, tiled=True)
        ffn_column = lax.all_gather(ffn_low, "mp", axis=0, tiled=True)
        ffn_pieces = [lax.all_gather(ffn_column, "dp", axis=0, tiled=True)]
    embedded_low = place_rows(0, rows_first) + extra_rows

    scalars = (own_lengths, own_levels)
    blocks = own_rows // BLOCK
    if by_bits:
        layer = attention_layer(0, blocks, scalars, embedded_low, dense_full, norm_gains, ())
        flow = together(*layer, *near, *far)
        layer, near, far = flow[:4], flow[4:16], flow[16:]
        far = [*far, flip(far[0], 1), flip(far[1], 1)]
        ffn_pieces = [*near[:4], *far[:2], *near[4:10], *far[2:], *near[10:]]
    else:
        layer = attention_layer(0, blocks, scalars, embedded_low, dense_full, norm_gains, ())
    project, head_mixture, first_sum, normed_low = layer
    class_pad = -classifier.shape[1] % 128
    hidden_low, grad_before, grad_feed_low, middle_low, grad_middle, grad_pool_rows, grad_class, ffn_sums = ffn_layer(
        scalars,
        first_sum,
        teacher_hidden.reshape(own_rows, MODEL_WIDTH),
        dense_full,
        jnp.pad(classifier, ((0, 0), (0, class_pad))).astype(low),
        jnp.pad(teacher_logits, ((0, 0), (0, class_pad))),
        norm_gains,
        neuron_index[None, :],
        ffn_pieces,
    )
    grad_class = grad_class[: classifier.shape[1]]

    def over_both(rows):
        rows = lax.psum_scatter(rows, "dp", scatter_dimension=0, tiled=True)
        return lax.psum_scatter(rows, "mp", scatter_dimension=0, tiled=True).astype(jnp.float32)

    def weight_sums(left, right):
        half = left.shape[1] // 2
        given = flip(contract_first(left[:, half:], right).astype(low), 1)
        return contract_first(left[:, :half], right).astype(low), given

    def by_core(rows):
        chunks = rows.reshape(4, 2, rows.shape[0] // 8, rows.shape[1])
        core = dp_index % 2
        return [lax.dynamic_index_in_dim(chunks, side, 1, keepdims=False) for side in (core, 1 - core)]

    def dense_scatter(own, other):
        place = dp_index // 2
        parts = add_low(own, flip(other, 1))
        half = parts.shape[1] // 2
        parts = [lax.dynamic_index_in_dim(parts, place ^ code, 0, keepdims=False) for code in (0, 1, 3, 2)]
        top = jnp.concatenate([part[:half] for part in parts], axis=0)
        rest = jnp.concatenate([part[half:] for part in parts], axis=0)
        parts = send_last(*send_first(top, rest))
        parts = jnp.concatenate(parts, axis=0).reshape(mp_count, -1, MODEL_WIDTH)
        parts = [lax.dynamic_index_in_dim(parts, mp_index ^ step, 0, keepdims=False) for step in range(mp_count)]
        return [parts[0]] + [pass_mp(parts[step], step) for step in range(1, mp_count)]

    arrays = [
        grad_middle,
        first_sum,
        project,
        embedded_low,
        teacher_embed.reshape(own_rows, MODEL_WIDTH),
    ]
    weights = (dense_full, dense_full, norm_gains)
    if by_bits:
        down_own, down_given = weight_sums(hidden_low, grad_feed_low)
        up_own, up_given = weight_sums(grad_before, middle_low)
        parts = (add_low(up_own, up_given), add_low(down_own, down_given))
        arrays[0], *parts = together(arrays[0], *parts)
        parts = send_first(*parts)
        before = attention_backward(0, blocks - 1, scalars, arrays, weights, ())
        arrays[0], *flow = together(arrays[0], *before, *parts)
        *before, sums_one = flow[:4]
        parts = send_last(*flow[4:])
        before = attention_backward(blocks - 1, 1, scalars, arrays, weights, before)
        flow = together(*before, *parts)
        *before, sums_last = flow[:4]
        parts = [part.reshape(mp_count, neuron_piece, MODEL_WIDTH) for part in flow[4:]]
        ffn_parts = [jnp.concatenate([part[step] for part in parts], axis=1) for step in range(mp_count)]
        ffn_parts = [ffn_parts[0]] + [pass_mp(ffn_parts[step], step) for step in range(1, mp_count)]
        sums = sums_one + sums_last
    else:
        ffn_grad = jnp.concatenate(
            [contract_first(grad_before, middle_low), contract_first(hidden_low, grad_feed_low)], axis=1
        ).astype(low)
        ffn_grad = over_both(ffn_grad)
        *before, sums = attention_backward(0, blocks, scalars, arrays, weights, ())
    grad_project, grad_att_low, grad_embed_low = before
    grad_dense = jnp.concatenate(
        [
            contract_first(grad_project, normed_low).astype(low),
            contract_first(head_mixture, grad_att_low).astype(low),
            grad_pool_rows,
        ],
        axis=0,
    )
    loss_own = jnp.sum(sums[4]) + jnp.sum(ffn_sums[2:4])

    small = jnp.concatenate([sums[:4], ffn_sums[:2], grad_class], axis=0)
    small_rows = small.shape[0]
    upper = lax.reduce_precision(small, 8, 7)
    rider = jnp.concatenate([upper, small - upper], axis=0).astype(low)
    rider = jnp.pad(rider, ((0, n_dev - 2 * small_rows), (0, 0)))

    def give_back(turn, rider):
        return give_rows(positions(turn), grad_embed_low, rider, depth).reshape(n_dev, depth, MODEL_WIDTH)

    def collect(asked, returned):
        ids = jnp.where(jnp.arange(depth)[None, :] < capacity, asked, -1).reshape(-1)
        return collect_rows(ids, returned.reshape(-1, MODEL_WIDTH), table_rows)

    def collect_more(state):
        turn, total, _ = state
        total = total + collect(exchange(wanted(turn)), exchange(give_back(turn, jnp.zeros_like(rider))))[0]
        return turn + 1, total, jnp.zeros((8, MODEL_WIDTH)).at[0].set(jnp.sum(total * total, axis=0))

    given = give_back(0, rider)
    if by_bits:
        given, *flow = together(given, *by_core(grad_dense), *ffn_parts)
        grad_dense, ffn_parts = flow[:2], flow[2:]
        ffn_grad = sum(part.astype(jnp.float32) for part in ffn_parts)
    returned = exchange(given)
    dense_parts = dense_scatter(*grad_dense) if by_bits else [over_both(grad_dense)]
    table_sums = collect(asked_first, returned)
    *table_sums, returned = together(*table_sums, returned)
    *table_sums, dense_first = together(*table_sums, dense_parts[0])
    dense_parts = together(*dense_parts[1:], dense_first)
    dense_grad = sum(part.astype(jnp.float32) for part in dense_parts)
    _, table_grad, table_squares = lax.while_loop(
        lambda state: state[0] < turns, collect_more, (jnp.int32(1), *table_sums)
    )
    small_row = jnp.sum(returned[:, capacity].astype(jnp.float32), axis=0)
    square_sum = jnp.sum(table_squares) + jnp.sum(dense_grad * dense_grad) + jnp.sum(ffn_grad * ffn_grad)
    message = jnp.concatenate([small_row, jnp.stack([square_sum, own_count, loss_own])])
    message = jnp.pad(message, (0, -message.shape[0] % 128))
    told = exchange(jnp.broadcast_to(message[None], (n_dev, message.shape[0])))
    scalars = jnp.sum(told[:, MODEL_WIDTH : MODEL_WIDTH + 128], axis=0, keepdims=True)
    token_count, loss_sum = scalars[:, 1:2], scalars[:, 2:3]
    small = told[:small_rows, :MODEL_WIDTH] + told[small_rows : 2 * small_rows, :MODEL_WIDTH]
    total_square = scalars[:, :1] + jnp.sum(jnp.sum(small * small, axis=0, keepdims=True), axis=1, keepdims=True)
    gains_grad, class_grad = small[:6], small[6:].T
    inverse = 1.0 / token_count
    grad_norm = jnp.sqrt(total_square) * inverse
    scaling = inverse * (clip_bound / jnp.maximum(grad_norm, clip_bound))
    table_new = adam_update(
        embed_table, table_grad * scaling, embed_moment, embed_square, weight_decay, learn_rate
    )
    dense_new = adam_update(
        dense_weights, dense_grad * scaling, dense_moment, dense_square, weight_decay, learn_rate
    )
    ffn_new = adam_update(
        feedforward,
        ffn_grad * scaling,
        feedforward_moment,
        feedforward_square,
        weight_decay,
        learn_rate,
    )
    class_new = adam_update(
        classifier,
        class_grad * scaling,
        classifier_moment,
        classifier_square,
        weight_decay,
        learn_rate,
    )
    gains_new = adam_update(
        norm_gains, gains_grad * scaling, norm_moment, norm_square, 0.0, gain_rate
    )
    return (
        loss_sum.reshape(()),
        token_count.reshape(()),
        grad_norm.reshape(()),
        table_new[0],
        table_new[1],
        table_new[2],
        table_new[0].astype(jnp.bfloat16),
        dense_new[0],
        dense_new[1],
        dense_new[2],
        dense_new[0].astype(jnp.bfloat16),
        ffn_new[0],
        ffn_new[1],
        ffn_new[2],
        ffn_new[0].astype(jnp.bfloat16),
        class_new[0],
        class_new[1],
        class_new[2],
        class_new[0].astype(jnp.bfloat16),
        gains_new[0],
        gains_new[1],
        gains_new[2],
    )


def solution(mesh):
    placed = (
        P("dp", None),
        P("dp", None),
        P("dp", None),
        P("dp"),
        P("dp"),
        P(("dp", "mp"), None, None),
        P(("dp", "mp"), None, None),
        P(("dp", "mp"), None),
        P(("dp", "mp"), None),
        P(("dp", "mp"), None),
        P(("dp", "mp"), None),
        P(("dp", "mp"), None),
        P(("dp", "mp"), None),
        P(("dp", "mp"), None),
        P(("dp", "mp"), None),
        P(("dp", "mp"), None),
        P(("dp", "mp"), None),
        P(),
        P(),
        P(),
        P(),
        P(),
        P(),
    )
    return jax.shard_map(
        per_device,
        mesh=mesh,
        in_specs=placed,
        out_specs=(
            P(),
            P(),
            P(),
            P(("dp", "mp"), None),
            P(("dp", "mp"), None),
            P(("dp", "mp"), None),
            P(("dp", "mp"), None),
            P(("dp", "mp"), None),
            P(("dp", "mp"), None),
            P(("dp", "mp"), None),
            P(("dp", "mp"), None),
            P(("dp", "mp"), None),
            P(("dp", "mp"), None),
            P(("dp", "mp"), None),
            P(("dp", "mp"), None),
            P(),
            P(),
            P(),
            P(),
            P(),
            P(),
            P(),
        ),
        check_vma=False,
    )
```

```python
import jax
import jax.numpy as jnp
from jax import lax
from jax.experimental import pallas as pl
from jax.experimental.pallas import tpu as pltpu
from jax.sharding import PartitionSpec as P

MODEL_WIDTH = 768
HEADS = 12
FF = 3072
L = 128
LEVELS = 4
STEP = 10


highest_precision = lax.Precision.HIGHEST
norm_epsilon = 1e-05
learn_rate = 0.05
gain_rate = 0.5
beta_one = 0.9
beta_two = 0.999
adam_epsilon = 1e-08
weight_decay = 0.01
clip_bound = 1.0


def norm_forward(values, gain_row, shift_row):
    center = values - jnp.mean(values, axis=-1, keepdims=True)
    spread = jnp.mean(center * center, axis=-1, keepdims=True)
    inverse = lax.rsqrt(spread + norm_epsilon)
    unit = center * inverse
    return (unit * gain_row + shift_row, unit, inverse)


def norm_backward(grad, unit, inverse, gain_row):
    scaled = grad * gain_row
    level = jnp.mean(scaled, axis=-1, keepdims=True)
    along = jnp.mean(scaled * unit, axis=-1, keepdims=True)
    grad_values = inverse * (scaled - level - unit * along)
    return (grad_values, jnp.sum(grad * unit, axis=0), jnp.sum(grad, axis=0))


gelu_rate = 0.7978845608028654
gelu_cube = 0.044715


def gelu_forward(before):
    bend = jnp.tanh(gelu_rate * (before + gelu_cube * before * before * before))
    return 0.5 * before * (1.0 + bend)


def gelu_slope(before):
    bend = jnp.tanh(gelu_rate * (before + gelu_cube * before * before * before))
    inner = gelu_rate * (1.0 + 3.0 * gelu_cube * before * before)
    return 0.5 * (1.0 + bend) + 0.5 * before * (1.0 - bend * bend) * inner


def adam_update(weight, gradient, first_moment, second, decay_rate, rate):
    first_new = beta_one * first_moment + (1.0 - beta_one) * gradient
    second_new = beta_two * second + (1.0 - beta_two) * gradient * gradient
    direction = (
        first_new
        / (1.0 - beta_one**STEP)
        / (jnp.sqrt(second_new / (1.0 - beta_two**STEP)) + adam_epsilon)
    )
    return (weight - rate * (direction + decay_rate * weight), first_new, second_new)


def contract_last(left, right):
    return lax.dot_general(
        left, right, (((1,), (1,)), ((), ())), preferred_element_type=jnp.float32
    )


def contract_first(left, right):
    return lax.dot_general(
        left, right, (((0,), (0,)), ((), ())), preferred_element_type=jnp.float32
    )


def flip(block, bit):
    size = lax.axis_size("dp")
    return lax.ppermute(block, "dp", [(i, i ^ bit) for i in range(size)])


def add_low(*terms):
    return sum(term.astype(jnp.float32) for term in terms).astype(jnp.bfloat16)


piece_codes = (0, 2, 6, 4, 1, 3, 7, 5)


def gather_near(own):
    return own, flip(own, 2), flip(own, 4)


def far_blocks(along_x, along_y):
    half = along_x.shape[0] // 2
    return flip(along_x[:half], 4), flip(along_y[half:], 2)


def all_blocks(own, along_x, along_y, far_top, far_low):
    mine = [own, along_x, far_top, far_low, along_y]
    return mine + [flip(block, 1) for block in mine]


def assemble_kernel(place_ref, *refs):
    pieces, full_ref, arrivals = refs[:10], refs[10], refs[11]
    chunk = pieces[0].shape[0]
    copies = []
    for block, piece in enumerate(pieces):
        code = (0, 2, 6, 6, 4)[block % 5] + block // 5
        at = (place_ref[0] ^ code) * chunk
        if block % 5 == 3:
            at = at + chunk // 2
        at = pl.multiple_of(at, 16)
        copies.append(
            pltpu.make_async_copy(piece, full_ref.at[pl.ds(at, piece.shape[0])], arrivals.at[block])
        )
    for copy in copies:
        copy.start()
    for copy in copies:
        copy.wait()


def assemble(place, pieces):
    chunk, width = pieces[0].shape
    return pl.pallas_call(
        assemble_kernel,
        in_specs=[pl.BlockSpec(memory_space=pltpu.SMEM)] + [pl.BlockSpec(memory_space=pl.ANY)] * len(pieces),
        out_specs=pl.BlockSpec(memory_space=pltpu.VMEM),
        out_shape=jax.ShapeDtypeStruct((8 * chunk, width), pieces[0].dtype),
        compiler_params=pltpu.CompilerParams(vmem_limit_bytes=VMEM_BYTES),
        scratch_shapes=[pltpu.SemaphoreType.DMA((len(pieces),))],
        cost_estimate=pl.CostEstimate(flops=0, bytes_accessed=32 * chunk * width, transcendentals=0),
        name="assemble",
    )(place.reshape(1), *pieces)


def partner(index, step):
    size = lax.axis_size("mp")
    return index ^ step if size & (size - 1) == 0 else (index + step) % size


def pass_mp(block, step):
    return lax.ppermute(block, "mp", [(i, partner(i, step)) for i in range(lax.axis_size("mp"))])


def gather_mp(rows):
    return [rows] + [pass_mp(rows, step) for step in range(1, lax.axis_size("mp"))]


def send_first(top, rest):
    from_x = flip(add_low(*top(1, 3)), 2)
    from_y = flip(add_low(*rest(2, 4)), 4)
    size = from_x.shape[0] // 2
    late_y = add_low(*top(3, 4), from_x[size:])
    late_x = add_low(*rest(1, 2), from_y[:size])
    return together(late_y, late_x, from_x, from_y)


def send_last(top, rest, late_y, late_x, from_x, from_y):
    size = late_y.shape[0]
    late_y, late_x = flip(late_y, 4), flip(late_x, 2)
    return add_low(*top(0, 1), from_x[:size], late_y), add_low(*rest(0, 1), from_y[size:], late_x)


def blocks_of(*terms):
    size = terms[0].shape[0] // 4
    return lambda first, last: [term[first * size : last * size] for term in terms]


def together(*values):
    return lax.optimization_barrier(values)


PAIR = 2 * (MODEL_WIDTH // HEADS)
PAIRS = HEADS // 2
BLOCK = 2 * L
VMEM_BYTES = 56 * 1024 * 1024


def dot_nt(left, right):
    return lax.dot_general(
        left, right, (((1,), (1,)), ((), ())), preferred_element_type=jnp.float32
    )


def dot_tn(left, right):
    return lax.dot_general(
        left, right, (((0,), (0,)), ((), ())), preferred_element_type=jnp.float32
    )


def dot_nn(left, right):
    return jnp.dot(left, right, preferred_element_type=jnp.float32)


def both_heads(pair, left_half):
    zero = jnp.zeros_like(pair)
    return jnp.concatenate([jnp.where(left_half, pair, zero), jnp.where(left_half, zero, pair)], axis=0)


def pair_attend(queries, keys, key_bias):
    scores = dot_nt(queries, keys) * (MODEL_WIDTH // HEADS) ** (-0.5) + key_bias
    raised = jnp.exp(scores - jnp.max(scores, axis=-1, keepdims=True))
    return raised * (1.0 / jnp.sum(raised, axis=-1, keepdims=True))


def attention_kernel(
    start, length_ref, level_ref, embed_ref, qkv_ref, out_ref, gains_ref, project_ref, mixture_ref, first_ref, normed_ref
):
    step = pl.program_id(0) + start
    normed, _, _ = norm_forward(embed_ref[...].astype(jnp.float32), gains_ref[0:1], gains_ref[1:2])
    normed_low = normed.astype(jnp.bfloat16)
    normed_ref[...] = normed_low
    for part in range(3):
        columns = slice(part * MODEL_WIDTH, (part + 1) * MODEL_WIDTH)
        project_ref[:, columns] = dot_nt(normed_low, qkv_ref[columns]).astype(jnp.bfloat16)
    lane = lax.broadcasted_iota(jnp.int32, (L, PAIR), 1)
    left_half = lane < PAIR // 2
    for seq in range(BLOCK // L):
        rows = slice(seq * L, (seq + 1) * L)
        length = length_ref[step * (BLOCK // L) + seq]
        heads = level_ref[step * (BLOCK // L) + seq] * (HEADS // LEVELS)
        key_bias = jnp.where(lax.broadcasted_iota(jnp.int32, (1, L), 1) < length, 0.0, -1000000000.0)
        for pair in range(PAIRS):
            at = pair * PAIR
            queries = both_heads(project_ref[rows, at : at + PAIR], left_half)
            keys = project_ref[rows, MODEL_WIDTH + at : MODEL_WIDTH + at + PAIR]
            values = project_ref[rows, 2 * MODEL_WIDTH + at : 2 * MODEL_WIDTH + at + PAIR]
            attend = pair_attend(queries, keys, key_bias).astype(jnp.bfloat16)
            mixed = dot_nn(attend, values)
            mixed = jnp.where(left_half, mixed[:L], mixed[L:])
            head = 2 * pair + (lane >= PAIR // 2).astype(jnp.int32)
            mixture_ref[rows, at : at + PAIR] = jnp.where(head < heads, mixed, 0.0).astype(jnp.bfloat16)
    first_ref[...] = normed + dot_nn(mixture_ref[...], out_ref[...])


def whole(shape):
    return pl.BlockSpec(shape, lambda step: (0,) * len(shape))


def by_rows(width):
    return pl.BlockSpec((BLOCK, width), lambda step: (step, 0))


def attention_layer(start, steps, scalars, embedded, dense_full, norm_gains, before):
    rows = embedded.shape[0]
    low = jnp.bfloat16
    count = len(before)

    def at_rows(width):
        return pl.BlockSpec((BLOCK, width), lambda step: (step + start, 0))

    def body(length_ref, level_ref, *refs):
        attention_kernel(start, length_ref, level_ref, *refs[:4], *refs[4 + count :])

    return pl.pallas_call(
        body,
        grid=(steps,),
        in_specs=[
            pl.BlockSpec(memory_space=pltpu.SMEM),
            pl.BlockSpec(memory_space=pltpu.SMEM),
            at_rows(MODEL_WIDTH),
            whole((3 * MODEL_WIDTH, MODEL_WIDTH)),
            pl.BlockSpec((MODEL_WIDTH, MODEL_WIDTH), lambda step: (3, 0)),
            whole((6, MODEL_WIDTH)),
        ]
        + [pl.BlockSpec(memory_space=pl.ANY)] * count,
        out_specs=[at_rows(3 * MODEL_WIDTH), at_rows(MODEL_WIDTH), at_rows(MODEL_WIDTH), at_rows(MODEL_WIDTH)],
        out_shape=[
            jax.ShapeDtypeStruct((rows, 3 * MODEL_WIDTH), low),
            jax.ShapeDtypeStruct((rows, MODEL_WIDTH), low),
            jax.ShapeDtypeStruct((rows, MODEL_WIDTH), jnp.float32),
            jax.ShapeDtypeStruct((rows, MODEL_WIDTH), low),
        ],
        input_output_aliases={6 + place: place for place in range(count)},
        compiler_params=pltpu.CompilerParams(vmem_limit_bytes=VMEM_BYTES),
        cost_estimate=pl.CostEstimate(
            flops=steps * BLOCK * MODEL_WIDTH * MODEL_WIDTH * 20,
            bytes_accessed=steps * BLOCK * MODEL_WIDTH * 16,
            transcendentals=0,
        ),
        name="attention_layer",
    )(*scalars, embedded, dense_full, dense_full, norm_gains, *before)


def give_kernel(depth, spots_ref, grad_ref, rider_ref, sums_ref):
    rows = sums_ref.shape[0]
    row = pl.program_id(0) * rows + lax.broadcasted_iota(jnp.int32, (rows, 1), 0)
    last = lax.broadcasted_iota(jnp.int32, (1, rider_ref.shape[0]), 1) * depth + depth - 1
    own = (row == spots_ref[...]).astype(jnp.float32).astype(jnp.bfloat16)
    ride = (row == last).astype(jnp.float32).astype(jnp.bfloat16)
    sums_ref[...] = (dot_nn(own, grad_ref[...]) + dot_nn(ride, rider_ref[...])).astype(jnp.bfloat16)


def give_rows(spots, grads, rider, depth):
    total = rider.shape[0] * depth
    size = 512 if total % 512 == 0 else total
    return pl.pallas_call(
        lambda *refs: give_kernel(depth, *refs),
        grid=(total // size,),
        in_specs=[whole((1, spots.shape[0])), whole(grads.shape), whole(rider.shape)],
        out_specs=pl.BlockSpec((size, MODEL_WIDTH), lambda step: (step, 0)),
        out_shape=jax.ShapeDtypeStruct((total, MODEL_WIDTH), jnp.bfloat16),
        compiler_params=pltpu.CompilerParams(vmem_limit_bytes=VMEM_BYTES),
        cost_estimate=pl.CostEstimate(
            flops=2 * total * spots.shape[0] * MODEL_WIDTH, bytes_accessed=4 * total * MODEL_WIDTH, transcendentals=0
        ),
        name="give_rows",
    )(spots[None, :], grads, rider)


def collect_kernel(ids_ref, returned_ref, sums_ref, squares_ref):
    step = pl.program_id(0)
    rows = sums_ref.shape[0]
    row = step * rows + lax.broadcasted_iota(jnp.int32, (rows, 1), 0)
    hot = (row == ids_ref[...]).astype(jnp.float32).astype(jnp.bfloat16)
    sums = dot_nn(hot, returned_ref[...])
    sums_ref[...] = sums

    @pl.when(step == 0)
    def _():
        squares_ref[...] = jnp.zeros_like(squares_ref)

    squares_ref[0:1] += jnp.sum(sums * sums, axis=0, keepdims=True)


def collect_rows(ids, returned, table_rows):
    size = 240
    return pl.pallas_call(
        collect_kernel,
        grid=(-(-table_rows // size),),
        in_specs=[whole((1, ids.shape[0])), whole(returned.shape)],
        out_specs=[pl.BlockSpec((size, MODEL_WIDTH), lambda step: (step, 0)), whole((8, MODEL_WIDTH))],
        out_shape=[
            jax.ShapeDtypeStruct((table_rows, MODEL_WIDTH), jnp.float32),
            jax.ShapeDtypeStruct((8, MODEL_WIDTH), jnp.float32),
        ],
        compiler_params=pltpu.CompilerParams(vmem_limit_bytes=VMEM_BYTES),
        cost_estimate=pl.CostEstimate(
            flops=2 * table_rows * ids.shape[0] * MODEL_WIDTH, bytes_accessed=8 * table_rows * MODEL_WIDTH, transcendentals=0
        ),
        name="collect_rows",
    )(ids[None, :], returned)


def attention_back_kernel(
    start,
    length_ref,
    level_ref,
    grad_ref,
    first_ref,
    project_ref,
    embed_ref,
    teacher_ref,
    qkv_ref,
    out_ref,
    gains_ref,
    grad_project_ref,
    grad_att_ref,
    grad_embed_ref,
    sums_ref,
    grad_mixture_ref,
):
    turn = pl.program_id(0)
    step = turn + start
    low = jnp.bfloat16
    _, unit_one, inverse_one = norm_forward(first_ref[...], gains_ref[2:3], gains_ref[3:4])
    grad_first, gain_one, shift_one = norm_backward(grad_ref[...], unit_one, inverse_one, gains_ref[2:3])
    grad_att = grad_first.astype(low)
    grad_att_ref[...] = grad_att
    grad_mixture_ref[...] = dot_nt(grad_att, out_ref[...]).astype(low)
    lane = lax.broadcasted_iota(jnp.int32, (L, PAIR), 1)
    left_half = lane < PAIR // 2
    scaling = (MODEL_WIDTH // HEADS) ** (-0.5)
    usable = []
    for seq in range(BLOCK // L):
        rows = slice(seq * L, (seq + 1) * L)
        length = length_ref[step * (BLOCK // L) + seq]
        heads = level_ref[step * (BLOCK // L) + seq] * (HEADS // LEVELS)
        usable.append((lax.broadcasted_iota(jnp.int32, (L, 1), 0) < length).astype(jnp.float32))
        key_bias = jnp.where(lax.broadcasted_iota(jnp.int32, (L, 1), 0) < length, 0.0, -1000000000.0)
        for pair in range(PAIRS):
            at = pair * PAIR
            queries = both_heads(project_ref[rows, at : at + PAIR], left_half)
            keys = project_ref[rows, MODEL_WIDTH + at : MODEL_WIDTH + at + PAIR]
            values = project_ref[rows, 2 * MODEL_WIDTH + at : 2 * MODEL_WIDTH + at + PAIR]
            scores = dot_nt(keys, queries) * scaling + key_bias
            raised = jnp.exp(scores - jnp.max(scores, axis=0, keepdims=True))
            attend = raised * (1.0 / jnp.sum(raised, axis=0, keepdims=True))
            head = 2 * pair + (lane >= PAIR // 2).astype(jnp.int32)
            mixture = grad_mixture_ref[rows, at : at + PAIR]
            mixture = both_heads(jnp.where(head < heads, mixture, jnp.zeros_like(mixture)), left_half)
            grad_values = dot_nn(attend.astype(low), mixture)
            grad_attend = dot_nt(values, mixture)
            level = jnp.sum(grad_attend * attend, axis=0, keepdims=True)
            grad_scores = (attend * (grad_attend - level)).astype(low)
            grad_keys = dot_nn(grad_scores, queries) * scaling
            grad_queries = dot_tn(grad_scores, keys) * scaling
            grad_queries = jnp.where(left_half, grad_queries[:L], grad_queries[L:])
            grad_project_ref[rows, at : at + PAIR] = grad_queries.astype(low)
            grad_project_ref[rows, MODEL_WIDTH + at : MODEL_WIDTH + at + PAIR] = grad_keys.astype(low)
            grad_project_ref[rows, 2 * MODEL_WIDTH + at : 2 * MODEL_WIDTH + at + PAIR] = grad_values.astype(low)
    normed, unit_base, inverse_base = norm_forward(
        embed_ref[...].astype(jnp.float32), gains_ref[0:1], gains_ref[1:2]
    )
    usable = jnp.concatenate(usable, axis=0)
    gap = usable * (normed - teacher_ref[...].astype(jnp.float32))
    grad_normed = grad_first + 2.0 * gap + dot_nn(grad_project_ref[...], qkv_ref[...])
    grad_embed, gain_base, shift_base = norm_backward(grad_normed, unit_base, inverse_base, gains_ref[0:1])
    grad_embed_ref[...] = grad_embed.astype(low)

    @pl.when(turn == 0)
    def _():
        sums_ref[...] = jnp.zeros_like(sums_ref)

    for row, value in enumerate((gain_base, shift_base, gain_one, shift_one, jnp.sum(gap * gap, axis=0))):
        sums_ref[row : row + 1] += value[None]


def attention_backward(start, steps, scalars, arrays, weights, before):
    rows = arrays[0].shape[0]
    low = jnp.bfloat16

    def at_rows(width):
        return pl.BlockSpec((BLOCK, width), lambda step: (step + start, 0))

    widths = (MODEL_WIDTH, MODEL_WIDTH, 3 * MODEL_WIDTH, MODEL_WIDTH, MODEL_WIDTH)
    count = len(before)

    def body(length_ref, level_ref, *refs):
        attention_back_kernel(start, length_ref, level_ref, *refs[:8], *refs[8 + count :])

    return pl.pallas_call(
        body,
        grid=(steps,),
        in_specs=[pl.BlockSpec(memory_space=pltpu.SMEM)] * 2
        + [at_rows(width) for width in widths]
        + [
            whole((3 * MODEL_WIDTH, MODEL_WIDTH)),
            pl.BlockSpec((MODEL_WIDTH, MODEL_WIDTH), lambda step: (3, 0)),
            whole((6, MODEL_WIDTH)),
        ]
        + [pl.BlockSpec(memory_space=pl.ANY)] * count,
        out_specs=[at_rows(3 * MODEL_WIDTH), at_rows(MODEL_WIDTH), at_rows(MODEL_WIDTH), whole((8, MODEL_WIDTH))],
        out_shape=[
            jax.ShapeDtypeStruct((rows, 3 * MODEL_WIDTH), low),
            jax.ShapeDtypeStruct((rows, MODEL_WIDTH), low),
            jax.ShapeDtypeStruct((rows, MODEL_WIDTH), low),
            jax.ShapeDtypeStruct((8, MODEL_WIDTH), jnp.float32),
        ],
        input_output_aliases={10 + place: place for place in range(count)},
        scratch_shapes=[pltpu.VMEM((BLOCK, MODEL_WIDTH), low)],
        compiler_params=pltpu.CompilerParams(vmem_limit_bytes=VMEM_BYTES),
        cost_estimate=pl.CostEstimate(
            flops=steps * BLOCK * MODEL_WIDTH * MODEL_WIDTH * 40,
            bytes_accessed=steps * BLOCK * MODEL_WIDTH * 24,
            transcendentals=0,
        ),
        name="attention_backward",
    )(*scalars, *arrays, *weights, *before)


FFN_CHUNK = 768


def split_low(value):
    upper = value.astype(jnp.bfloat16)
    return jnp.concatenate([upper, (value - upper.astype(jnp.float32)).astype(jnp.bfloat16)], axis=0)


def ffn_kernel(sizes, length_ref, level_ref, first_ref, teacher_ref, pool_ref, class_ref, logits_ref, gains_ref, index_ref, *refs):
    pieces = refs[: len(sizes)]
    (hidden_ref, grad_before_ref, grad_feed_ref, middle_ref, grad_middle_ref, grad_pool_ref, grad_class_ref, sums_ref) = refs[
        len(sizes) : len(sizes) + 8
    ]
    weights_ref, slope_ref, unit_ref, inverse_ref, pooled_rows_ref, grad_rows_ref, arrivals = refs[len(sizes) + 8 :]
    step = pl.program_id(0)
    blocks = slope_ref.shape[0]
    seqs = BLOCK // L
    low = jnp.bfloat16
    row = lax.broadcasted_iota(jnp.int32, (BLOCK, 1), 0)

    def copies():
        at = 0
        for place, size in enumerate(sizes):
            yield pltpu.make_async_copy(pieces[place], weights_ref.at[pl.ds(at, size)], arrivals.at[place])
            at += size

    def go(waiting):
        arriving = list(copies()) if waiting else []
        for copy in arriving:
            copy.start()
        if waiting:
            sums_ref[...] = jnp.zeros_like(sums_ref)
        waited, arrived = 0, 0
        middle, _, _ = norm_forward(first_ref[...], gains_ref[2:3], gains_ref[3:4])
        middle_low = middle.astype(low)
        middle_ref[...] = middle_low
        limit = jnp.full((BLOCK, 1), level_ref[step * seqs])
        for seq in range(1, seqs):
            limit = jnp.where(row >= seq * L, level_ref[step * seqs + seq], limit)
        limit = limit * (FF // LEVELS)
        for at in range(0, FF, FFN_CHUNK):
            columns = slice(at, at + FFN_CHUNK)
            while waiting and arrived < at + FFN_CHUNK:
                arriving[waited].wait()
                arrived += sizes[waited]
                waited += 1
            before = dot_nt(middle_low, weights_ref[columns, :MODEL_WIDTH])
            square = before * before
            bend = jnp.tanh(before * (gelu_rate + gelu_rate * gelu_cube * square))
            rise = 0.5 + 0.5 * bend
            value = before * rise
            slope = rise + (0.5 * before) * (1.0 - bend * bend) * (gelu_rate + 3.0 * gelu_rate * gelu_cube * square)
            on = index_ref[:, columns] < limit
            hidden_ref[:, columns] = jnp.where(on, value, 0.0).astype(low)
            slope_ref[step, :, columns] = jnp.where(on, slope, 0.0).astype(low)
        feed = dot_nn(hidden_ref[...], weights_ref[:, MODEL_WIDTH:])
        output, unit, inverse = norm_forward(middle + feed, gains_ref[4:5], gains_ref[5:6])
        unit_ref[step] = unit
        inverse_ref[step] = inverse
        for seq in range(seqs):
            pooled_rows_ref[pl.ds(step * seqs + seq, 1), :] = output[seq * L : seq * L + 1]

    @pl.when(step == 0)
    def _():
        go(True)

    @pl.when((step > 0) & (step < blocks))
    def _():
        go(False)

    @pl.when(step == blocks)
    def _():
        first_low = pooled_rows_ref[...].astype(low)
        pooled = jnp.tanh(dot_nn(first_low, pool_ref[...]))
        pooled_low = pooled.astype(low)
        gap = dot_nn(pooled_low, class_ref[...]) - logits_ref[...]
        grad_logits = split_low(2.0 * L * gap)
        rows = gap.shape[0]
        grad_class = dot_tn(grad_logits, jnp.concatenate([pooled_low, pooled_low], axis=0))
        grad_class_ref[...] = grad_class[: grad_class_ref.shape[0]]
        grad_pooled = dot_nt(grad_logits, class_ref[...])
        grad_inner = split_low((grad_pooled[:rows] + grad_pooled[rows:]) * (1.0 - pooled * pooled))
        grad_pool_ref[...] = dot_tn(jnp.concatenate([first_low, first_low], axis=0), grad_inner).astype(low)
        grad_rows = dot_nt(grad_inner, pool_ref[...])
        grad_rows_ref[...] = grad_rows[:rows] + grad_rows[rows:]
        sums_ref[3:4, : gap.shape[1]] += L * jnp.sum(gap * gap, axis=0, keepdims=True)

    @pl.when(step > blocks)
    def _():
        block = step - blocks - 1
        unit = unit_ref[block]
        reach = jnp.full((BLOCK, 1), length_ref[block * seqs])
        pooled_grad = jnp.where(row == 0, grad_rows_ref[pl.ds(block * seqs, 1), :], 0.0)
        for seq in range(1, seqs):
            reach = jnp.where(row >= seq * L, length_ref[block * seqs + seq] + seq * L, reach)
            pooled_grad = jnp.where(row == seq * L, grad_rows_ref[pl.ds(block * seqs + seq, 1), :], pooled_grad)
        output = unit * gains_ref[4:5] + gains_ref[5:6]
        gap = jnp.where(row < reach, output - teacher_ref[...].astype(jnp.float32), 0.0)
        grad_second, gain, shift = norm_backward(2.0 * gap + pooled_grad, unit, inverse_ref[block], gains_ref[4:5])
        grad_feed = grad_second.astype(low)
        grad_feed_ref[...] = grad_feed
        for at in range(0, FF, FFN_CHUNK):
            columns = slice(at, at + FFN_CHUNK)
            grad_hidden = dot_nt(grad_feed, weights_ref[columns, MODEL_WIDTH:])
            grad_before_ref[:, columns] = (grad_hidden * slope_ref[block, :, columns].astype(jnp.float32)).astype(low)
        grad_middle_ref[...] = grad_second + dot_nn(grad_before_ref[...], weights_ref[:, :MODEL_WIDTH])
        for place, value in enumerate((gain, shift, jnp.sum(gap * gap, axis=0))):
            sums_ref[place : place + 1] += value[None]


def ffn_layer(scalars, first, teacher, dense_full, class_wide, logits_wide, norm_gains, neuron_index, pieces):
    rows = first.shape[0]
    seqs = rows // L
    blocks = rows // BLOCK
    low = jnp.bfloat16
    sizes = tuple(piece.shape[0] for piece in pieces)

    def going(width):
        return pl.BlockSpec((BLOCK, width), lambda step: (jnp.minimum(step, blocks - 1), 0))

    def coming(width):
        return pl.BlockSpec((BLOCK, width), lambda step: (jnp.maximum(step - blocks - 1, 0), 0))

    return pl.pallas_call(
        lambda *refs: ffn_kernel(sizes, *refs),
        grid=(2 * blocks + 1,),
        in_specs=[
            pl.BlockSpec(memory_space=pltpu.SMEM),
            pl.BlockSpec(memory_space=pltpu.SMEM),
            going(MODEL_WIDTH),
            coming(MODEL_WIDTH),
            pl.BlockSpec((MODEL_WIDTH, MODEL_WIDTH), lambda step: (4, 0)),
            whole(class_wide.shape),
            whole(logits_wide.shape),
            whole((6, MODEL_WIDTH)),
            whole((1, FF)),
        ]
        + [pl.BlockSpec(memory_space=pl.ANY)] * len(sizes),
        out_specs=[
            going(FF),
            coming(FF),
            coming(MODEL_WIDTH),
            going(MODEL_WIDTH),
            coming(MODEL_WIDTH),
            whole((MODEL_WIDTH, MODEL_WIDTH)),
            whole((8, MODEL_WIDTH)),
            whole((8, MODEL_WIDTH)),
        ],
        out_shape=[
            jax.ShapeDtypeStruct((rows, FF), low),
            jax.ShapeDtypeStruct((rows, FF), low),
            jax.ShapeDtypeStruct((rows, MODEL_WIDTH), low),
            jax.ShapeDtypeStruct((rows, MODEL_WIDTH), low),
            jax.ShapeDtypeStruct((rows, MODEL_WIDTH), jnp.float32),
            jax.ShapeDtypeStruct((MODEL_WIDTH, MODEL_WIDTH), low),
            jax.ShapeDtypeStruct((8, MODEL_WIDTH), jnp.float32),
            jax.ShapeDtypeStruct((8, MODEL_WIDTH), jnp.float32),
        ],
        scratch_shapes=[
            pltpu.VMEM((FF, 2 * MODEL_WIDTH), low),
            pltpu.VMEM((blocks, BLOCK, FF), low),
            pltpu.VMEM((blocks, BLOCK, MODEL_WIDTH), jnp.float32),
            pltpu.VMEM((blocks, BLOCK, 1), jnp.float32),
            pltpu.VMEM((seqs, MODEL_WIDTH), jnp.float32),
            pltpu.VMEM((seqs, MODEL_WIDTH), jnp.float32),
            pltpu.SemaphoreType.DMA((len(sizes),)),
        ],
        compiler_params=pltpu.CompilerParams(vmem_limit_bytes=VMEM_BYTES),
        cost_estimate=pl.CostEstimate(
            flops=rows * MODEL_WIDTH * FF * 16, bytes_accessed=rows * FF * 8, transcendentals=rows * FF
        ),
        name="ffn_layer",
    )(*scalars, first, teacher, dense_full, class_wide, logits_wide, norm_gains, neuron_index, *pieces)


def per_device(
    token_ids,
    replacements,
    replaced,
    lengths,
    widths,
    teacher_embed,
    teacher_hidden,
    teacher_logits,
    embed_table,
    embed_moment,
    embed_square,
    dense_weights,
    dense_moment,
    dense_square,
    feedforward,
    feedforward_moment,
    feedforward_square,
    classifier,
    classifier_moment,
    classifier_square,
    norm_gains,
    norm_moment,
    norm_square,
):
    both = ("dp", "mp")
    mp_count = lax.axis_size("mp")
    mp_index = lax.axis_index("mp")
    n_dev = lax.axis_size("dp") * mp_count
    own_seqs = teacher_logits.shape[0]
    own_rows = own_seqs * L
    table_rows = embed_table.shape[0]
    low = jnp.bfloat16
    by_bits = lax.axis_size("dp") == 8 and mp_count & (mp_count - 1) == 0
    if by_bits:
        dense_steps = gather_mp(dense_weights.astype(low))
        dense_column = jnp.concatenate(
            [lax.select_n(mp_index, *[dense_steps[k ^ z] for z in range(mp_count)]) for k in range(mp_count)],
            axis=0,
        )
    else:
        dense_column = lax.all_gather(dense_weights.astype(low), "mp", axis=0, tiled=True)
    dp_index = lax.axis_index("dp")
    neuron_piece = feedforward.shape[0]
    neuron_slot = jnp.arange(FF)
    if by_bits:
        chunk = neuron_piece * mp_count
        codes = jnp.repeat(jnp.array(piece_codes), chunk, total_repeat_length=FF)
        steps = neuron_slot % chunk // neuron_piece
        neuron_index = (dp_index ^ codes) * chunk + (mp_index ^ steps) * neuron_piece + neuron_slot % neuron_piece
    else:
        neuron_index = neuron_slot

    depth = -(-(own_rows * 3 // 2) // (n_dev * 16)) * 16
    capacity = depth - 1
    own_start = mp_index * own_seqs
    own_ids = lax.dynamic_slice_in_dim(
        jnp.where(replaced == 1, replacements, token_ids), own_start, own_seqs
    ).reshape(own_rows)
    owner = own_ids // table_rows
    local = own_ids - owner * table_rows
    place = jnp.arange(own_rows)
    first = jnp.min(
        jnp.where(own_ids[:, None] == own_ids[None, :], place[None, :], own_rows), axis=1
    )
    leads = first == place
    slot = jnp.sum(
        (leads[None, :] & (owner[:, None] == owner[None, :]) & (place[None, :] < first[:, None])).astype(
            jnp.int32
        ),
        axis=1,
    )
    deepest = jnp.max(slot)

    def positions(turn):
        rank = slot - turn * capacity
        return jnp.where((rank >= 0) & (rank < capacity), owner * depth + rank, -1)

    def wanted(turn):
        spot = jnp.where(leads, positions(turn), -1)
        hits = spot[:, None] == jnp.arange(n_dev * depth)[None, :]
        rows = jnp.max(jnp.where(hits, local[:, None], -1), axis=0).reshape(n_dev, depth)
        return jnp.where(jnp.arange(depth)[None, :] == capacity, deepest, rows)

    def exchange(blocks):
        return lax.all_to_all(blocks, both, split_axis=0, concat_axis=0)

    def asked_hot(asked):
        flat = jnp.where(jnp.arange(depth)[None, :] < capacity, asked, -1).reshape(-1)
        return (flat[:, None] == jnp.arange(table_rows)[None, :]).astype(low)

    def own_hot(turn):
        return (positions(turn)[:, None] == jnp.arange(n_dev * depth)[None, :]).astype(low)

    def answer(asked, table):
        rows = jnp.dot(asked_hot(asked), table.astype(low), preferred_element_type=low)
        return rows.reshape(n_dev, depth, MODEL_WIDTH)

    def place_rows(turn, rows):
        return jnp.dot(own_hot(turn), rows.reshape(-1, MODEL_WIDTH), preferred_element_type=low)

    own_lengths = lax.dynamic_slice_in_dim(lengths, own_start, own_seqs)
    own_levels = lax.dynamic_slice_in_dim(widths, own_start, own_seqs)
    asked_first = exchange(wanted(0))
    ffn_low = feedforward.astype(low)
    if by_bits:
        dense_column, ffn_low = together(dense_column, ffn_low)
        dense_near = gather_near(dense_column)
        ffn_column = jnp.concatenate(gather_mp(ffn_low), axis=0)
        dense_far = far_blocks(*dense_near[1:])
        rows_first, ffn_column, *dense_blocks = together(
            answer(asked_first, embed_table), ffn_column, *dense_near, *dense_far
        )
    else:
        rows_first = answer(asked_first, embed_table)
    turns = jnp.max(asked_first[:, capacity]) // capacity + 1
    extra_rows = lax.while_loop(
        lambda state: state[0] < turns,
        lambda state: (
            state[0] + 1,
            state[1] + place_rows(state[0], exchange(answer(exchange(wanted(state[0])), embed_table))),
        ),
        (jnp.int32(1), jnp.zeros((own_rows, MODEL_WIDTH), low)),
    )[1]
    rows_first, extra_rows = together(rows_first, extra_rows)
    rows_first = exchange(rows_first)
    if by_bits:
        dense_full = assemble(dp_index, all_blocks(*dense_blocks))
        half = ffn_column.shape[0] // 2
        top, rest = ffn_column[:half], ffn_column[half:]
        x_top, y_rest = flip(top, 2), flip(rest, 4)
        x_rest, y_top = flip(rest, 2), flip(top, 4)
        own_lengths, own_levels, dense_full, *near = together(
            own_lengths, own_levels, dense_full, top, rest, x_top, x_rest, y_top, y_rest
        )
        far = flip(near[2], 4), flip(near[5], 2)
        near = near + [flip(block, 1) for block in near]
    else:
        dense_full = lax.all_gather(dense_column, "dp", axis=0, tiled=True)
        ffn_column = lax.all_gather(ffn_low, "mp", axis=0, tiled=True)
        ffn_pieces = [lax.all_gather(ffn_column, "dp", axis=0, tiled=True)]
    embedded_low = place_rows(0, rows_first) + extra_rows

    scalars = (own_lengths, own_levels)
    blocks = own_rows // BLOCK
    if by_bits:
        layer = attention_layer(0, blocks, scalars, embedded_low, dense_full, norm_gains, ())
        flow = together(*layer, *near, *far)
        layer, near, far = flow[:4], flow[4:16], flow[16:]
        far = [*far, flip(far[0], 1), flip(far[1], 1)]
        ffn_pieces = [*near[:4], *far[:2], *near[4:10], *far[2:], *near[10:]]
    else:
        layer = attention_layer(0, blocks, scalars, embedded_low, dense_full, norm_gains, ())
    project, head_mixture, first_sum, normed_low = layer
    class_pad = -classifier.shape[1] % 128
    hidden_low, grad_before, grad_feed_low, middle_low, grad_middle, grad_pool_rows, grad_class, ffn_sums = ffn_layer(
        scalars,
        first_sum,
        teacher_hidden.reshape(own_rows, MODEL_WIDTH),
        dense_full,
        jnp.pad(classifier, ((0, 0), (0, class_pad))).astype(low),
        jnp.pad(teacher_logits, ((0, 0), (0, class_pad))),
        norm_gains,
        neuron_index[None, :],
        ffn_pieces,
    )
    grad_class = grad_class[: classifier.shape[1]]

    def over_both(rows):
        rows = lax.psum_scatter(rows, "dp", scatter_dimension=0, tiled=True)
        return lax.psum_scatter(rows, "mp", scatter_dimension=0, tiled=True).astype(jnp.float32)

    def weight_sums(left, right):
        half = left.shape[1] // 2
        given = flip(contract_first(left[:, half:], right).astype(low), 1)
        return contract_first(left[:, :half], right).astype(low), given

    def by_core(rows):
        chunks = rows.reshape(4, 2, rows.shape[0] // 8, rows.shape[1])
        core = dp_index % 2
        return [lax.dynamic_index_in_dim(chunks, side, 1, keepdims=False) for side in (core, 1 - core)]

    def dense_scatter(own, other):
        place = dp_index // 2
        half = own.shape[1] // 2
        terms = own, flip(other, 1)

        def blocks_from(start):
            def blocks(first, last):
                codes = (0, 1, 3, 2)[first:last]
                picked = [
                    [lax.dynamic_index_in_dim(term, place ^ code, 0, keepdims=False) for code in codes] for term in terms
                ]
                return [
                    jnp.concatenate([block[start : start + half] for block in term], axis=0) for term in picked
                ]

            return blocks

        halves = blocks_from(0), blocks_from(half)
        parts = send_last(*halves, *send_first(*halves))
        parts = jnp.concatenate(parts, axis=0).reshape(mp_count, -1, MODEL_WIDTH)
        parts = [lax.dynamic_index_in_dim(parts, mp_index ^ step, 0, keepdims=False) for step in range(mp_count)]
        return [parts[0]] + [pass_mp(parts[step], step) for step in range(1, mp_count)]

    arrays = [
        grad_middle,
        first_sum,
        project,
        embedded_low,
        teacher_embed.reshape(own_rows, MODEL_WIDTH),
    ]
    weights = (dense_full, dense_full, norm_gains)
    if by_bits:
        down_own, down_given = weight_sums(hidden_low, grad_feed_low)
        up_own, up_given = weight_sums(grad_before, middle_low)
        arrays[0], *parts = together(arrays[0], up_own, up_given, down_own, down_given)
        halves = blocks_of(*parts[:2]), blocks_of(*parts[2:])
        parts = send_first(*halves)
        before = attention_backward(0, blocks - 1, scalars, arrays, weights, ())
        arrays[0], *flow = together(arrays[0], *before, *parts)
        *before, sums_one = flow[:4]
        parts = send_last(*halves, *flow[4:])
        before = attention_backward(blocks - 1, 1, scalars, arrays, weights, before)
        flow = together(*before, *parts)
        *before, sums_last = flow[:4]
        parts = [part.reshape(mp_count, neuron_piece, MODEL_WIDTH) for part in flow[4:]]
        ffn_parts = [jnp.concatenate([part[step] for part in parts], axis=1) for step in range(mp_count)]
        ffn_parts = [ffn_parts[0]] + [pass_mp(ffn_parts[step], step) for step in range(1, mp_count)]
        sums = sums_one + sums_last
    else:
        ffn_grad = jnp.concatenate(
            [contract_first(grad_before, middle_low), contract_first(hidden_low, grad_feed_low)], axis=1
        ).astype(low)
        ffn_grad = over_both(ffn_grad)
        *before, sums = attention_backward(0, blocks, scalars, arrays, weights, ())
    grad_project, grad_att_low, grad_embed_low = before
    grad_dense = jnp.concatenate(
        [
            contract_first(grad_project, normed_low).astype(low),
            contract_first(head_mixture, grad_att_low).astype(low),
            grad_pool_rows,
        ],
        axis=0,
    )

    small = jnp.concatenate([sums[:4], ffn_sums[:2], grad_class], axis=0)
    small_rows = small.shape[0]
    upper = lax.reduce_precision(small, 8, 7)
    rider = jnp.concatenate([upper, small - upper], axis=0).astype(low)
    rider = jnp.pad(rider, ((0, n_dev - 2 * small_rows), (0, 0)))

    def give_back(turn, rider):
        return give_rows(positions(turn), grad_embed_low, rider, depth).reshape(n_dev, depth, MODEL_WIDTH)

    def collect(asked, returned):
        ids = jnp.where(jnp.arange(depth)[None, :] < capacity, asked, -1).reshape(-1)
        return collect_rows(ids, returned.reshape(-1, MODEL_WIDTH), table_rows)

    def collect_more(state):
        turn, total, _ = state
        total = total + collect(exchange(wanted(turn)), exchange(give_back(turn, jnp.zeros_like(rider))))[0]
        return turn + 1, total, jnp.zeros((8, MODEL_WIDTH)).at[0].set(jnp.sum(total * total, axis=0))

    given = give_back(0, rider)
    if by_bits:
        given, *flow = together(given, *by_core(grad_dense), *ffn_parts)
        grad_dense, ffn_parts = flow[:2], flow[2:]
        ffn_grad = sum(part.astype(jnp.float32) for part in ffn_parts)
    returned = exchange(given)
    dense_parts = dense_scatter(*grad_dense) if by_bits else [over_both(grad_dense)]
    table_sums = collect(asked_first, returned)
    *table_sums, returned = together(*table_sums, returned)
    *table_sums, dense_first = together(*table_sums, dense_parts[0])
    dense_parts = together(*dense_parts[1:], dense_first)
    dense_grad = sum(part.astype(jnp.float32) for part in dense_parts)
    _, table_grad, table_squares = lax.while_loop(
        lambda state: state[0] < turns, collect_more, (jnp.int32(1), *table_sums)
    )
    small_row = jnp.sum(returned[:, capacity].astype(jnp.float32), axis=0)

    def folded(row):
        return sum(row[:, at : at + 128] for at in range(0, MODEL_WIDTH, 128))

    ffn_squares = jnp.sum(ffn_grad * ffn_grad, axis=0, keepdims=True)
    squares = table_squares[:1] + jnp.sum(dense_grad * dense_grad, axis=0, keepdims=True)
    squares = squares + ffn_squares[:, :MODEL_WIDTH] + ffn_squares[:, MODEL_WIDTH:]
    losses = sums[4:5] + ffn_sums[2:3] + ffn_sums[3:4]
    count_row = jnp.pad(own_lengths.astype(jnp.float32), (0, 128 - own_seqs))[None]
    message = jnp.concatenate([small_row[None], folded(squares), folded(losses), count_row], axis=1)
    told = exchange(jnp.broadcast_to(message, (n_dev, message.shape[1])))
    scalars = jnp.sum(told[:, MODEL_WIDTH:], axis=0, keepdims=True)
    total_square, loss_sum, token_count = [
        jnp.sum(scalars[:, at : at + 128], axis=1, keepdims=True) for at in (0, 128, 256)
    ]
    small = told[:small_rows, :MODEL_WIDTH] + told[small_rows : 2 * small_rows, :MODEL_WIDTH]
    total_square = total_square + jnp.sum(jnp.sum(small * small, axis=0, keepdims=True), axis=1, keepdims=True)
    gains_grad, class_grad = small[:6], small[6:].T
    inverse = 1.0 / token_count
    grad_norm = jnp.sqrt(total_square) * inverse
    scaling = inverse * (clip_bound / jnp.maximum(grad_norm, clip_bound))
    table_new = adam_update(
        embed_table, table_grad * scaling, embed_moment, embed_square, weight_decay, learn_rate
    )
    dense_new = adam_update(
        dense_weights, dense_grad * scaling, dense_moment, dense_square, weight_decay, learn_rate
    )
    ffn_new = adam_update(
        feedforward,
        ffn_grad * scaling,
        feedforward_moment,
        feedforward_square,
        weight_decay,
        learn_rate,
    )
    class_new = adam_update(
        classifier,
        class_grad * scaling,
        classifier_moment,
        classifier_square,
        weight_decay,
        learn_rate,
    )
    gains_new = adam_update(
        norm_gains, gains_grad * scaling, norm_moment, norm_square, 0.0, gain_rate
    )
    return (
        loss_sum.reshape(()),
        token_count.reshape(()),
        grad_norm.reshape(()),
        table_new[0],
        table_new[1],
        table_new[2],
        table_new[0].astype(jnp.bfloat16),
        dense_new[0],
        dense_new[1],
        dense_new[2],
        dense_new[0].astype(jnp.bfloat16),
        ffn_new[0],
        ffn_new[1],
        ffn_new[2],
        ffn_new[0].astype(jnp.bfloat16),
        class_new[0],
        class_new[1],
        class_new[2],
        class_new[0].astype(jnp.bfloat16),
        gains_new[0],
        gains_new[1],
        gains_new[2],
    )


def solution(mesh):
    placed = (
        P("dp", None),
        P("dp", None),
        P("dp", None),
        P("dp"),
        P("dp"),
        P(("dp", "mp"), None, None),
        P(("dp", "mp"), None, None),
        P(("dp", "mp"), None),
        P(("dp", "mp"), None),
        P(("dp", "mp"), None),
        P(("dp", "mp"), None),
        P(("dp", "mp"), None),
        P(("dp", "mp"), None),
        P(("dp", "mp"), None),
        P(("dp", "mp"), None),
        P(("dp", "mp"), None),
        P(("dp", "mp"), None),
        P(),
        P(),
        P(),
        P(),
        P(),
        P(),
    )
    return jax.shard_map(
        per_device,
        mesh=mesh,
        in_specs=placed,
        out_specs=(
            P(),
            P(),
            P(),
            P(("dp", "mp"), None),
            P(("dp", "mp"), None),
            P(("dp", "mp"), None),
            P(("dp", "mp"), None),
            P(("dp", "mp"), None),
            P(("dp", "mp"), None),
            P(("dp", "mp"), None),
            P(("dp", "mp"), None),
            P(("dp", "mp"), None),
            P(("dp", "mp"), None),
            P(("dp", "mp"), None),
            P(("dp", "mp"), None),
            P(),
            P(),
            P(),
            P(),
            P(),
            P(),
            P(),
        ),
        check_vma=False,
    )
```

```python
import jax
import jax.numpy as jnp
from jax import lax
from jax.experimental import pallas as pl
from jax.experimental.pallas import tpu as pltpu
from jax.sharding import PartitionSpec as P

MODEL_WIDTH = 768
HEADS = 12
FF = 3072
L = 128
LEVELS = 4
STEP = 10


highest_precision = lax.Precision.HIGHEST
norm_epsilon = 1e-05
learn_rate = 0.05
gain_rate = 0.5
beta_one = 0.9
beta_two = 0.999
adam_epsilon = 1e-08
weight_decay = 0.01
clip_bound = 1.0


def norm_forward(values, gain_row, shift_row):
    center = values - jnp.mean(values, axis=-1, keepdims=True)
    spread = jnp.mean(center * center, axis=-1, keepdims=True)
    inverse = lax.rsqrt(spread + norm_epsilon)
    unit = center * inverse
    return (unit * gain_row + shift_row, unit, inverse)


def norm_backward(grad, unit, inverse, gain_row):
    scaled = grad * gain_row
    level = jnp.mean(scaled, axis=-1, keepdims=True)
    along = jnp.mean(scaled * unit, axis=-1, keepdims=True)
    grad_values = inverse * (scaled - level - unit * along)
    return (grad_values, jnp.sum(grad * unit, axis=0), jnp.sum(grad, axis=0))


gelu_rate = 0.7978845608028654
gelu_cube = 0.044715


def gelu_forward(before):
    bend = jnp.tanh(gelu_rate * (before + gelu_cube * before * before * before))
    return 0.5 * before * (1.0 + bend)


def gelu_slope(before):
    bend = jnp.tanh(gelu_rate * (before + gelu_cube * before * before * before))
    inner = gelu_rate * (1.0 + 3.0 * gelu_cube * before * before)
    return 0.5 * (1.0 + bend) + 0.5 * before * (1.0 - bend * bend) * inner


def adam_update(weight, gradient, first_moment, second, decay_rate, rate):
    first_new = beta_one * first_moment + (1.0 - beta_one) * gradient
    second_new = beta_two * second + (1.0 - beta_two) * gradient * gradient
    direction = (
        first_new
        / (1.0 - beta_one**STEP)
        / (jnp.sqrt(second_new / (1.0 - beta_two**STEP)) + adam_epsilon)
    )
    return (weight - rate * (direction + decay_rate * weight), first_new, second_new)


def contract_last(left, right):
    return lax.dot_general(
        left, right, (((1,), (1,)), ((), ())), preferred_element_type=jnp.float32
    )


def contract_first(left, right):
    return lax.dot_general(
        left, right, (((0,), (0,)), ((), ())), preferred_element_type=jnp.float32
    )


def flip(block, bit):
    size = lax.axis_size("dp")
    return lax.ppermute(block, "dp", [(i, i ^ bit) for i in range(size)])


def add_low(*terms):
    return sum(term.astype(jnp.float32) for term in terms).astype(jnp.bfloat16)


piece_codes = (0, 2, 6, 4, 1, 3, 7, 5)


def gather_near(own):
    return own, flip(own, 2), flip(own, 4)


def far_blocks(along_x, along_y):
    half = along_x.shape[0] // 2
    return flip(along_x[:half], 4), flip(along_y[half:], 2)


def all_blocks(own, along_x, along_y, far_top, far_low):
    mine = [own, along_x, far_top, far_low, along_y]
    return mine + [flip(block, 1) for block in mine]


def assemble_kernel(place_ref, *refs):
    pieces, full_ref, arrivals = refs[:10], refs[10], refs[11]
    chunk = pieces[0].shape[0]
    copies = []
    for block, piece in enumerate(pieces):
        code = (0, 2, 6, 6, 4)[block % 5] + block // 5
        at = (place_ref[0] ^ code) * chunk
        if block % 5 == 3:
            at = at + chunk // 2
        at = pl.multiple_of(at, 16)
        copies.append(
            pltpu.make_async_copy(piece, full_ref.at[pl.ds(at, piece.shape[0])], arrivals.at[block])
        )
    for copy in copies:
        copy.start()
    for copy in copies:
        copy.wait()


def assemble(place, pieces):
    chunk, width = pieces[0].shape
    return pl.pallas_call(
        assemble_kernel,
        in_specs=[pl.BlockSpec(memory_space=pltpu.SMEM)] + [pl.BlockSpec(memory_space=pl.ANY)] * len(pieces),
        out_specs=pl.BlockSpec(memory_space=pltpu.VMEM),
        out_shape=jax.ShapeDtypeStruct((8 * chunk, width), pieces[0].dtype),
        compiler_params=pltpu.CompilerParams(vmem_limit_bytes=VMEM_BYTES),
        scratch_shapes=[pltpu.SemaphoreType.DMA((len(pieces),))],
        cost_estimate=pl.CostEstimate(flops=0, bytes_accessed=32 * chunk * width, transcendentals=0),
        name="assemble",
    )(place.reshape(1), *pieces)


def partner(index, step):
    size = lax.axis_size("mp")
    return index ^ step if size & (size - 1) == 0 else (index + step) % size


def pass_mp(block, step):
    return lax.ppermute(block, "mp", [(i, partner(i, step)) for i in range(lax.axis_size("mp"))])


def gather_mp(rows):
    return [rows] + [pass_mp(rows, step) for step in range(1, lax.axis_size("mp"))]


def send_first(top, rest):
    from_x = flip(add_low(*top(1, 3)), 2)
    from_y = flip(add_low(*rest(2, 4)), 4)
    size = from_x.shape[0] // 2
    late_y = add_low(*top(3, 4), from_x[size:])
    late_x = add_low(*rest(1, 2), from_y[:size])
    return together(late_y, late_x, from_x, from_y)


def send_last(top, rest, late_y, late_x, from_x, from_y):
    size = late_y.shape[0]
    late_y, late_x = flip(late_y, 4), flip(late_x, 2)
    return add_low(*top(0, 1), from_x[:size], late_y), add_low(*rest(0, 1), from_y[size:], late_x)


def blocks_of(*terms):
    size = terms[0].shape[0] // 4
    return lambda first, last: [term[first * size : last * size] for term in terms]


def together(*values):
    return lax.optimization_barrier(values)


PAIR = 2 * (MODEL_WIDTH // HEADS)
PAIRS = HEADS // 2
BLOCK = 2 * L
VMEM_BYTES = 56 * 1024 * 1024


def dot_nt(left, right):
    return lax.dot_general(
        left, right, (((1,), (1,)), ((), ())), preferred_element_type=jnp.float32
    )


def dot_tn(left, right):
    return lax.dot_general(
        left, right, (((0,), (0,)), ((), ())), preferred_element_type=jnp.float32
    )


def dot_nn(left, right):
    return jnp.dot(left, right, preferred_element_type=jnp.float32)


def both_heads(pair, left_half):
    zero = jnp.zeros_like(pair)
    return jnp.concatenate([jnp.where(left_half, pair, zero), jnp.where(left_half, zero, pair)], axis=0)


def pair_attend(queries, keys, key_bias):
    scores = dot_nt(queries, keys) * (MODEL_WIDTH // HEADS) ** (-0.5) + key_bias
    raised = jnp.exp(scores - jnp.max(scores, axis=-1, keepdims=True))
    return raised * (1.0 / jnp.sum(raised, axis=-1, keepdims=True))


def attention_kernel(
    start, length_ref, level_ref, embed_ref, qkv_ref, out_ref, gains_ref, project_ref, mixture_ref, first_ref, normed_ref
):
    step = pl.program_id(0) + start
    normed, _, _ = norm_forward(embed_ref[...].astype(jnp.float32), gains_ref[0:1], gains_ref[1:2])
    normed_low = normed.astype(jnp.bfloat16)
    normed_ref[...] = normed_low
    for part in range(3):
        columns = slice(part * MODEL_WIDTH, (part + 1) * MODEL_WIDTH)
        project_ref[:, columns] = dot_nt(normed_low, qkv_ref[columns]).astype(jnp.bfloat16)
    lane = lax.broadcasted_iota(jnp.int32, (L, PAIR), 1)
    left_half = lane < PAIR // 2
    for seq in range(BLOCK // L):
        rows = slice(seq * L, (seq + 1) * L)
        length = length_ref[step * (BLOCK // L) + seq]
        heads = level_ref[step * (BLOCK // L) + seq] * (HEADS // LEVELS)
        key_bias = jnp.where(lax.broadcasted_iota(jnp.int32, (1, L), 1) < length, 0.0, -1000000000.0)
        for pair in range(PAIRS):
            at = pair * PAIR
            queries = both_heads(project_ref[rows, at : at + PAIR], left_half)
            keys = project_ref[rows, MODEL_WIDTH + at : MODEL_WIDTH + at + PAIR]
            values = project_ref[rows, 2 * MODEL_WIDTH + at : 2 * MODEL_WIDTH + at + PAIR]
            attend = pair_attend(queries, keys, key_bias).astype(jnp.bfloat16)
            mixed = dot_nn(attend, values)
            mixed = jnp.where(left_half, mixed[:L], mixed[L:])
            head = 2 * pair + (lane >= PAIR // 2).astype(jnp.int32)
            mixture_ref[rows, at : at + PAIR] = jnp.where(head < heads, mixed, 0.0).astype(jnp.bfloat16)
    first_ref[...] = normed + dot_nn(mixture_ref[...], out_ref[...])


def whole(shape):
    return pl.BlockSpec(shape, lambda step: (0,) * len(shape))


def by_rows(width):
    return pl.BlockSpec((BLOCK, width), lambda step: (step, 0))


def attention_layer(start, steps, scalars, embedded, dense_full, norm_gains, before):
    rows = embedded.shape[0]
    low = jnp.bfloat16
    count = len(before)

    def at_rows(width):
        return pl.BlockSpec((BLOCK, width), lambda step: (step + start, 0))

    def body(length_ref, level_ref, *refs):
        attention_kernel(start, length_ref, level_ref, *refs[:4], *refs[4 + count :])

    return pl.pallas_call(
        body,
        grid=(steps,),
        in_specs=[
            pl.BlockSpec(memory_space=pltpu.SMEM),
            pl.BlockSpec(memory_space=pltpu.SMEM),
            at_rows(MODEL_WIDTH),
            whole((3 * MODEL_WIDTH, MODEL_WIDTH)),
            pl.BlockSpec((MODEL_WIDTH, MODEL_WIDTH), lambda step: (3, 0)),
            whole((6, MODEL_WIDTH)),
        ]
        + [pl.BlockSpec(memory_space=pl.ANY)] * count,
        out_specs=[at_rows(3 * MODEL_WIDTH), at_rows(MODEL_WIDTH), at_rows(MODEL_WIDTH), at_rows(MODEL_WIDTH)],
        out_shape=[
            jax.ShapeDtypeStruct((rows, 3 * MODEL_WIDTH), low),
            jax.ShapeDtypeStruct((rows, MODEL_WIDTH), low),
            jax.ShapeDtypeStruct((rows, MODEL_WIDTH), jnp.float32),
            jax.ShapeDtypeStruct((rows, MODEL_WIDTH), low),
        ],
        input_output_aliases={6 + place: place for place in range(count)},
        compiler_params=pltpu.CompilerParams(vmem_limit_bytes=VMEM_BYTES),
        cost_estimate=pl.CostEstimate(
            flops=steps * BLOCK * MODEL_WIDTH * MODEL_WIDTH * 20,
            bytes_accessed=steps * BLOCK * MODEL_WIDTH * 16,
            transcendentals=0,
        ),
        name="attention_layer",
    )(*scalars, embedded, dense_full, dense_full, norm_gains, *before)


def give_kernel(depth, spots_ref, grad_ref, rider_ref, sums_ref):
    rows = sums_ref.shape[0]
    row = pl.program_id(0) * rows + lax.broadcasted_iota(jnp.int32, (rows, 1), 0)
    last = lax.broadcasted_iota(jnp.int32, (1, rider_ref.shape[0]), 1) * depth + depth - 1
    own = (row == spots_ref[...]).astype(jnp.float32).astype(jnp.bfloat16)
    ride = (row == last).astype(jnp.float32).astype(jnp.bfloat16)
    sums_ref[...] = (dot_nn(own, grad_ref[...]) + dot_nn(ride, rider_ref[...])).astype(jnp.bfloat16)


def give_rows(spots, grads, rider, depth):
    total = rider.shape[0] * depth
    size = 512 if total % 512 == 0 else total
    return pl.pallas_call(
        lambda *refs: give_kernel(depth, *refs),
        grid=(total // size,),
        in_specs=[whole((1, spots.shape[0])), whole(grads.shape), whole(rider.shape)],
        out_specs=pl.BlockSpec((size, MODEL_WIDTH), lambda step: (step, 0)),
        out_shape=jax.ShapeDtypeStruct((total, MODEL_WIDTH), jnp.bfloat16),
        compiler_params=pltpu.CompilerParams(vmem_limit_bytes=VMEM_BYTES),
        cost_estimate=pl.CostEstimate(
            flops=2 * total * spots.shape[0] * MODEL_WIDTH, bytes_accessed=4 * total * MODEL_WIDTH, transcendentals=0
        ),
        name="give_rows",
    )(spots[None, :], grads, rider)


def collect_kernel(ids_ref, returned_ref, sums_ref, squares_ref):
    step = pl.program_id(0)
    rows = sums_ref.shape[0]
    row = step * rows + lax.broadcasted_iota(jnp.int32, (rows, 1), 0)
    hot = (row == ids_ref[...]).astype(jnp.float32).astype(jnp.bfloat16)
    sums = dot_nn(hot, returned_ref[...])
    sums_ref[...] = sums

    @pl.when(step == 0)
    def _():
        squares_ref[...] = jnp.zeros_like(squares_ref)

    squares_ref[0:1] += jnp.sum(sums * sums, axis=0, keepdims=True)


def collect_rows(ids, returned, table_rows):
    size = 240
    return pl.pallas_call(
        collect_kernel,
        grid=(-(-table_rows // size),),
        in_specs=[whole((1, ids.shape[0])), whole(returned.shape)],
        out_specs=[pl.BlockSpec((size, MODEL_WIDTH), lambda step: (step, 0)), whole((8, MODEL_WIDTH))],
        out_shape=[
            jax.ShapeDtypeStruct((table_rows, MODEL_WIDTH), jnp.float32),
            jax.ShapeDtypeStruct((8, MODEL_WIDTH), jnp.float32),
        ],
        compiler_params=pltpu.CompilerParams(vmem_limit_bytes=VMEM_BYTES),
        cost_estimate=pl.CostEstimate(
            flops=2 * table_rows * ids.shape[0] * MODEL_WIDTH, bytes_accessed=8 * table_rows * MODEL_WIDTH, transcendentals=0
        ),
        name="collect_rows",
    )(ids[None, :], returned)


def attention_back_kernel(
    start,
    length_ref,
    level_ref,
    grad_ref,
    first_ref,
    project_ref,
    embed_ref,
    teacher_ref,
    qkv_ref,
    out_ref,
    gains_ref,
    grad_project_ref,
    grad_att_ref,
    grad_embed_ref,
    sums_ref,
    grad_mixture_ref,
):
    turn = pl.program_id(0)
    step = turn + start
    low = jnp.bfloat16
    _, unit_one, inverse_one = norm_forward(first_ref[...], gains_ref[2:3], gains_ref[3:4])
    grad_first, gain_one, shift_one = norm_backward(grad_ref[...], unit_one, inverse_one, gains_ref[2:3])
    grad_att = grad_first.astype(low)
    grad_att_ref[...] = grad_att
    grad_mixture_ref[...] = dot_nt(grad_att, out_ref[...]).astype(low)
    lane = lax.broadcasted_iota(jnp.int32, (L, PAIR), 1)
    left_half = lane < PAIR // 2
    scaling = (MODEL_WIDTH // HEADS) ** (-0.5)
    usable = []
    for seq in range(BLOCK // L):
        rows = slice(seq * L, (seq + 1) * L)
        length = length_ref[step * (BLOCK // L) + seq]
        heads = level_ref[step * (BLOCK // L) + seq] * (HEADS // LEVELS)
        usable.append((lax.broadcasted_iota(jnp.int32, (L, 1), 0) < length).astype(jnp.float32))
        key_bias = jnp.where(lax.broadcasted_iota(jnp.int32, (L, 1), 0) < length, 0.0, -1000000000.0)
        for pair in range(PAIRS):
            at = pair * PAIR
            queries = both_heads(project_ref[rows, at : at + PAIR], left_half)
            keys = project_ref[rows, MODEL_WIDTH + at : MODEL_WIDTH + at + PAIR]
            values = project_ref[rows, 2 * MODEL_WIDTH + at : 2 * MODEL_WIDTH + at + PAIR]
            scores = dot_nt(keys, queries) * scaling + key_bias
            raised = jnp.exp(scores - jnp.max(scores, axis=0, keepdims=True))
            attend = raised * (1.0 / jnp.sum(raised, axis=0, keepdims=True))
            head = 2 * pair + (lane >= PAIR // 2).astype(jnp.int32)
            mixture = grad_mixture_ref[rows, at : at + PAIR]
            mixture = both_heads(jnp.where(head < heads, mixture, jnp.zeros_like(mixture)), left_half)
            grad_values = dot_nn(attend.astype(low), mixture)
            grad_attend = dot_nt(values, mixture)
            level = jnp.sum(grad_attend * attend, axis=0, keepdims=True)
            grad_scores = (attend * (grad_attend - level)).astype(low)
            grad_keys = dot_nn(grad_scores, queries) * scaling
            grad_queries = dot_tn(grad_scores, keys) * scaling
            grad_queries = jnp.where(left_half, grad_queries[:L], grad_queries[L:])
            grad_project_ref[rows, at : at + PAIR] = grad_queries.astype(low)
            grad_project_ref[rows, MODEL_WIDTH + at : MODEL_WIDTH + at + PAIR] = grad_keys.astype(low)
            grad_project_ref[rows, 2 * MODEL_WIDTH + at : 2 * MODEL_WIDTH + at + PAIR] = grad_values.astype(low)
    normed, unit_base, inverse_base = norm_forward(
        embed_ref[...].astype(jnp.float32), gains_ref[0:1], gains_ref[1:2]
    )
    usable = jnp.concatenate(usable, axis=0)
    gap = usable * (normed - teacher_ref[...].astype(jnp.float32))
    grad_normed = grad_first + 2.0 * gap + dot_nn(grad_project_ref[...], qkv_ref[...])
    grad_embed, gain_base, shift_base = norm_backward(grad_normed, unit_base, inverse_base, gains_ref[0:1])
    grad_embed_ref[...] = grad_embed.astype(low)

    @pl.when(turn == 0)
    def _():
        sums_ref[...] = jnp.zeros_like(sums_ref)

    for row, value in enumerate((gain_base, shift_base, gain_one, shift_one, jnp.sum(gap * gap, axis=0))):
        sums_ref[row : row + 1] += value[None]


def attention_backward(start, steps, scalars, arrays, weights, before):
    rows = arrays[0].shape[0]
    low = jnp.bfloat16

    def at_rows(width):
        return pl.BlockSpec((BLOCK, width), lambda step: (step + start, 0))

    widths = (MODEL_WIDTH, MODEL_WIDTH, 3 * MODEL_WIDTH, MODEL_WIDTH, MODEL_WIDTH)
    count = len(before)

    def body(length_ref, level_ref, *refs):
        attention_back_kernel(start, length_ref, level_ref, *refs[:8], *refs[8 + count :])

    return pl.pallas_call(
        body,
        grid=(steps,),
        in_specs=[pl.BlockSpec(memory_space=pltpu.SMEM)] * 2
        + [at_rows(width) for width in widths]
        + [
            whole((3 * MODEL_WIDTH, MODEL_WIDTH)),
            pl.BlockSpec((MODEL_WIDTH, MODEL_WIDTH), lambda step: (3, 0)),
            whole((6, MODEL_WIDTH)),
        ]
        + [pl.BlockSpec(memory_space=pl.ANY)] * count,
        out_specs=[at_rows(3 * MODEL_WIDTH), at_rows(MODEL_WIDTH), at_rows(MODEL_WIDTH), whole((8, MODEL_WIDTH))],
        out_shape=[
            jax.ShapeDtypeStruct((rows, 3 * MODEL_WIDTH), low),
            jax.ShapeDtypeStruct((rows, MODEL_WIDTH), low),
            jax.ShapeDtypeStruct((rows, MODEL_WIDTH), low),
            jax.ShapeDtypeStruct((8, MODEL_WIDTH), jnp.float32),
        ],
        input_output_aliases={10 + place: place for place in range(count)},
        scratch_shapes=[pltpu.VMEM((BLOCK, MODEL_WIDTH), low)],
        compiler_params=pltpu.CompilerParams(vmem_limit_bytes=VMEM_BYTES),
        cost_estimate=pl.CostEstimate(
            flops=steps * BLOCK * MODEL_WIDTH * MODEL_WIDTH * 40,
            bytes_accessed=steps * BLOCK * MODEL_WIDTH * 24,
            transcendentals=0,
        ),
        name="attention_backward",
    )(*scalars, *arrays, *weights, *before)


FFN_CHUNK = 768


def split_low(value):
    upper = value.astype(jnp.bfloat16)
    return jnp.concatenate([upper, (value - upper.astype(jnp.float32)).astype(jnp.bfloat16)], axis=0)


def ffn_kernel(sizes, length_ref, level_ref, first_ref, teacher_ref, pool_ref, class_ref, logits_ref, gains_ref, index_ref, *refs):
    pieces = refs[: len(sizes)]
    (hidden_ref, grad_before_ref, grad_feed_ref, middle_ref, grad_middle_ref, grad_pool_ref, grad_class_ref, sums_ref) = refs[
        len(sizes) : len(sizes) + 8
    ]
    weights_ref, slope_ref, unit_ref, inverse_ref, pooled_rows_ref, grad_rows_ref, arrivals = refs[len(sizes) + 8 :]
    step = pl.program_id(0)
    blocks = slope_ref.shape[0]
    seqs = BLOCK // L
    low = jnp.bfloat16
    row = lax.broadcasted_iota(jnp.int32, (BLOCK, 1), 0)

    def copies():
        at = 0
        for place, size in enumerate(sizes):
            yield pltpu.make_async_copy(pieces[place], weights_ref.at[pl.ds(at, size)], arrivals.at[place])
            at += size

    def go(waiting):
        arriving = list(copies()) if waiting else []
        for copy in arriving:
            copy.start()
        if waiting:
            sums_ref[...] = jnp.zeros_like(sums_ref)
        waited, arrived = 0, 0
        middle, _, _ = norm_forward(first_ref[...], gains_ref[2:3], gains_ref[3:4])
        middle_low = middle.astype(low)
        middle_ref[...] = middle_low
        limit = jnp.full((BLOCK, 1), level_ref[step * seqs])
        for seq in range(1, seqs):
            limit = jnp.where(row >= seq * L, level_ref[step * seqs + seq], limit)
        limit = limit * (FF // LEVELS)
        for at in range(0, FF, FFN_CHUNK):
            columns = slice(at, at + FFN_CHUNK)
            while waiting and arrived < at + FFN_CHUNK:
                arriving[waited].wait()
                arrived += sizes[waited]
                waited += 1
            before = dot_nt(middle_low, weights_ref[columns, :MODEL_WIDTH])
            square = before * before
            bend = jnp.tanh(before * (gelu_rate + gelu_rate * gelu_cube * square))
            rise = 0.5 + 0.5 * bend
            value = before * rise
            slope = rise + (0.5 * before) * (1.0 - bend * bend) * (gelu_rate + 3.0 * gelu_rate * gelu_cube * square)
            on = index_ref[:, columns] < limit
            hidden_ref[:, columns] = jnp.where(on, value, 0.0).astype(low)
            slope_ref[step, :, columns] = jnp.where(on, slope, 0.0).astype(low)
        feed = dot_nn(hidden_ref[...], weights_ref[:, MODEL_WIDTH:])
        output, unit, inverse = norm_forward(middle + feed, gains_ref[4:5], gains_ref[5:6])
        unit_ref[step] = unit
        inverse_ref[step] = inverse
        for seq in range(seqs):
            pooled_rows_ref[pl.ds(step * seqs + seq, 1), :] = output[seq * L : seq * L + 1]

    @pl.when(step == 0)
    def _():
        go(True)

    @pl.when((step > 0) & (step < blocks))
    def _():
        go(False)

    @pl.when(step == blocks)
    def _():
        first_low = pooled_rows_ref[...].astype(low)
        pooled = jnp.tanh(dot_nn(first_low, pool_ref[...]))
        pooled_low = pooled.astype(low)
        gap = dot_nn(pooled_low, class_ref[...]) - logits_ref[...]
        grad_logits = split_low(2.0 * L * gap)
        rows = gap.shape[0]
        grad_class = dot_tn(grad_logits, jnp.concatenate([pooled_low, pooled_low], axis=0))
        grad_class_ref[...] = grad_class[: grad_class_ref.shape[0]]
        grad_pooled = dot_nt(grad_logits, class_ref[...])
        grad_inner = split_low((grad_pooled[:rows] + grad_pooled[rows:]) * (1.0 - pooled * pooled))
        grad_pool_ref[...] = dot_tn(jnp.concatenate([first_low, first_low], axis=0), grad_inner).astype(low)
        grad_rows = dot_nt(grad_inner, pool_ref[...])
        grad_rows_ref[...] = grad_rows[:rows] + grad_rows[rows:]
        sums_ref[3:4, : gap.shape[1]] += L * jnp.sum(gap * gap, axis=0, keepdims=True)

    @pl.when(step > blocks)
    def _():
        block = step - blocks - 1
        unit = unit_ref[block]
        reach = jnp.full((BLOCK, 1), length_ref[block * seqs])
        pooled_grad = jnp.where(row == 0, grad_rows_ref[pl.ds(block * seqs, 1), :], 0.0)
        for seq in range(1, seqs):
            reach = jnp.where(row >= seq * L, length_ref[block * seqs + seq] + seq * L, reach)
            pooled_grad = jnp.where(row == seq * L, grad_rows_ref[pl.ds(block * seqs + seq, 1), :], pooled_grad)
        output = unit * gains_ref[4:5] + gains_ref[5:6]
        gap = jnp.where(row < reach, output - teacher_ref[...].astype(jnp.float32), 0.0)
        grad_second, gain, shift = norm_backward(2.0 * gap + pooled_grad, unit, inverse_ref[block], gains_ref[4:5])
        grad_feed = grad_second.astype(low)
        grad_feed_ref[...] = grad_feed
        for at in range(0, FF, FFN_CHUNK):
            columns = slice(at, at + FFN_CHUNK)
            grad_hidden = dot_nt(grad_feed, weights_ref[columns, MODEL_WIDTH:])
            grad_before_ref[:, columns] = (grad_hidden * slope_ref[block, :, columns].astype(jnp.float32)).astype(low)
        grad_middle_ref[...] = grad_second + dot_nn(grad_before_ref[...], weights_ref[:, :MODEL_WIDTH])
        for place, value in enumerate((gain, shift, jnp.sum(gap * gap, axis=0))):
            sums_ref[place : place + 1] += value[None]


def ffn_layer(scalars, first, teacher, dense_full, class_wide, logits_wide, norm_gains, neuron_index, pieces):
    rows = first.shape[0]
    seqs = rows // L
    blocks = rows // BLOCK
    low = jnp.bfloat16
    sizes = tuple(piece.shape[0] for piece in pieces)

    def going(width):
        return pl.BlockSpec((BLOCK, width), lambda step: (jnp.minimum(step, blocks - 1), 0))

    def coming(width):
        return pl.BlockSpec((BLOCK, width), lambda step: (jnp.maximum(step - blocks - 1, 0), 0))

    return pl.pallas_call(
        lambda *refs: ffn_kernel(sizes, *refs),
        grid=(2 * blocks + 1,),
        in_specs=[
            pl.BlockSpec(memory_space=pltpu.SMEM),
            pl.BlockSpec(memory_space=pltpu.SMEM),
            going(MODEL_WIDTH),
            coming(MODEL_WIDTH),
            pl.BlockSpec((MODEL_WIDTH, MODEL_WIDTH), lambda step: (4, 0)),
            whole(class_wide.shape),
            whole(logits_wide.shape),
            whole((6, MODEL_WIDTH)),
            whole((1, FF)),
        ]
        + [pl.BlockSpec(memory_space=pl.ANY)] * len(sizes),
        out_specs=[
            going(FF),
            coming(FF),
            coming(MODEL_WIDTH),
            going(MODEL_WIDTH),
            coming(MODEL_WIDTH),
            whole((MODEL_WIDTH, MODEL_WIDTH)),
            whole((8, MODEL_WIDTH)),
            whole((8, MODEL_WIDTH)),
        ],
        out_shape=[
            jax.ShapeDtypeStruct((rows, FF), low),
            jax.ShapeDtypeStruct((rows, FF), low),
            jax.ShapeDtypeStruct((rows, MODEL_WIDTH), low),
            jax.ShapeDtypeStruct((rows, MODEL_WIDTH), low),
            jax.ShapeDtypeStruct((rows, MODEL_WIDTH), jnp.float32),
            jax.ShapeDtypeStruct((MODEL_WIDTH, MODEL_WIDTH), low),
            jax.ShapeDtypeStruct((8, MODEL_WIDTH), jnp.float32),
            jax.ShapeDtypeStruct((8, MODEL_WIDTH), jnp.float32),
        ],
        scratch_shapes=[
            pltpu.VMEM((FF, 2 * MODEL_WIDTH), low),
            pltpu.VMEM((blocks, BLOCK, FF), low),
            pltpu.VMEM((blocks, BLOCK, MODEL_WIDTH), jnp.float32),
            pltpu.VMEM((blocks, BLOCK, 1), jnp.float32),
            pltpu.VMEM((seqs, MODEL_WIDTH), jnp.float32),
            pltpu.VMEM((seqs, MODEL_WIDTH), jnp.float32),
            pltpu.SemaphoreType.DMA((len(sizes),)),
        ],
        compiler_params=pltpu.CompilerParams(vmem_limit_bytes=VMEM_BYTES),
        cost_estimate=pl.CostEstimate(
            flops=rows * MODEL_WIDTH * FF * 16, bytes_accessed=rows * FF * 8, transcendentals=rows * FF
        ),
        name="ffn_layer",
    )(*scalars, first, teacher, dense_full, class_wide, logits_wide, norm_gains, neuron_index, *pieces)


def finish_kernel(small_rows, told_ref, *refs):
    gains_ref, moment_ref, square_ref = refs[:3]
    dense_refs, ffn_refs = refs[3:7], refs[7:11]
    scale_ref, facts_ref, rest_ref, new_ref, new_moment_ref, new_square_ref = refs[11:17]
    tails = jnp.sum(told_ref[:, MODEL_WIDTH:], axis=0, keepdims=True)
    squares, loss, count = [jnp.sum(tails[:, at : at + 128], axis=1, keepdims=True) for at in (0, 128, 256)]
    small = told_ref[:small_rows, :MODEL_WIDTH] + told_ref[small_rows : 2 * small_rows, :MODEL_WIDTH]
    squares = squares + jnp.sum(jnp.sum(small * small, axis=0, keepdims=True), axis=1, keepdims=True)
    inverse = 1.0 / count
    grad_norm = jnp.sqrt(squares) * inverse
    scaling = inverse * (clip_bound / jnp.maximum(grad_norm, clip_bound))
    scale_ref[...] = jnp.broadcast_to(scaling, scale_ref.shape)
    row = lax.broadcasted_iota(jnp.int32, facts_ref.shape, 0)
    facts_ref[...] = jnp.where(row == 0, loss, jnp.where(row == 1, count, grad_norm))
    gains = gains_ref.shape[0]
    rest_ref[...] = jnp.zeros_like(rest_ref)
    rest_ref[: small_rows - gains] = small[gains:] * scaling
    new_ref[...], new_moment_ref[...], new_square_ref[...] = adam_update(
        gains_ref[...], small[:gains] * scaling, moment_ref[...], square_ref[...], 0.0, gain_rate
    )
    for old, new in ((dense_refs, refs[17:21]), (ffn_refs, refs[21:25])):
        weight, moment, square, grad = [ref[...] for ref in old]
        weight, moment, square = adam_update(weight, grad * scaling, moment, square, weight_decay, learn_rate)
        new[0][...], new[1][...], new[2][...] = weight, moment, square
        new[3][...] = weight.astype(jnp.bfloat16)


def finish(small_rows, told, gains, dense, ffn):
    shapes = [(8, 128), (8, 128), (8, MODEL_WIDTH)] + [gains[0].shape] * 3
    shapes = [jax.ShapeDtypeStruct(shape, jnp.float32) for shape in shapes]
    for weights in (dense, ffn):
        shape = weights[0].shape
        shapes += [jax.ShapeDtypeStruct(shape, jnp.float32)] * 3 + [jax.ShapeDtypeStruct(shape, jnp.bfloat16)]
    return pl.pallas_call(
        lambda *refs: finish_kernel(small_rows, *refs),
        out_shape=shapes,
        compiler_params=pltpu.CompilerParams(vmem_limit_bytes=VMEM_BYTES),
        name="finish",
    )(told, *gains, *dense, *ffn)


def per_device(
    token_ids,
    replacements,
    replaced,
    lengths,
    widths,
    teacher_embed,
    teacher_hidden,
    teacher_logits,
    embed_table,
    embed_moment,
    embed_square,
    dense_weights,
    dense_moment,
    dense_square,
    feedforward,
    feedforward_moment,
    feedforward_square,
    classifier,
    classifier_moment,
    classifier_square,
    norm_gains,
    norm_moment,
    norm_square,
):
    both = ("dp", "mp")
    mp_count = lax.axis_size("mp")
    mp_index = lax.axis_index("mp")
    n_dev = lax.axis_size("dp") * mp_count
    own_seqs = teacher_logits.shape[0]
    own_rows = own_seqs * L
    table_rows = embed_table.shape[0]
    low = jnp.bfloat16
    by_bits = lax.axis_size("dp") == 8 and mp_count & (mp_count - 1) == 0
    if by_bits:
        dense_steps = gather_mp(dense_weights.astype(low))
        dense_column = jnp.concatenate(
            [lax.select_n(mp_index, *[dense_steps[k ^ z] for z in range(mp_count)]) for k in range(mp_count)],
            axis=0,
        )
    else:
        dense_column = lax.all_gather(dense_weights.astype(low), "mp", axis=0, tiled=True)
    dp_index = lax.axis_index("dp")
    neuron_piece = feedforward.shape[0]
    neuron_slot = jnp.arange(FF)
    if by_bits:
        chunk = neuron_piece * mp_count
        codes = jnp.repeat(jnp.array(piece_codes), chunk, total_repeat_length=FF)
        steps = neuron_slot % chunk // neuron_piece
        neuron_index = (dp_index ^ codes) * chunk + (mp_index ^ steps) * neuron_piece + neuron_slot % neuron_piece
    else:
        neuron_index = neuron_slot

    depth = -(-(own_rows * 3 // 2) // (n_dev * 16)) * 16
    capacity = depth - 1
    own_start = mp_index * own_seqs
    own_ids = lax.dynamic_slice_in_dim(
        jnp.where(replaced == 1, replacements, token_ids), own_start, own_seqs
    ).reshape(own_rows)
    owner = own_ids // table_rows
    local = own_ids - owner * table_rows
    place = jnp.arange(own_rows)
    first = jnp.min(
        jnp.where(own_ids[:, None] == own_ids[None, :], place[None, :], own_rows), axis=1
    )
    leads = first == place
    slot = jnp.sum(
        (leads[None, :] & (owner[:, None] == owner[None, :]) & (place[None, :] < first[:, None])).astype(
            jnp.int32
        ),
        axis=1,
    )
    deepest = jnp.max(slot)

    def positions(turn):
        rank = slot - turn * capacity
        return jnp.where((rank >= 0) & (rank < capacity), owner * depth + rank, -1)

    def wanted(turn):
        spot = jnp.where(leads, positions(turn), -1)
        hits = spot[:, None] == jnp.arange(n_dev * depth)[None, :]
        rows = jnp.max(jnp.where(hits, local[:, None], -1), axis=0).reshape(n_dev, depth)
        return jnp.where(jnp.arange(depth)[None, :] == capacity, deepest, rows)

    def exchange(blocks):
        return lax.all_to_all(blocks, both, split_axis=0, concat_axis=0)

    def flat_ids(asked):
        return jnp.where(jnp.arange(depth)[None, :] < capacity, asked, -1).reshape(-1)

    def asked_hot(asked):
        return (flat_ids(asked)[:, None] == jnp.arange(table_rows)[None, :]).astype(low)

    def own_hot(turn):
        return (positions(turn)[:, None] == jnp.arange(n_dev * depth)[None, :]).astype(low)

    def answer(asked, table):
        rows = jnp.dot(asked_hot(asked), table.astype(low), preferred_element_type=low)
        return rows.reshape(n_dev, depth, MODEL_WIDTH)

    def place_rows(turn, rows):
        return jnp.dot(own_hot(turn), rows.reshape(-1, MODEL_WIDTH), preferred_element_type=low)

    own_lengths = lax.dynamic_slice_in_dim(lengths, own_start, own_seqs)
    own_levels = lax.dynamic_slice_in_dim(widths, own_start, own_seqs)
    asked_first = exchange(wanted(0))
    ffn_low = feedforward.astype(low)
    if by_bits:
        dense_column, ffn_low = together(dense_column, ffn_low)
        dense_near = gather_near(dense_column)
        ffn_column = jnp.concatenate(gather_mp(ffn_low), axis=0)
        dense_far = far_blocks(*dense_near[1:])
        rows_first, ffn_column, *dense_blocks = together(
            answer(asked_first, embed_table), ffn_column, *dense_near, *dense_far
        )
    else:
        rows_first = answer(asked_first, embed_table)
    turns = jnp.max(asked_first[:, capacity]) // capacity + 1
    extra_rows = lax.while_loop(
        lambda state: state[0] < turns,
        lambda state: (
            state[0] + 1,
            state[1] + place_rows(state[0], exchange(answer(exchange(wanted(state[0])), embed_table))),
        ),
        (jnp.int32(1), jnp.zeros((own_rows, MODEL_WIDTH), low)),
    )[1]
    rows_first, extra_rows = together(rows_first, extra_rows)
    rows_first = exchange(rows_first)
    if by_bits:
        dense_full = assemble(dp_index, all_blocks(*dense_blocks))
        half = ffn_column.shape[0] // 2
        top, rest = ffn_column[:half], ffn_column[half:]
        x_top, y_rest = flip(top, 2), flip(rest, 4)
        x_rest, y_top = flip(rest, 2), flip(top, 4)
        ids_first, own_lengths, own_levels, dense_full, *near = together(
            flat_ids(asked_first), own_lengths, own_levels, dense_full, top, rest, x_top, x_rest, y_top, y_rest
        )
        far = flip(near[2], 4), flip(near[5], 2)
        near = near + [flip(block, 1) for block in near]
    else:
        ids_first = flat_ids(asked_first)
        dense_full = lax.all_gather(dense_column, "dp", axis=0, tiled=True)
        ffn_column = lax.all_gather(ffn_low, "mp", axis=0, tiled=True)
        ffn_pieces = [lax.all_gather(ffn_column, "dp", axis=0, tiled=True)]
    embedded_low = place_rows(0, rows_first) + extra_rows

    scalars = (own_lengths, own_levels)
    blocks = own_rows // BLOCK
    if by_bits:
        layer = attention_layer(0, blocks, scalars, embedded_low, dense_full, norm_gains, ())
        flow = together(*layer, *near, *far)
        layer, near, far = flow[:4], flow[4:16], flow[16:]
        far = [*far, flip(far[0], 1), flip(far[1], 1)]
        ffn_pieces = [*near[:4], *far[:2], *near[4:10], *far[2:], *near[10:]]
    else:
        layer = attention_layer(0, blocks, scalars, embedded_low, dense_full, norm_gains, ())
    project, head_mixture, first_sum, normed_low = layer
    class_pad = -classifier.shape[1] % 128
    hidden_low, grad_before, grad_feed_low, middle_low, grad_middle, grad_pool_rows, grad_class, ffn_sums = ffn_layer(
        scalars,
        first_sum,
        teacher_hidden.reshape(own_rows, MODEL_WIDTH),
        dense_full,
        jnp.pad(classifier, ((0, 0), (0, class_pad))).astype(low),
        jnp.pad(teacher_logits, ((0, 0), (0, class_pad))),
        norm_gains,
        neuron_index[None, :],
        ffn_pieces,
    )
    grad_class = grad_class[: classifier.shape[1]]

    def over_both(rows):
        rows = lax.psum_scatter(rows, "dp", scatter_dimension=0, tiled=True)
        return lax.psum_scatter(rows, "mp", scatter_dimension=0, tiled=True).astype(jnp.float32)

    def weight_sums(left, right):
        half = left.shape[1] // 2
        given = flip(contract_first(left[:, half:], right).astype(low), 1)
        return contract_first(left[:, :half], right).astype(low), given

    def by_core(rows):
        chunks = rows.reshape(4, 2, rows.shape[0] // 8, rows.shape[1])
        core = dp_index % 2
        return [lax.dynamic_index_in_dim(chunks, side, 1, keepdims=False) for side in (core, 1 - core)]

    def dense_scatter(own, other):
        place = dp_index // 2
        half = own.shape[1] // 2
        terms = own, flip(other, 1)

        def blocks_from(start):
            def blocks(first, last):
                codes = (0, 1, 3, 2)[first:last]
                picked = [
                    [lax.dynamic_index_in_dim(term, place ^ code, 0, keepdims=False) for code in codes] for term in terms
                ]
                return [
                    jnp.concatenate([block[start : start + half] for block in term], axis=0) for term in picked
                ]

            return blocks

        halves = blocks_from(0), blocks_from(half)
        parts = send_last(*halves, *send_first(*halves))
        parts = jnp.concatenate(parts, axis=0).reshape(mp_count, -1, MODEL_WIDTH)
        parts = [lax.dynamic_index_in_dim(parts, mp_index ^ step, 0, keepdims=False) for step in range(mp_count)]
        return [parts[0]] + [pass_mp(parts[step], step) for step in range(1, mp_count)]

    arrays = [
        grad_middle,
        first_sum,
        project,
        embedded_low,
        teacher_embed.reshape(own_rows, MODEL_WIDTH),
    ]
    weights = (dense_full, dense_full, norm_gains)
    if by_bits:
        down_own, down_given = weight_sums(hidden_low, grad_feed_low)
        up_own, up_given = weight_sums(grad_before, middle_low)
        arrays[0], *parts = together(arrays[0], up_own, up_given, down_own, down_given)
        halves = blocks_of(*parts[:2]), blocks_of(*parts[2:])
        parts = send_first(*halves)
        before = attention_backward(0, blocks - 1, scalars, arrays, weights, ())
        arrays[0], *flow = together(arrays[0], *before, *parts)
        *before, sums_one = flow[:4]
        parts = send_last(*halves, *flow[4:])
        before = attention_backward(blocks - 1, 1, scalars, arrays, weights, before)
        flow = together(*before, *parts)
        *before, sums_last = flow[:4]
        parts = [part.reshape(mp_count, neuron_piece, MODEL_WIDTH) for part in flow[4:]]
        ffn_parts = [jnp.concatenate([part[step] for part in parts], axis=1) for step in range(mp_count)]
        ffn_parts = [ffn_parts[0]] + [pass_mp(ffn_parts[step], step) for step in range(1, mp_count)]
        sums = sums_one + sums_last
    else:
        ffn_grad = jnp.concatenate(
            [contract_first(grad_before, middle_low), contract_first(hidden_low, grad_feed_low)], axis=1
        ).astype(low)
        ffn_grad = over_both(ffn_grad)
        *before, sums = attention_backward(0, blocks, scalars, arrays, weights, ())
    grad_project, grad_att_low, grad_embed_low = before
    grad_dense = jnp.concatenate(
        [
            contract_first(grad_project, normed_low).astype(low),
            contract_first(head_mixture, grad_att_low).astype(low),
            grad_pool_rows,
        ],
        axis=0,
    )

    small = jnp.concatenate([sums[:4], ffn_sums[:2], grad_class], axis=0)
    small_rows = small.shape[0]
    upper = lax.reduce_precision(small, 8, 7)
    rider = jnp.concatenate([upper, small - upper], axis=0).astype(low)
    rider = jnp.pad(rider, ((0, n_dev - 2 * small_rows), (0, 0)))

    def give_back(turn, rider):
        return give_rows(positions(turn), grad_embed_low, rider, depth).reshape(n_dev, depth, MODEL_WIDTH)

    def collect(ids, returned):
        return collect_rows(ids, returned.reshape(-1, MODEL_WIDTH), table_rows)

    def collect_more(state):
        turn, total, _ = state
        total = total + collect(flat_ids(exchange(wanted(turn))), exchange(give_back(turn, jnp.zeros_like(rider))))[0]
        return turn + 1, total, jnp.zeros((8, MODEL_WIDTH)).at[0].set(jnp.sum(total * total, axis=0))

    given = give_back(0, rider)
    if by_bits:
        given, *flow = together(given, *by_core(grad_dense), *ffn_parts)
        grad_dense, ffn_parts = flow[:2], flow[2:]
        ffn_grad = sum(part.astype(jnp.float32) for part in ffn_parts)
    returned = exchange(given)
    dense_parts = dense_scatter(*grad_dense) if by_bits else [over_both(grad_dense)]
    table_sums = collect(ids_first, returned)
    *table_sums, returned = together(*table_sums, returned)
    *table_sums, dense_first = together(*table_sums, dense_parts[0])
    dense_parts = together(*dense_parts[1:], dense_first)
    dense_grad = sum(part.astype(jnp.float32) for part in dense_parts)
    _, table_grad, table_squares = lax.while_loop(
        lambda state: state[0] < turns, collect_more, (jnp.int32(1), *table_sums)
    )
    small_row = jnp.sum(returned[:, capacity].astype(jnp.float32), axis=0)

    def folded(row):
        return sum(row[:, at : at + 128] for at in range(0, MODEL_WIDTH, 128))

    ffn_squares = jnp.sum(ffn_grad * ffn_grad, axis=0, keepdims=True)
    squares = table_squares[:1] + jnp.sum(dense_grad * dense_grad, axis=0, keepdims=True)
    squares = squares + ffn_squares[:, :MODEL_WIDTH] + ffn_squares[:, MODEL_WIDTH:]
    losses = sums[4:5] + ffn_sums[2:3] + ffn_sums[3:4]
    count_row = jnp.pad(own_lengths.astype(jnp.float32), (0, 128 - own_seqs))[None]
    message = jnp.concatenate([small_row[None], folded(squares), folded(losses), count_row], axis=1)
    told = exchange(jnp.broadcast_to(message, (n_dev, message.shape[1])))
    scaling, facts, rest, *updated = finish(
        small_rows,
        told,
        (norm_gains, norm_moment, norm_square),
        (dense_weights, dense_moment, dense_square, dense_grad),
        (feedforward, feedforward_moment, feedforward_square, ffn_grad),
    )
    gains_new, dense_new, ffn_new = updated[:3], updated[3:7], updated[7:]
    loss_sum, token_count, grad_norm = facts[0, 0], facts[1, 0], facts[2, 0]
    class_grad = rest[: classifier.shape[1]].T
    table_new = adam_update(
        embed_table, table_grad * scaling[:1, :1], embed_moment, embed_square, weight_decay, learn_rate
    )
    class_new = adam_update(
        classifier,
        class_grad,
        classifier_moment,
        classifier_square,
        weight_decay,
        learn_rate,
    )
    return (
        loss_sum,
        token_count,
        grad_norm,
        table_new[0],
        table_new[1],
        table_new[2],
        table_new[0].astype(jnp.bfloat16),
        dense_new[0],
        dense_new[1],
        dense_new[2],
        dense_new[3],
        ffn_new[0],
        ffn_new[1],
        ffn_new[2],
        ffn_new[3],
        class_new[0],
        class_new[1],
        class_new[2],
        class_new[0].astype(jnp.bfloat16),
        gains_new[0],
        gains_new[1],
        gains_new[2],
    )


def solution(mesh):
    placed = (
        P("dp", None),
        P("dp", None),
        P("dp", None),
        P("dp"),
        P("dp"),
        P(("dp", "mp"), None, None),
        P(("dp", "mp"), None, None),
        P(("dp", "mp"), None),
        P(("dp", "mp"), None),
        P(("dp", "mp"), None),
        P(("dp", "mp"), None),
        P(("dp", "mp"), None),
        P(("dp", "mp"), None),
        P(("dp", "mp"), None),
        P(("dp", "mp"), None),
        P(("dp", "mp"), None),
        P(("dp", "mp"), None),
        P(),
        P(),
        P(),
        P(),
        P(),
        P(),
    )
    return jax.shard_map(
        per_device,
        mesh=mesh,
        in_specs=placed,
        out_specs=(
            P(),
            P(),
            P(),
            P(("dp", "mp"), None),
            P(("dp", "mp"), None),
            P(("dp", "mp"), None),
            P(("dp", "mp"), None),
            P(("dp", "mp"), None),
            P(("dp", "mp"), None),
            P(("dp", "mp"), None),
            P(("dp", "mp"), None),
            P(("dp", "mp"), None),
            P(("dp", "mp"), None),
            P(("dp", "mp"), None),
            P(("dp", "mp"), None),
            P(),
            P(),
            P(),
            P(),
            P(),
            P(),
            P(),
        ),
        check_vma=False,
    )
```

```python
import jax
import jax.numpy as jnp
from jax import lax
from jax.experimental import pallas as pl
from jax.experimental.pallas import tpu as pltpu
from jax.sharding import PartitionSpec as P

MODEL_WIDTH = 768
HEADS = 12
FF = 3072
L = 128
LEVELS = 4
STEP = 10


highest_precision = lax.Precision.HIGHEST
norm_epsilon = 1e-05
learn_rate = 0.05
gain_rate = 0.5
beta_one = 0.9
beta_two = 0.999
adam_epsilon = 1e-08
weight_decay = 0.01
clip_bound = 1.0


def norm_forward(values, gain_row, shift_row):
    center = values - jnp.mean(values, axis=-1, keepdims=True)
    spread = jnp.mean(center * center, axis=-1, keepdims=True)
    inverse = lax.rsqrt(spread + norm_epsilon)
    unit = center * inverse
    return (unit * gain_row + shift_row, unit, inverse)


def norm_backward(grad, unit, inverse, gain_row):
    scaled = grad * gain_row
    level = jnp.mean(scaled, axis=-1, keepdims=True)
    along = jnp.mean(scaled * unit, axis=-1, keepdims=True)
    grad_values = inverse * (scaled - level - unit * along)
    return (grad_values, jnp.sum(grad * unit, axis=0), jnp.sum(grad, axis=0))


gelu_rate = 0.7978845608028654
gelu_cube = 0.044715


def gelu_forward(before):
    bend = jnp.tanh(gelu_rate * (before + gelu_cube * before * before * before))
    return 0.5 * before * (1.0 + bend)


def gelu_slope(before):
    bend = jnp.tanh(gelu_rate * (before + gelu_cube * before * before * before))
    inner = gelu_rate * (1.0 + 3.0 * gelu_cube * before * before)
    return 0.5 * (1.0 + bend) + 0.5 * before * (1.0 - bend * bend) * inner


def adam_update(weight, gradient, first_moment, second, decay_rate, rate):
    first_new = beta_one * first_moment + (1.0 - beta_one) * gradient
    second_new = beta_two * second + (1.0 - beta_two) * gradient * gradient
    direction = (
        first_new
        / (1.0 - beta_one**STEP)
        / (jnp.sqrt(second_new / (1.0 - beta_two**STEP)) + adam_epsilon)
    )
    return (weight - rate * (direction + decay_rate * weight), first_new, second_new)


def contract_last(left, right):
    return lax.dot_general(
        left, right, (((1,), (1,)), ((), ())), preferred_element_type=jnp.float32
    )


def contract_first(left, right):
    return lax.dot_general(
        left, right, (((0,), (0,)), ((), ())), preferred_element_type=jnp.float32
    )


def flip(block, bit):
    size = lax.axis_size("dp")
    return lax.ppermute(block, "dp", [(i, i ^ bit) for i in range(size)])


def add_low(*terms):
    return sum(term.astype(jnp.float32) for term in terms).astype(jnp.bfloat16)


piece_codes = (0, 2, 6, 4, 1, 3, 7, 5)


def gather_near(own):
    return own, flip(own, 2), flip(own, 4)


def far_blocks(along_x, along_y):
    half = along_x.shape[0] // 2
    return flip(along_x[:half], 4), flip(along_y[half:], 2)


def all_blocks(own, along_x, along_y, far_top, far_low):
    mine = [own, along_x, far_top, far_low, along_y]
    return mine + [flip(block, 1) for block in mine]


def assemble_kernel(place_ref, *refs):
    pieces, full_ref, arrivals = refs[:10], refs[10], refs[11]
    chunk = pieces[0].shape[0]
    copies = []
    for block, piece in enumerate(pieces):
        code = (0, 2, 6, 6, 4)[block % 5] + block // 5
        at = (place_ref[0] ^ code) * chunk
        if block % 5 == 3:
            at = at + chunk // 2
        at = pl.multiple_of(at, 16)
        copies.append(
            pltpu.make_async_copy(piece, full_ref.at[pl.ds(at, piece.shape[0])], arrivals.at[block])
        )
    for copy in copies:
        copy.start()
    for copy in copies:
        copy.wait()


def assemble(place, pieces):
    chunk, width = pieces[0].shape
    return pl.pallas_call(
        assemble_kernel,
        in_specs=[pl.BlockSpec(memory_space=pltpu.SMEM)] + [pl.BlockSpec(memory_space=pl.ANY)] * len(pieces),
        out_specs=pl.BlockSpec(memory_space=pltpu.VMEM),
        out_shape=jax.ShapeDtypeStruct((8 * chunk, width), pieces[0].dtype),
        compiler_params=pltpu.CompilerParams(vmem_limit_bytes=VMEM_BYTES),
        scratch_shapes=[pltpu.SemaphoreType.DMA((len(pieces),))],
        cost_estimate=pl.CostEstimate(flops=0, bytes_accessed=32 * chunk * width, transcendentals=0),
        name="assemble",
    )(place.reshape(1), *pieces)


def partner(index, step):
    size = lax.axis_size("mp")
    return index ^ step if size & (size - 1) == 0 else (index + step) % size


def pass_mp(block, step):
    return lax.ppermute(block, "mp", [(i, partner(i, step)) for i in range(lax.axis_size("mp"))])


def gather_mp(rows):
    return [rows] + [pass_mp(rows, step) for step in range(1, lax.axis_size("mp"))]


def send_first(top, rest):
    from_x = flip(add_low(*top(1, 3)), 2)
    from_y = flip(add_low(*rest(2, 4)), 4)
    size = from_x.shape[0] // 2
    late_y = add_low(*top(3, 4), from_x[size:])
    late_x = add_low(*rest(1, 2), from_y[:size])
    return together(late_y, late_x, from_x, from_y)


def send_last(top, rest, late_y, late_x, from_x, from_y):
    size = late_y.shape[0]
    late_y, late_x = flip(late_y, 4), flip(late_x, 2)
    return add_low(*top(0, 1), from_x[:size], late_y), add_low(*rest(0, 1), from_y[size:], late_x)


def blocks_of(*terms):
    size = terms[0].shape[0] // 4
    return lambda first, last: [term[first * size : last * size] for term in terms]


def together(*values):
    return lax.optimization_barrier(values)


PAIR = 2 * (MODEL_WIDTH // HEADS)
PAIRS = HEADS // 2
BLOCK = 2 * L
VMEM_BYTES = 56 * 1024 * 1024


def dot_nt(left, right):
    return lax.dot_general(
        left, right, (((1,), (1,)), ((), ())), preferred_element_type=jnp.float32
    )


def dot_tn(left, right):
    return lax.dot_general(
        left, right, (((0,), (0,)), ((), ())), preferred_element_type=jnp.float32
    )


def dot_nn(left, right):
    return jnp.dot(left, right, preferred_element_type=jnp.float32)


def both_heads(pair, left_half):
    zero = jnp.zeros_like(pair)
    return jnp.concatenate([jnp.where(left_half, pair, zero), jnp.where(left_half, zero, pair)], axis=0)


def pair_attend(queries, keys, key_bias):
    scores = dot_nt(queries, keys) * (MODEL_WIDTH // HEADS) ** (-0.5) + key_bias
    raised = jnp.exp(scores - jnp.max(scores, axis=-1, keepdims=True))
    return raised * (1.0 / jnp.sum(raised, axis=-1, keepdims=True))


def attention_kernel(
    start, length_ref, level_ref, embed_ref, qkv_ref, out_ref, gains_ref, project_ref, mixture_ref, first_ref, normed_ref
):
    step = pl.program_id(0) + start
    normed, _, _ = norm_forward(embed_ref[...].astype(jnp.float32), gains_ref[0:1], gains_ref[1:2])
    normed_low = normed.astype(jnp.bfloat16)
    normed_ref[...] = normed_low
    for part in range(3):
        columns = slice(part * MODEL_WIDTH, (part + 1) * MODEL_WIDTH)
        project_ref[:, columns] = dot_nt(normed_low, qkv_ref[columns]).astype(jnp.bfloat16)
    lane = lax.broadcasted_iota(jnp.int32, (L, PAIR), 1)
    left_half = lane < PAIR // 2
    for seq in range(BLOCK // L):
        rows = slice(seq * L, (seq + 1) * L)
        length = length_ref[step * (BLOCK // L) + seq]
        heads = level_ref[step * (BLOCK // L) + seq] * (HEADS // LEVELS)
        key_bias = jnp.where(lax.broadcasted_iota(jnp.int32, (1, L), 1) < length, 0.0, -1000000000.0)
        for pair in range(PAIRS):
            at = pair * PAIR
            queries = both_heads(project_ref[rows, at : at + PAIR], left_half)
            keys = project_ref[rows, MODEL_WIDTH + at : MODEL_WIDTH + at + PAIR]
            values = project_ref[rows, 2 * MODEL_WIDTH + at : 2 * MODEL_WIDTH + at + PAIR]
            attend = pair_attend(queries, keys, key_bias).astype(jnp.bfloat16)
            mixed = dot_nn(attend, values)
            mixed = jnp.where(left_half, mixed[:L], mixed[L:])
            head = 2 * pair + (lane >= PAIR // 2).astype(jnp.int32)
            mixture_ref[rows, at : at + PAIR] = jnp.where(head < heads, mixed, 0.0).astype(jnp.bfloat16)
    first_ref[...] = normed + dot_nn(mixture_ref[...], out_ref[...])


def whole(shape):
    return pl.BlockSpec(shape, lambda step: (0,) * len(shape))


def by_rows(width):
    return pl.BlockSpec((BLOCK, width), lambda step: (step, 0))


def attention_layer(start, steps, scalars, embedded, dense_full, norm_gains, before):
    rows = embedded.shape[0]
    low = jnp.bfloat16
    count = len(before)

    def at_rows(width):
        return pl.BlockSpec((BLOCK, width), lambda step: (step + start, 0))

    def body(length_ref, level_ref, *refs):
        attention_kernel(start, length_ref, level_ref, *refs[:4], *refs[4 + count :])

    return pl.pallas_call(
        body,
        grid=(steps,),
        in_specs=[
            pl.BlockSpec(memory_space=pltpu.SMEM),
            pl.BlockSpec(memory_space=pltpu.SMEM),
            at_rows(MODEL_WIDTH),
            whole((3 * MODEL_WIDTH, MODEL_WIDTH)),
            pl.BlockSpec((MODEL_WIDTH, MODEL_WIDTH), lambda step: (3, 0)),
            whole((6, MODEL_WIDTH)),
        ]
        + [pl.BlockSpec(memory_space=pl.ANY)] * count,
        out_specs=[at_rows(3 * MODEL_WIDTH), at_rows(MODEL_WIDTH), at_rows(MODEL_WIDTH), at_rows(MODEL_WIDTH)],
        out_shape=[
            jax.ShapeDtypeStruct((rows, 3 * MODEL_WIDTH), low),
            jax.ShapeDtypeStruct((rows, MODEL_WIDTH), low),
            jax.ShapeDtypeStruct((rows, MODEL_WIDTH), jnp.float32),
            jax.ShapeDtypeStruct((rows, MODEL_WIDTH), low),
        ],
        input_output_aliases={6 + place: place for place in range(count)},
        compiler_params=pltpu.CompilerParams(vmem_limit_bytes=VMEM_BYTES),
        cost_estimate=pl.CostEstimate(
            flops=steps * BLOCK * MODEL_WIDTH * MODEL_WIDTH * 20,
            bytes_accessed=steps * BLOCK * MODEL_WIDTH * 16,
            transcendentals=0,
        ),
        name="attention_layer",
    )(*scalars, embedded, dense_full, dense_full, norm_gains, *before)


def give_kernel(depth, spots_ref, grad_ref, rider_ref, sums_ref):
    rows = sums_ref.shape[0]
    row = pl.program_id(0) * rows + lax.broadcasted_iota(jnp.int32, (rows, 1), 0)
    last = lax.broadcasted_iota(jnp.int32, (1, rider_ref.shape[0]), 1) * depth + depth - 1
    own = (row == spots_ref[...]).astype(jnp.float32).astype(jnp.bfloat16)
    ride = (row == last).astype(jnp.float32).astype(jnp.bfloat16)
    sums_ref[...] = (dot_nn(own, grad_ref[...]) + dot_nn(ride, rider_ref[...])).astype(jnp.bfloat16)


def give_rows(spots, grads, rider, depth):
    total = rider.shape[0] * depth
    size = 512 if total % 512 == 0 else total
    return pl.pallas_call(
        lambda *refs: give_kernel(depth, *refs),
        grid=(total // size,),
        in_specs=[whole((1, spots.shape[0])), whole(grads.shape), whole(rider.shape)],
        out_specs=pl.BlockSpec((size, MODEL_WIDTH), lambda step: (step, 0)),
        out_shape=jax.ShapeDtypeStruct((total, MODEL_WIDTH), jnp.bfloat16),
        compiler_params=pltpu.CompilerParams(vmem_limit_bytes=VMEM_BYTES),
        cost_estimate=pl.CostEstimate(
            flops=2 * total * spots.shape[0] * MODEL_WIDTH, bytes_accessed=4 * total * MODEL_WIDTH, transcendentals=0
        ),
        name="give_rows",
    )(spots[None, :], grads, rider)


def collect_kernel(ids_ref, returned_ref, sums_ref, squares_ref):
    step = pl.program_id(0)
    rows = sums_ref.shape[0]
    row = step * rows + lax.broadcasted_iota(jnp.int32, (rows, 1), 0)
    hot = (row == ids_ref[...]).astype(jnp.float32).astype(jnp.bfloat16)
    sums = dot_nn(hot, returned_ref[...])
    sums_ref[...] = sums

    @pl.when(step == 0)
    def _():
        squares_ref[...] = jnp.zeros_like(squares_ref)

    squares_ref[0:1] += jnp.sum(sums * sums, axis=0, keepdims=True)


def collect_rows(ids, returned, table_rows):
    size = 240
    return pl.pallas_call(
        collect_kernel,
        grid=(-(-table_rows // size),),
        in_specs=[whole((1, ids.shape[0])), whole(returned.shape)],
        out_specs=[pl.BlockSpec((size, MODEL_WIDTH), lambda step: (step, 0)), whole((8, MODEL_WIDTH))],
        out_shape=[
            jax.ShapeDtypeStruct((table_rows, MODEL_WIDTH), jnp.float32),
            jax.ShapeDtypeStruct((8, MODEL_WIDTH), jnp.float32),
        ],
        compiler_params=pltpu.CompilerParams(vmem_limit_bytes=VMEM_BYTES),
        cost_estimate=pl.CostEstimate(
            flops=2 * table_rows * ids.shape[0] * MODEL_WIDTH, bytes_accessed=8 * table_rows * MODEL_WIDTH, transcendentals=0
        ),
        name="collect_rows",
    )(ids[None, :], returned)


def attention_back_kernel(
    start,
    length_ref,
    level_ref,
    grad_ref,
    first_ref,
    project_ref,
    embed_ref,
    teacher_ref,
    qkv_ref,
    out_ref,
    gains_ref,
    grad_project_ref,
    grad_att_ref,
    grad_embed_ref,
    sums_ref,
    grad_mixture_ref,
):
    turn = pl.program_id(0)
    step = turn + start
    low = jnp.bfloat16
    _, unit_one, inverse_one = norm_forward(first_ref[...], gains_ref[2:3], gains_ref[3:4])
    grad_first, gain_one, shift_one = norm_backward(grad_ref[...], unit_one, inverse_one, gains_ref[2:3])
    grad_att = grad_first.astype(low)
    grad_att_ref[...] = grad_att
    grad_mixture_ref[...] = dot_nt(grad_att, out_ref[...]).astype(low)
    lane = lax.broadcasted_iota(jnp.int32, (L, PAIR), 1)
    left_half = lane < PAIR // 2
    scaling = (MODEL_WIDTH // HEADS) ** (-0.5)
    usable = []
    for seq in range(BLOCK // L):
        rows = slice(seq * L, (seq + 1) * L)
        length = length_ref[step * (BLOCK // L) + seq]
        heads = level_ref[step * (BLOCK // L) + seq] * (HEADS // LEVELS)
        usable.append((lax.broadcasted_iota(jnp.int32, (L, 1), 0) < length).astype(jnp.float32))
        key_bias = jnp.where(lax.broadcasted_iota(jnp.int32, (L, 1), 0) < length, 0.0, -1000000000.0)
        for pair in range(PAIRS):
            at = pair * PAIR
            queries = both_heads(project_ref[rows, at : at + PAIR], left_half)
            keys = project_ref[rows, MODEL_WIDTH + at : MODEL_WIDTH + at + PAIR]
            values = project_ref[rows, 2 * MODEL_WIDTH + at : 2 * MODEL_WIDTH + at + PAIR]
            scores = dot_nt(keys, queries) * scaling + key_bias
            raised = jnp.exp(scores - jnp.max(scores, axis=0, keepdims=True))
            attend = raised * (1.0 / jnp.sum(raised, axis=0, keepdims=True))
            head = 2 * pair + (lane >= PAIR // 2).astype(jnp.int32)
            mixture = grad_mixture_ref[rows, at : at + PAIR]
            mixture = both_heads(jnp.where(head < heads, mixture, jnp.zeros_like(mixture)), left_half)
            grad_values = dot_nn(attend.astype(low), mixture)
            grad_attend = dot_nt(values, mixture)
            level = jnp.sum(grad_attend * attend, axis=0, keepdims=True)
            grad_scores = (attend * (grad_attend - level)).astype(low)
            grad_keys = dot_nn(grad_scores, queries) * scaling
            grad_queries = dot_tn(grad_scores, keys) * scaling
            grad_queries = jnp.where(left_half, grad_queries[:L], grad_queries[L:])
            grad_project_ref[rows, at : at + PAIR] = grad_queries.astype(low)
            grad_project_ref[rows, MODEL_WIDTH + at : MODEL_WIDTH + at + PAIR] = grad_keys.astype(low)
            grad_project_ref[rows, 2 * MODEL_WIDTH + at : 2 * MODEL_WIDTH + at + PAIR] = grad_values.astype(low)
    normed, unit_base, inverse_base = norm_forward(
        embed_ref[...].astype(jnp.float32), gains_ref[0:1], gains_ref[1:2]
    )
    usable = jnp.concatenate(usable, axis=0)
    gap = usable * (normed - teacher_ref[...].astype(jnp.float32))
    grad_normed = grad_first + 2.0 * gap + dot_nn(grad_project_ref[...], qkv_ref[...])
    grad_embed, gain_base, shift_base = norm_backward(grad_normed, unit_base, inverse_base, gains_ref[0:1])
    grad_embed_ref[...] = grad_embed.astype(low)

    @pl.when(turn == 0)
    def _():
        sums_ref[...] = jnp.zeros_like(sums_ref)

    for row, value in enumerate((gain_base, shift_base, gain_one, shift_one, jnp.sum(gap * gap, axis=0))):
        sums_ref[row : row + 1] += value[None]


def attention_backward(start, steps, scalars, arrays, weights, before):
    rows = arrays[0].shape[0]
    low = jnp.bfloat16

    def at_rows(width):
        return pl.BlockSpec((BLOCK, width), lambda step: (step + start, 0))

    widths = (MODEL_WIDTH, MODEL_WIDTH, 3 * MODEL_WIDTH, MODEL_WIDTH, MODEL_WIDTH)
    count = len(before)

    def body(length_ref, level_ref, *refs):
        attention_back_kernel(start, length_ref, level_ref, *refs[:8], *refs[8 + count :])

    return pl.pallas_call(
        body,
        grid=(steps,),
        in_specs=[pl.BlockSpec(memory_space=pltpu.SMEM)] * 2
        + [at_rows(width) for width in widths]
        + [
            whole((3 * MODEL_WIDTH, MODEL_WIDTH)),
            pl.BlockSpec((MODEL_WIDTH, MODEL_WIDTH), lambda step: (3, 0)),
            whole((6, MODEL_WIDTH)),
        ]
        + [pl.BlockSpec(memory_space=pl.ANY)] * count,
        out_specs=[at_rows(3 * MODEL_WIDTH), at_rows(MODEL_WIDTH), at_rows(MODEL_WIDTH), whole((8, MODEL_WIDTH))],
        out_shape=[
            jax.ShapeDtypeStruct((rows, 3 * MODEL_WIDTH), low),
            jax.ShapeDtypeStruct((rows, MODEL_WIDTH), low),
            jax.ShapeDtypeStruct((rows, MODEL_WIDTH), low),
            jax.ShapeDtypeStruct((8, MODEL_WIDTH), jnp.float32),
        ],
        input_output_aliases={10 + place: place for place in range(count)},
        scratch_shapes=[pltpu.VMEM((BLOCK, MODEL_WIDTH), low)],
        compiler_params=pltpu.CompilerParams(vmem_limit_bytes=VMEM_BYTES),
        cost_estimate=pl.CostEstimate(
            flops=steps * BLOCK * MODEL_WIDTH * MODEL_WIDTH * 40,
            bytes_accessed=steps * BLOCK * MODEL_WIDTH * 24,
            transcendentals=0,
        ),
        name="attention_backward",
    )(*scalars, *arrays, *weights, *before)


FFN_CHUNK = 768


def split_low(value):
    upper = value.astype(jnp.bfloat16)
    return jnp.concatenate([upper, (value - upper.astype(jnp.float32)).astype(jnp.bfloat16)], axis=0)


def ffn_kernel(sizes, length_ref, level_ref, first_ref, teacher_ref, pool_ref, class_ref, logits_ref, gains_ref, index_ref, *refs):
    pieces = refs[: len(sizes)]
    (hidden_ref, grad_before_ref, grad_feed_ref, middle_ref, grad_middle_ref, grad_pool_ref, grad_class_ref, sums_ref) = refs[
        len(sizes) : len(sizes) + 8
    ]
    weights_ref, slope_ref, unit_ref, inverse_ref, pooled_rows_ref, grad_rows_ref, arrivals = refs[len(sizes) + 8 :]
    step = pl.program_id(0)
    blocks = slope_ref.shape[0]
    seqs = BLOCK // L
    low = jnp.bfloat16
    row = lax.broadcasted_iota(jnp.int32, (BLOCK, 1), 0)

    def copies():
        at = 0
        for place, size in enumerate(sizes):
            yield pltpu.make_async_copy(pieces[place], weights_ref.at[pl.ds(at, size)], arrivals.at[place])
            at += size

    def go(waiting):
        arriving = list(copies()) if waiting else []
        for copy in arriving:
            copy.start()
        if waiting:
            sums_ref[...] = jnp.zeros_like(sums_ref)
        waited, arrived = 0, 0
        middle, _, _ = norm_forward(first_ref[...], gains_ref[2:3], gains_ref[3:4])
        middle_low = middle.astype(low)
        middle_ref[...] = middle_low
        limit = jnp.full((BLOCK, 1), level_ref[step * seqs])
        for seq in range(1, seqs):
            limit = jnp.where(row >= seq * L, level_ref[step * seqs + seq], limit)
        limit = limit * (FF // LEVELS)
        for at in range(0, FF, FFN_CHUNK):
            columns = slice(at, at + FFN_CHUNK)
            while waiting and arrived < at + FFN_CHUNK:
                arriving[waited].wait()
                arrived += sizes[waited]
                waited += 1
            before = dot_nt(middle_low, weights_ref[columns, :MODEL_WIDTH])
            square = before * before
            bend = jnp.tanh(before * (gelu_rate + gelu_rate * gelu_cube * square))
            rise = 0.5 + 0.5 * bend
            value = before * rise
            slope = rise + (0.5 * before) * (1.0 - bend * bend) * (gelu_rate + 3.0 * gelu_rate * gelu_cube * square)
            on = index_ref[:, columns] < limit
            hidden_ref[:, columns] = jnp.where(on, value, 0.0).astype(low)
            slope_ref[step, :, columns] = jnp.where(on, slope, 0.0).astype(low)
        feed = dot_nn(hidden_ref[...], weights_ref[:, MODEL_WIDTH:])
        output, unit, inverse = norm_forward(middle + feed, gains_ref[4:5], gains_ref[5:6])
        unit_ref[step] = unit
        inverse_ref[step] = inverse
        for seq in range(seqs):
            pooled_rows_ref[pl.ds(step * seqs + seq, 1), :] = output[seq * L : seq * L + 1]

    @pl.when(step == 0)
    def _():
        go(True)

    @pl.when((step > 0) & (step < blocks))
    def _():
        go(False)

    @pl.when(step == blocks)
    def _():
        first_low = pooled_rows_ref[...].astype(low)
        pooled = jnp.tanh(dot_nn(first_low, pool_ref[...]))
        pooled_low = pooled.astype(low)
        gap = dot_nn(pooled_low, class_ref[...]) - logits_ref[...]
        grad_logits = split_low(2.0 * L * gap)
        rows = gap.shape[0]
        grad_class = dot_tn(grad_logits, jnp.concatenate([pooled_low, pooled_low], axis=0))
        grad_class_ref[...] = grad_class[: grad_class_ref.shape[0]]
        grad_pooled = dot_nt(grad_logits, class_ref[...])
        grad_inner = split_low((grad_pooled[:rows] + grad_pooled[rows:]) * (1.0 - pooled * pooled))
        grad_pool_ref[...] = dot_tn(jnp.concatenate([first_low, first_low], axis=0), grad_inner).astype(low)
        grad_rows = dot_nt(grad_inner, pool_ref[...])
        grad_rows_ref[...] = grad_rows[:rows] + grad_rows[rows:]
        sums_ref[3:4, : gap.shape[1]] += L * jnp.sum(gap * gap, axis=0, keepdims=True)

    @pl.when(step > blocks)
    def _():
        block = step - blocks - 1
        unit = unit_ref[block]
        reach = jnp.full((BLOCK, 1), length_ref[block * seqs])
        pooled_grad = jnp.where(row == 0, grad_rows_ref[pl.ds(block * seqs, 1), :], 0.0)
        for seq in range(1, seqs):
            reach = jnp.where(row >= seq * L, length_ref[block * seqs + seq] + seq * L, reach)
            pooled_grad = jnp.where(row == seq * L, grad_rows_ref[pl.ds(block * seqs + seq, 1), :], pooled_grad)
        output = unit * gains_ref[4:5] + gains_ref[5:6]
        gap = jnp.where(row < reach, output - teacher_ref[...].astype(jnp.float32), 0.0)
        grad_second, gain, shift = norm_backward(2.0 * gap + pooled_grad, unit, inverse_ref[block], gains_ref[4:5])
        grad_feed = grad_second.astype(low)
        grad_feed_ref[...] = grad_feed
        for at in range(0, FF, FFN_CHUNK):
            columns = slice(at, at + FFN_CHUNK)
            grad_hidden = dot_nt(grad_feed, weights_ref[columns, MODEL_WIDTH:])
            grad_before_ref[:, columns] = (grad_hidden * slope_ref[block, :, columns].astype(jnp.float32)).astype(low)
        grad_middle_ref[...] = grad_second + dot_nn(grad_before_ref[...], weights_ref[:, :MODEL_WIDTH])
        for place, value in enumerate((gain, shift, jnp.sum(gap * gap, axis=0))):
            sums_ref[place : place + 1] += value[None]


def ffn_layer(scalars, first, teacher, dense_full, class_wide, logits_wide, norm_gains, neuron_index, pieces):
    rows = first.shape[0]
    seqs = rows // L
    blocks = rows // BLOCK
    low = jnp.bfloat16
    sizes = tuple(piece.shape[0] for piece in pieces)

    def going(width):
        return pl.BlockSpec((BLOCK, width), lambda step: (jnp.minimum(step, blocks - 1), 0))

    def coming(width):
        return pl.BlockSpec((BLOCK, width), lambda step: (jnp.maximum(step - blocks - 1, 0), 0))

    return pl.pallas_call(
        lambda *refs: ffn_kernel(sizes, *refs),
        grid=(2 * blocks + 1,),
        in_specs=[
            pl.BlockSpec(memory_space=pltpu.SMEM),
            pl.BlockSpec(memory_space=pltpu.SMEM),
            going(MODEL_WIDTH),
            coming(MODEL_WIDTH),
            pl.BlockSpec((MODEL_WIDTH, MODEL_WIDTH), lambda step: (4, 0)),
            whole(class_wide.shape),
            whole(logits_wide.shape),
            whole((6, MODEL_WIDTH)),
            whole((1, FF)),
        ]
        + [pl.BlockSpec(memory_space=pl.ANY)] * len(sizes),
        out_specs=[
            going(FF),
            coming(FF),
            coming(MODEL_WIDTH),
            going(MODEL_WIDTH),
            coming(MODEL_WIDTH),
            whole((MODEL_WIDTH, MODEL_WIDTH)),
            whole((8, MODEL_WIDTH)),
            whole((8, MODEL_WIDTH)),
        ],
        out_shape=[
            jax.ShapeDtypeStruct((rows, FF), low),
            jax.ShapeDtypeStruct((rows, FF), low),
            jax.ShapeDtypeStruct((rows, MODEL_WIDTH), low),
            jax.ShapeDtypeStruct((rows, MODEL_WIDTH), low),
            jax.ShapeDtypeStruct((rows, MODEL_WIDTH), jnp.float32),
            jax.ShapeDtypeStruct((MODEL_WIDTH, MODEL_WIDTH), low),
            jax.ShapeDtypeStruct((8, MODEL_WIDTH), jnp.float32),
            jax.ShapeDtypeStruct((8, MODEL_WIDTH), jnp.float32),
        ],
        scratch_shapes=[
            pltpu.VMEM((FF, 2 * MODEL_WIDTH), low),
            pltpu.VMEM((blocks, BLOCK, FF), low),
            pltpu.VMEM((blocks, BLOCK, MODEL_WIDTH), jnp.float32),
            pltpu.VMEM((blocks, BLOCK, 1), jnp.float32),
            pltpu.VMEM((seqs, MODEL_WIDTH), jnp.float32),
            pltpu.VMEM((seqs, MODEL_WIDTH), jnp.float32),
            pltpu.SemaphoreType.DMA((len(sizes),)),
        ],
        compiler_params=pltpu.CompilerParams(vmem_limit_bytes=VMEM_BYTES),
        cost_estimate=pl.CostEstimate(
            flops=rows * MODEL_WIDTH * FF * 16, bytes_accessed=rows * FF * 8, transcendentals=rows * FF
        ),
        name="ffn_layer",
    )(*scalars, first, teacher, dense_full, class_wide, logits_wide, norm_gains, neuron_index, *pieces)


def finish_kernel(small_rows, told_ref, *refs):
    gains_ref, moment_ref, square_ref = refs[:3]
    dense_refs, ffn_refs = refs[3:7], refs[7:11]
    class_refs = refs[11:14]
    scale_ref, loss_ref, count_ref, norm_ref, new_ref, new_moment_ref, new_square_ref = refs[14:21]
    tails = jnp.sum(told_ref[:, MODEL_WIDTH:], axis=0, keepdims=True)
    squares, loss, count = [jnp.sum(tails[:, at : at + 128], axis=1, keepdims=True) for at in (0, 128, 256)]
    small = told_ref[:small_rows, :MODEL_WIDTH] + told_ref[small_rows : 2 * small_rows, :MODEL_WIDTH]
    squares = squares + jnp.sum(jnp.sum(small * small, axis=0, keepdims=True), axis=1, keepdims=True)
    inverse = 1.0 / count
    grad_norm = jnp.sqrt(squares) * inverse
    scaling = inverse * (clip_bound / jnp.maximum(grad_norm, clip_bound))
    scale_ref[...], loss_ref[...], count_ref[...], norm_ref[...] = scaling, loss, count, grad_norm
    gains = gains_ref.shape[0]
    new_ref[...], new_moment_ref[...], new_square_ref[...] = adam_update(
        gains_ref[...], small[:gains] * scaling, moment_ref[...], square_ref[...], 0.0, gain_rate
    )
    groups = (
        ([ref[...] for ref in dense_refs], refs[21:25]),
        ([ref[...] for ref in ffn_refs], refs[25:29]),
        ([ref[...] for ref in class_refs] + [small[gains:]], refs[29:33]),
    )
    for (weight, moment, square, grad), new in groups:
        weight, moment, square = adam_update(weight, grad * scaling, moment, square, weight_decay, learn_rate)
        new[0][...], new[1][...], new[2][...] = weight, moment, square
        new[3][...] = weight.astype(jnp.bfloat16)


def finish(small_rows, told, gains, dense, ffn, classes):
    shapes = [(1, 1)] * 4 + [gains[0].shape] * 3
    shapes = [jax.ShapeDtypeStruct(shape, jnp.float32) for shape in shapes]
    for weights in (dense, ffn, classes):
        shape = weights[0].shape
        shapes += [jax.ShapeDtypeStruct(shape, jnp.float32)] * 3 + [jax.ShapeDtypeStruct(shape, jnp.bfloat16)]
    return pl.pallas_call(
        lambda *refs: finish_kernel(small_rows, *refs),
        out_shape=shapes,
        compiler_params=pltpu.CompilerParams(vmem_limit_bytes=VMEM_BYTES),
        name="finish",
    )(told, *gains, *dense, *ffn, *classes)


def per_device(
    token_ids,
    replacements,
    replaced,
    lengths,
    widths,
    teacher_embed,
    teacher_hidden,
    teacher_logits,
    embed_table,
    embed_moment,
    embed_square,
    dense_weights,
    dense_moment,
    dense_square,
    feedforward,
    feedforward_moment,
    feedforward_square,
    classifier,
    classifier_moment,
    classifier_square,
    norm_gains,
    norm_moment,
    norm_square,
):
    both = ("dp", "mp")
    mp_count = lax.axis_size("mp")
    mp_index = lax.axis_index("mp")
    n_dev = lax.axis_size("dp") * mp_count
    own_seqs = teacher_logits.shape[0]
    own_rows = own_seqs * L
    table_rows = embed_table.shape[0]
    low = jnp.bfloat16
    by_bits = lax.axis_size("dp") == 8 and mp_count & (mp_count - 1) == 0
    if by_bits:
        dense_steps = gather_mp(dense_weights.astype(low))
        dense_column = jnp.concatenate(
            [lax.select_n(mp_index, *[dense_steps[k ^ z] for z in range(mp_count)]) for k in range(mp_count)],
            axis=0,
        )
    else:
        dense_column = lax.all_gather(dense_weights.astype(low), "mp", axis=0, tiled=True)
    dp_index = lax.axis_index("dp")
    neuron_piece = feedforward.shape[0]
    neuron_slot = jnp.arange(FF)
    if by_bits:
        chunk = neuron_piece * mp_count
        codes = jnp.repeat(jnp.array(piece_codes), chunk, total_repeat_length=FF)
        steps = neuron_slot % chunk // neuron_piece
        neuron_index = (dp_index ^ codes) * chunk + (mp_index ^ steps) * neuron_piece + neuron_slot % neuron_piece
    else:
        neuron_index = neuron_slot

    depth = -(-(own_rows * 3 // 2) // (n_dev * 16)) * 16
    capacity = depth - 1
    own_start = mp_index * own_seqs
    own_ids = lax.dynamic_slice_in_dim(
        jnp.where(replaced == 1, replacements, token_ids), own_start, own_seqs
    ).reshape(own_rows)
    owner = own_ids // table_rows
    local = own_ids - owner * table_rows
    place = jnp.arange(own_rows)
    first = jnp.min(
        jnp.where(own_ids[:, None] == own_ids[None, :], place[None, :], own_rows), axis=1
    )
    leads = first == place
    slot = jnp.sum(
        (leads[None, :] & (owner[:, None] == owner[None, :]) & (place[None, :] < first[:, None])).astype(
            jnp.int32
        ),
        axis=1,
    )
    deepest = jnp.max(slot)

    def positions(turn):
        rank = slot - turn * capacity
        return jnp.where((rank >= 0) & (rank < capacity), owner * depth + rank, -1)

    def wanted(turn):
        spot = jnp.where(leads, positions(turn), -1)
        hits = spot[:, None] == jnp.arange(n_dev * depth)[None, :]
        rows = jnp.max(jnp.where(hits, local[:, None], -1), axis=0).reshape(n_dev, depth)
        return jnp.where(jnp.arange(depth)[None, :] == capacity, deepest, rows)

    def exchange(blocks):
        return lax.all_to_all(blocks, both, split_axis=0, concat_axis=0)

    def flat_ids(asked):
        return jnp.where(jnp.arange(depth)[None, :] < capacity, asked, -1).reshape(-1)

    def asked_hot(asked):
        return (flat_ids(asked)[:, None] == jnp.arange(table_rows)[None, :]).astype(low)

    def own_hot(turn):
        return (positions(turn)[:, None] == jnp.arange(n_dev * depth)[None, :]).astype(low)

    def answer(asked, table):
        rows = jnp.dot(asked_hot(asked), table.astype(low), preferred_element_type=low)
        return rows.reshape(n_dev, depth, MODEL_WIDTH)

    def place_rows(turn, rows):
        return jnp.dot(own_hot(turn), rows.reshape(-1, MODEL_WIDTH), preferred_element_type=low)

    own_lengths = lax.dynamic_slice_in_dim(lengths, own_start, own_seqs)
    own_levels = lax.dynamic_slice_in_dim(widths, own_start, own_seqs)
    asked_first = exchange(wanted(0))
    ffn_low = feedforward.astype(low)
    if by_bits:
        dense_column, ffn_low = together(dense_column, ffn_low)
        dense_near = gather_near(dense_column)
        ffn_column = jnp.concatenate(gather_mp(ffn_low), axis=0)
        dense_far = far_blocks(*dense_near[1:])
        rows_first, ffn_column, *dense_blocks = together(
            answer(asked_first, embed_table), ffn_column, *dense_near, *dense_far
        )
    else:
        rows_first = answer(asked_first, embed_table)
    turns = jnp.max(asked_first[:, capacity]) // capacity + 1
    extra_rows = lax.while_loop(
        lambda state: state[0] < turns,
        lambda state: (
            state[0] + 1,
            state[1] + place_rows(state[0], exchange(answer(exchange(wanted(state[0])), embed_table))),
        ),
        (jnp.int32(1), jnp.zeros((own_rows, MODEL_WIDTH), low)),
    )[1]
    rows_first, extra_rows = together(rows_first, extra_rows)
    rows_first = exchange(rows_first)
    if by_bits:
        dense_full = assemble(dp_index, all_blocks(*dense_blocks))
        half = ffn_column.shape[0] // 2
        top, rest = ffn_column[:half], ffn_column[half:]
        x_top, y_rest = flip(top, 2), flip(rest, 4)
        x_rest, y_top = flip(rest, 2), flip(top, 4)
        ids_first, own_lengths, own_levels, dense_full, *near = together(
            flat_ids(asked_first), own_lengths, own_levels, dense_full, top, rest, x_top, x_rest, y_top, y_rest
        )
        far = flip(near[2], 4), flip(near[5], 2)
        near = near + [flip(block, 1) for block in near]
    else:
        ids_first = flat_ids(asked_first)
        dense_full = lax.all_gather(dense_column, "dp", axis=0, tiled=True)
        ffn_column = lax.all_gather(ffn_low, "mp", axis=0, tiled=True)
        ffn_pieces = [lax.all_gather(ffn_column, "dp", axis=0, tiled=True)]
    embedded_low = place_rows(0, rows_first) + extra_rows

    scalars = (own_lengths, own_levels)
    blocks = own_rows // BLOCK
    if by_bits:
        layer = attention_layer(0, blocks, scalars, embedded_low, dense_full, norm_gains, ())
        flow = together(*layer, *near, *far)
        layer, near, far = flow[:4], flow[4:16], flow[16:]
        far = [*far, flip(far[0], 1), flip(far[1], 1)]
        ffn_pieces = [*near[:4], *far[:2], *near[4:10], *far[2:], *near[10:]]
    else:
        layer = attention_layer(0, blocks, scalars, embedded_low, dense_full, norm_gains, ())
    project, head_mixture, first_sum, normed_low = layer
    class_pad = -classifier.shape[1] % 128
    hidden_low, grad_before, grad_feed_low, middle_low, grad_middle, grad_pool_rows, grad_class, ffn_sums = ffn_layer(
        scalars,
        first_sum,
        teacher_hidden.reshape(own_rows, MODEL_WIDTH),
        dense_full,
        jnp.pad(classifier, ((0, 0), (0, class_pad))).astype(low),
        jnp.pad(teacher_logits, ((0, 0), (0, class_pad))),
        norm_gains,
        neuron_index[None, :],
        ffn_pieces,
    )
    grad_class = grad_class[: classifier.shape[1]]

    def over_both(rows):
        rows = lax.psum_scatter(rows, "dp", scatter_dimension=0, tiled=True)
        return lax.psum_scatter(rows, "mp", scatter_dimension=0, tiled=True).astype(jnp.float32)

    def weight_sums(left, right):
        half = left.shape[1] // 2
        given = flip(contract_first(left[:, half:], right).astype(low), 1)
        return contract_first(left[:, :half], right).astype(low), given

    def by_core(rows):
        chunks = rows.reshape(4, 2, rows.shape[0] // 8, rows.shape[1])
        core = dp_index % 2
        return [lax.dynamic_index_in_dim(chunks, side, 1, keepdims=False) for side in (core, 1 - core)]

    def dense_scatter(own, other):
        place = dp_index // 2
        half = own.shape[1] // 2
        terms = own, flip(other, 1)

        def blocks_from(start):
            def blocks(first, last):
                codes = (0, 1, 3, 2)[first:last]
                picked = [
                    [lax.dynamic_index_in_dim(term, place ^ code, 0, keepdims=False) for code in codes] for term in terms
                ]
                return [
                    jnp.concatenate([block[start : start + half] for block in term], axis=0) for term in picked
                ]

            return blocks

        halves = blocks_from(0), blocks_from(half)
        parts = send_last(*halves, *send_first(*halves))
        parts = jnp.concatenate(parts, axis=0).reshape(mp_count, -1, MODEL_WIDTH)
        parts = [lax.dynamic_index_in_dim(parts, mp_index ^ step, 0, keepdims=False) for step in range(mp_count)]
        return [parts[0]] + [pass_mp(parts[step], step) for step in range(1, mp_count)]

    arrays = [
        grad_middle,
        first_sum,
        project,
        embedded_low,
        teacher_embed.reshape(own_rows, MODEL_WIDTH),
    ]
    weights = (dense_full, dense_full, norm_gains)
    if by_bits:
        down_own, down_given = weight_sums(hidden_low, grad_feed_low)
        up_own, up_given = weight_sums(grad_before, middle_low)
        arrays[0], *parts = together(arrays[0], up_own, up_given, down_own, down_given)
        halves = blocks_of(*parts[:2]), blocks_of(*parts[2:])
        parts = send_first(*halves)
        before = attention_backward(0, blocks - 1, scalars, arrays, weights, ())
        arrays[0], *flow = together(arrays[0], *before, *parts)
        *before, sums_one = flow[:4]
        parts = send_last(*halves, *flow[4:])
        before = attention_backward(blocks - 1, 1, scalars, arrays, weights, before)
        flow = together(*before, *parts)
        *before, sums_last = flow[:4]
        parts = [part.reshape(mp_count, neuron_piece, MODEL_WIDTH) for part in flow[4:]]
        ffn_parts = [jnp.concatenate([part[step] for part in parts], axis=1) for step in range(mp_count)]
        ffn_parts = [ffn_parts[0]] + [pass_mp(ffn_parts[step], step) for step in range(1, mp_count)]
        sums = sums_one + sums_last
    else:
        ffn_grad = jnp.concatenate(
            [contract_first(grad_before, middle_low), contract_first(hidden_low, grad_feed_low)], axis=1
        ).astype(low)
        ffn_grad = over_both(ffn_grad)
        *before, sums = attention_backward(0, blocks, scalars, arrays, weights, ())
    grad_project, grad_att_low, grad_embed_low = before
    grad_dense = jnp.concatenate(
        [
            contract_first(grad_project, normed_low).astype(low),
            contract_first(head_mixture, grad_att_low).astype(low),
            grad_pool_rows,
        ],
        axis=0,
    )

    small = jnp.concatenate([sums[:4], ffn_sums[:2], grad_class], axis=0)
    small_rows = small.shape[0]
    upper = lax.reduce_precision(small, 8, 7)
    rider = jnp.concatenate([upper, small - upper], axis=0).astype(low)
    rider = jnp.pad(rider, ((0, n_dev - 2 * small_rows), (0, 0)))

    def give_back(turn, rider):
        return give_rows(positions(turn), grad_embed_low, rider, depth).reshape(n_dev, depth, MODEL_WIDTH)

    def collect(ids, returned):
        return collect_rows(ids, returned.reshape(-1, MODEL_WIDTH), table_rows)

    def collect_more(state):
        turn, total, _ = state
        total = total + collect(flat_ids(exchange(wanted(turn))), exchange(give_back(turn, jnp.zeros_like(rider))))[0]
        return turn + 1, total, jnp.zeros((8, MODEL_WIDTH)).at[0].set(jnp.sum(total * total, axis=0))

    given = give_back(0, rider)
    if by_bits:
        given, *flow = together(given, *by_core(grad_dense), *ffn_parts)
        grad_dense, ffn_parts = flow[:2], flow[2:]
        ffn_grad = sum(part.astype(jnp.float32) for part in ffn_parts)
    returned = exchange(given)
    dense_parts = dense_scatter(*grad_dense) if by_bits else [over_both(grad_dense)]
    table_sums = collect(ids_first, returned)
    *table_sums, returned = together(*table_sums, returned)
    *table_sums, dense_first = together(*table_sums, dense_parts[0])
    dense_parts = together(*dense_parts[1:], dense_first)
    dense_grad = sum(part.astype(jnp.float32) for part in dense_parts)
    _, table_grad, table_squares = lax.while_loop(
        lambda state: state[0] < turns, collect_more, (jnp.int32(1), *table_sums)
    )
    small_row = jnp.sum(returned[:, capacity].astype(jnp.float32), axis=0)

    def folded(row):
        return sum(row[:, at : at + 128] for at in range(0, MODEL_WIDTH, 128))

    ffn_squares = jnp.sum(ffn_grad * ffn_grad, axis=0, keepdims=True)
    squares = table_squares[:1] + jnp.sum(dense_grad * dense_grad, axis=0, keepdims=True)
    squares = squares + ffn_squares[:, :MODEL_WIDTH] + ffn_squares[:, MODEL_WIDTH:]
    losses = sums[4:5] + ffn_sums[2:3] + ffn_sums[3:4]
    count_row = jnp.pad(own_lengths.astype(jnp.float32), (0, 128 - own_seqs))[None]
    message = jnp.concatenate([small_row[None], folded(squares), folded(losses), count_row], axis=1)
    told = exchange(jnp.broadcast_to(message, (n_dev, message.shape[1])))
    scaling, loss_sum, token_count, grad_norm, *updated = finish(
        small_rows,
        told,
        (norm_gains, norm_moment, norm_square),
        (dense_weights, dense_moment, dense_square, dense_grad),
        (feedforward, feedforward_moment, feedforward_square, ffn_grad),
        (classifier.T, classifier_moment.T, classifier_square.T),
    )
    gains_new, dense_new, ffn_new, class_new = updated[:3], updated[3:7], updated[7:11], [part.T for part in updated[11:]]
    table_new = adam_update(
        embed_table, table_grad * scaling, embed_moment, embed_square, weight_decay, learn_rate
    )
    return (
        loss_sum.reshape(()),
        token_count.reshape(()),
        grad_norm.reshape(()),
        table_new[0],
        table_new[1],
        table_new[2],
        table_new[0].astype(jnp.bfloat16),
        dense_new[0],
        dense_new[1],
        dense_new[2],
        dense_new[3],
        ffn_new[0],
        ffn_new[1],
        ffn_new[2],
        ffn_new[3],
        class_new[0],
        class_new[1],
        class_new[2],
        class_new[3],
        gains_new[0],
        gains_new[1],
        gains_new[2],
    )


def solution(mesh):
    placed = (
        P("dp", None),
        P("dp", None),
        P("dp", None),
        P("dp"),
        P("dp"),
        P(("dp", "mp"), None, None),
        P(("dp", "mp"), None, None),
        P(("dp", "mp"), None),
        P(("dp", "mp"), None),
        P(("dp", "mp"), None),
        P(("dp", "mp"), None),
        P(("dp", "mp"), None),
        P(("dp", "mp"), None),
        P(("dp", "mp"), None),
        P(("dp", "mp"), None),
        P(("dp", "mp"), None),
        P(("dp", "mp"), None),
        P(),
        P(),
        P(),
        P(),
        P(),
        P(),
    )
    return jax.shard_map(
        per_device,
        mesh=mesh,
        in_specs=placed,
        out_specs=(
            P(),
            P(),
            P(),
            P(("dp", "mp"), None),
            P(("dp", "mp"), None),
            P(("dp", "mp"), None),
            P(("dp", "mp"), None),
            P(("dp", "mp"), None),
            P(("dp", "mp"), None),
            P(("dp", "mp"), None),
            P(("dp", "mp"), None),
            P(("dp", "mp"), None),
            P(("dp", "mp"), None),
            P(("dp", "mp"), None),
            P(("dp", "mp"), None),
            P(),
            P(),
            P(),
            P(),
            P(),
            P(),
            P(),
        ),
        check_vma=False,
    )
```
